256 devices in a mesh: depth: 8 (over z), height: 32 (over y, x, core).
Axes of the slice: x: 4, y: 4, z: 8, core: 2. Of those that a mesh axis runs over, the one named last changes fastest.
Arguments:
- volume: float32 [256, 256, 2048], P('depth', 'height'), may hold values from -6 to 6
- colour_coef: float32 [3, 4], replicated, may hold values from -4 to 4
- opacity_coef: float32 [4], replicated, may hold values from -4 to 4
- light_dir: float32 [4, 3], replicated, may hold values from -4 to 4
- light_colour: float32 [4, 3], replicated, may hold values from 0.2 to 1.5
Outputs:
- composite_image: float32 [13, 256, 2048], P(None, 'height')
The draws below stay inside these ranges and needn't reach their ends.
All inputs are finite; a program needn't handle non-finite values.
Results may differ from the reference program's by a relative error of at most 0.00002.
Values sent between devices are 32-bit elements; how exact they have to be, the bound alone decides.
No kernel may reach another device: no remote copies, remote signals or barrier semaphores. Data moves between devices by JAX's collectives and lax.ppermute only.
A program may use at most 128 MiB of HBM per device.

```python
import jax
import jax.numpy as jnp
from jax import lax

CD = 32
W = 2048
NZ = 256
NY = 256
N_DEPTH = 8


def levels(stream_key, dims, cuts, least, top_value):
    factor_of = 1.0
    for position, parts in cuts:
        steps = jax.random.uniform(jax.random.fold_in(jax.random.fold_in(stream_key, 6), position), (parts,), jnp.float32, least / len(cuts), top_value / len(cuts))
        factor_of = factor_of * jnp.repeat(jnp.exp(steps), dims[position] // parts).reshape((-1,) + (1,) * (len(dims) - 1 - position))
    return factor_of


def scatter_about(rng, extent, scale, most, pieces=(), kind=jnp.bfloat16):
    values = scale * jax.random.normal(rng, extent, jnp.float32)
    if pieces:
        values = values * levels(rng, extent, pieces, -0.22, 0.18)
    return jnp.clip(values, -most, most).astype(kind)


def setup_inputs(seed: int = 0) -> dict:
    seeds = jax.random.split(jax.random.key(seed), 6)
    return {
        "volume": scatter_about(seeds[0], (NZ, NY, W), 1.0, 6.0, ((0, 8), (1, 32)), jnp.float32),
        "colour_coef": scatter_about(seeds[1], (3, 4), 1.0, 4.0, (), jnp.float32),
        "opacity_coef": scatter_about(seeds[2], (4,), 1.0, 4.0, (), jnp.float32),
        "light_dir": scatter_about(seeds[3], (4, 3), 1.0, 4.0, (), jnp.float32),
        "light_colour": jnp.clip(jax.random.uniform(seeds[4], (4, 3), jnp.float32, 0.2, 1.5), 0.2, 1.5),
    }


def diffuse(padded):
    centre = padded[1:-1, 1:-1]
    widened = jnp.pad(centre, ((0, 0), (0, 0), (1, 1)))
    neighbours = (padded[2:, 1:-1], padded[:-2, 1:-1], padded[1:-1, 2:], padded[1:-1, :-2], widened[:, :, 2:], widened[:, :, :-2])
    flux_sum = jnp.zeros_like(centre)
    for neighbour in neighbours:
        differ = neighbour - centre
        flux_sum = flux_sum + differ / (1.0 + differ * differ)
    return centre + 0.12 * flux_sum

def slopes(padded):
    centre = padded[1:-1, 1:-1]
    widened = jnp.pad(centre, ((0, 0), (0, 0), (1, 1)))
    return (0.5 * (padded[2:, 1:-1] - padded[:-2, 1:-1]), 0.5 * (padded[1:-1, 2:] - padded[1:-1, :-2]), 0.5 * (widened[:, :, 2:] - widened[:, :, :-2]))

def shade(values, grad_depth, grad_height, grad_width, colour_coef, opacity_coef, light_dir, light_colour, alpha_top):
    squared = values * values
    cubed = squared * values
    base_colour = [0.5 + 0.5 * jnp.tanh(colour_coef[channel, 0] + colour_coef[channel, 1] * values + colour_coef[channel, 2] * squared + colour_coef[channel, 3] * cubed) for channel in range(3)]
    polynomial = opacity_coef[0] + opacity_coef[1] * values + opacity_coef[2] * squared + opacity_coef[3] * cubed
    strength = polynomial * polynomial
    opacity = alpha_top * strength / (1.0 + strength)
    inverse = lax.rsqrt(grad_depth * grad_depth + grad_height * grad_height + grad_width * grad_width + 1.0)
    colours = []
    for light_index in range(4):
        facing = jnp.abs(inverse * (grad_depth * light_dir[light_index, 0] + grad_height * light_dir[light_index, 1] + grad_width * light_dir[light_index, 2]))
        for channel in range(3):
            colours.append(base_colour[channel] * light_colour[light_index, channel] * (0.2 + facing))
    return (jnp.stack(colours), opacity)

def render_slab(smooth, grad_depth, grad_height, grad_width, colour_coef, opacity_coef, light_dir, light_colour, alpha_top):
    colours, opacity = shade(smooth, grad_depth, grad_height, grad_width, colour_coef, opacity_coef, light_dir, light_colour, alpha_top)
    remaining = jnp.cumprod(1.0 - opacity, axis=0)
    before = jnp.concatenate([jnp.ones_like(remaining[:1]), remaining[:-1]], 0)
    weights = before * opacity
    colour_sum = lax.optimization_barrier(jnp.sum(weights[None] * colours, axis=1))
    return jnp.concatenate([colour_sum, (1.0 - remaining[-1])[None]], 0)

def over(front, back):
    return front + (1.0 - front[12:13]) * back

def reference(volume, colour_coef, opacity_coef, light_dir, light_colour):
    margin = ((1, 1), (1, 1), (0, 0))
    smooth_one = diffuse(jnp.pad(volume, margin))
    smooth_two = diffuse(jnp.pad(smooth_one, margin))
    grad_depth, grad_height, grad_width = slopes(jnp.pad(smooth_two, margin))
    alpha_top = 2.0 / NZ
    stacked = tuple((array.reshape(N_DEPTH, CD, NY, W) for array in (smooth_two, grad_depth, grad_height, grad_width)))

    def one_slab(blocks):
        return render_slab(blocks[0], blocks[1], blocks[2], blocks[3], colour_coef, opacity_coef, light_dir, light_colour, alpha_top)
    partials = lax.map(one_slab, stacked)
    forward = partials[0]
    for slab_index in range(1, N_DEPTH):
        forward = over(forward, partials[slab_index])
    return forward
```

```python
import functools

import jax
import jax.numpy as jnp
from jax import lax
from jax.experimental import pallas as pl
from jax.experimental.pallas import tpu as pltpu
from jax.sharding import PartitionSpec as P

VMEM = pltpu.VMEM
F32 = jnp.float32
LANES = 128
ROWS = 8


def flux(d):
    q = d * d + 1.0
    r = pl.reciprocal(q, approx=True)
    return d * (r * (2.0 - q * r))


def inverse_of(q):
    r = pl.reciprocal(q, approx=True)
    return r * (2.0 - q * r)


def pack_rows(vol_ref, down_ref, up_ref):
    cells, tiles = vol_ref.shape[0], vol_ref.shape[1]
    flat = vol_ref.reshape(cells * tiles * ROWS, LANES)
    stride = tiles * ROWS
    for row in range(3):
        for tile in range(tiles):
            for z in range(0, cells, 8):
                base = z * stride + tile * ROWS
                up_ref[row, tile, z : z + 8, :] = flat[pl.ds(base + row, 8, stride=stride), :]
                down_ref[row, tile, z : z + 8, :] = flat[
                    pl.ds(base + 5 + row, 8, stride=stride), :
                ]


def pack_corners(low_ref, high_ref, down_ref, up_ref):
    tiles = low_ref.shape[1]
    for tile in range(tiles):
        for slot, (ref, plane, depth) in enumerate(
            (
                (low_ref, 2, 0),
                (low_ref, 1, 0),
                (low_ref, 2, 1),
                (high_ref, 0, 0),
                (high_ref, 1, 0),
                (high_ref, 0, 1),
            )
        ):
            up_ref[tile, slot : slot + 1, :] = ref[plane, tile, depth : depth + 1, :]
            down_ref[tile, slot : slot + 1, :] = ref[plane, tile, 7 - depth : 8 - depth, :]
        for slot in (6, 7):
            up_ref[tile, slot : slot + 1, :] = jnp.zeros((1, LANES), F32)
            down_ref[tile, slot : slot + 1, :] = jnp.zeros((1, LANES), F32)


def diffuse_planes(src, dst, held, planes, rim):
    tiles = src.shape[1]
    lane = lax.broadcasted_iota(jnp.int32, (ROWS, LANES), 1)
    sub = lax.broadcasted_iota(jnp.int32, (ROWS, LANES), 0)
    last_lane, first_lane = lane == LANES - 1, lane == 0
    last_sub, first_sub = sub == ROWS - 1, sub == 0

    for tile in range(tiles):
        for part in range(2):
            held[tile, part] = flux(src[1, tile, part] - src[0, tile, part])

    def step(z, carry):
        here = z + 1
        previous = [None, None]
        now = [src[here, 0, part] for part in range(2)]
        turned = [pltpu.roll(now[part], LANES - 1, 1) for part in range(2)]
        for tile in range(tiles):
            if tile + 1 < tiles:
                later = [src[here, tile + 1, part] for part in range(2)]
                later_turned = [pltpu.roll(later[part], LANES - 1, 1) for part in range(2)]
            else:
                later = later_turned = [None, None]
            raised = [pltpu.roll(now[part], ROWS - 1, 0) for part in range(2)]
            across = []
            up = []
            for part in range(2):
                beside = jnp.where(
                    last_lane, 0.0 if later[part] is None else later_turned[part], turned[part]
                )
                across.append(flux(beside - now[part]))
                up.append(flux(jnp.where(last_sub, raised[1 - part], raised[part]) - now[part]))
            across_turned = [pltpu.roll(a, 1, 1) for a in across]
            up_turned = [pltpu.roll(a, 1, 0) for a in up]
            for part in range(2):
                left = jnp.where(
                    first_lane,
                    flux(now[part]) if previous[part] is None else previous[part],
                    across_turned[part],
                )
                below = jnp.where(first_sub, up_turned[1 - part], up_turned[part])
                ahead = flux(src[here + 1, tile, part] - now[part])
                total = ((across[part] - left) + (up[part] - below)) + (ahead - held[tile, part])
                held[tile, part] = ahead
                value = now[part] + 0.12 * total
                dst[z, tile, part] = value if part == 0 else value * rim
            previous, now, turned = across_turned, later, later_turned
        return carry

    lax.fori_loop(0, planes, step, 0)


def render(
    edge_ref,
    colour_ref,
    opacity_ref,
    dir_ref,
    light_ref,
    vol_ref,
    low_ref,
    high_ref,
    top_ref,
    bottom_ref,
    top_corner_ref,
    bottom_corner_ref,
    out_ref,
    field,
    once,
    twice,
    held,
    alpha_top,
):
    cells, tiles = vol_ref.shape[0], vol_ref.shape[1]
    sub = lax.broadcasted_iota(jnp.int32, (ROWS, LANES), 0)
    lane = lax.broadcasted_iota(jnp.int32, (ROWS, LANES), 1)
    keep_low, keep_high = edge_ref[0], edge_ref[1]
    keep_top, keep_bottom = edge_ref[2], edge_ref[3]
    rim = jnp.where(sub >= 4, jnp.full((ROWS, LANES), keep_top), jnp.full((ROWS, LANES), keep_bottom))

    for k in range(3):
        for tile in range(tiles):
            field[k, tile, 0] = low_ref[k, tile] * keep_low
            field[cells + 3 + k, tile, 0] = high_ref[k, tile] * keep_high
            field[k, tile, 1] = jnp.zeros((ROWS, LANES), F32)
            field[cells + 3 + k, tile, 1] = jnp.zeros((ROWS, LANES), F32)

    def fill(z, carry):
        for tile in range(tiles):
            field[z + 3, tile, 0] = vol_ref[z, tile]
            field[z + 3, tile, 1] = jnp.zeros((ROWS, LANES), F32)
        return carry

    lax.fori_loop(0, cells, fill, 0)
    flat = field.reshape((cells + 6) * tiles * 2 * ROWS, LANES)
    stride = tiles * 2 * ROWS
    for tile in range(tiles):
        offset = (tile * 2 + 1) * ROWS
        for row in range(3):
            for z in range(0, cells, 8):
                base = (z + 3) * stride + offset
                flat[pl.ds(base + 5 + row, 8, stride=stride), :] = (
                    top_ref[row, tile, z : z + 8, :] * keep_top
                )
                flat[pl.ds(base + row, 8, stride=stride), :] = (
                    bottom_ref[row, tile, z : z + 8, :] * keep_bottom
                )
        for slot, (plane, away) in enumerate(
            ((2, 0), (1, 0), (2, 1), (cells + 3, 0), (cells + 4, 0), (cells + 3, 1))
        ):
            keep_z = keep_low if slot < 3 else keep_high
            field[plane, tile, 1, 7 - away : 8 - away, :] = (
                top_corner_ref[tile, slot : slot + 1, :] * (keep_z * keep_top)
            )
            field[plane, tile, 1, away : away + 1, :] = (
                bottom_corner_ref[tile, slot : slot + 1, :] * (keep_z * keep_bottom)
            )

    diffuse_planes(field, once, held, cells + 4, rim)
    for k in range(2):
        for tile in range(tiles):
            for part in range(2):
                once[k, tile, part] = once[k, tile, part] * keep_low
                once[cells + 2 + k, tile, part] = once[cells + 2 + k, tile, part] * keep_high
    diffuse_planes(once, twice, held, cells + 2, rim)
    for tile in range(tiles):
        twice[0, tile, 0] = twice[0, tile, 0] * keep_low
        twice[cells + 1, tile, 0] = twice[cells + 1, tile, 0] * keep_high

    colour = [[colour_ref[c, j] for j in range(4)] for c in range(3)]
    opac = [opacity_ref[j] for j in range(4)]
    light = [[0.5 * dir_ref[l, d] for d in range(3)] for l in range(4)]

    def poly(c, v):
        return ((c[3] * v + c[2]) * v + c[1]) * v + c[0]

    def column(tile, carry):
        left_tile = jnp.maximum(tile - 1, 0)
        right_tile = jnp.minimum(tile + 1, tiles - 1)
        keep_left = jnp.where(tile > 0, 1.0, 0.0)
        keep_right = jnp.where(tile < tiles - 1, 1.0, 0.0)

        def cell(z, state):
            through, sums, base_sums = state
            v = twice[z + 1, tile, 0]
            beyond = twice[z + 1, tile, 1]
            g_z = twice[z + 2, tile, 0] - twice[z, tile, 0]
            g_h = jnp.where(
                sub == 7, pltpu.roll(beyond, 7, 0), pltpu.roll(v, 7, 0)
            ) - jnp.where(sub == 0, pltpu.roll(beyond, 1, 0), pltpu.roll(v, 1, 0))
            right = twice[z + 1, right_tile, 0] * keep_right
            left = twice[z + 1, left_tile, 0] * keep_left
            g_w = jnp.where(
                lane == LANES - 1, pltpu.roll(right, LANES - 1, 1), pltpu.roll(v, LANES - 1, 1)
            ) - jnp.where(lane == 0, pltpu.roll(left, 1, 1), pltpu.roll(v, 1, 1))
            inverse = lax.rsqrt(0.25 * (g_z * g_z + g_h * g_h + g_w * g_w) + 1.0)
            p = poly(opac, v)
            s = p * p
            opacity = (alpha_top * s) * inverse_of(1.0 + s)
            weight = through * opacity
            through = through - weight
            half = 0.5 * weight
            shaded = [half + half * jnp.tanh(poly(colour[c], v)) for c in range(3)]
            base_sums = [base_sums[c] + shaded[c] for c in range(3)]
            tilted = [inverse * shaded[c] for c in range(3)]
            new = []
            for l in range(4):
                facing = jnp.abs(g_z * light[l][0] + g_h * light[l][1] + g_w * light[l][2])
                for c in range(3):
                    new.append(sums[3 * l + c] + facing * tilted[c])
            return through, new, base_sums

        zero = jnp.zeros((ROWS, LANES), F32)
        state = (jnp.ones((ROWS, LANES), F32), [zero] * 12, [zero] * 3)

        def group(g, state):
            for k in range(4):
                state = cell(g * 4 + k, state)
            return state

        through, sums, base_sums = lax.fori_loop(0, cells // 4, group, state)
        for l in range(4):
            for c in range(3):
                out_ref[tile // 2, 3 * l + c, tile % 2] = light_ref[l, c] * (
                    0.2 * base_sums[c] + sums[3 * l + c]
                )
        out_ref[tile // 2, 12, tile % 2] = 1.0 - through
        return carry

    lax.fori_loop(0, tiles, column, 0)


def fold(parts_ref, out_ref):
    slabs, channels = parts_ref.shape[0], parts_ref.shape[1]
    for tile in range(2):
        through = 1.0 - parts_ref[0, 12, tile]
        total = [parts_ref[0, ch, tile] for ch in range(channels)]
        for slab in range(1, slabs):
            total = [total[ch] + through * parts_ref[slab, ch, tile] for ch in range(channels)]
            through = through * (1.0 - parts_ref[slab, 12, tile])
        for ch in range(channels):
            out_ref[ch, tile] = total[ch]


def spread(place_ref, *refs):
    pieces, out_ref = refs[:-1], refs[-1]
    count = len(pieces)
    channels = out_ref.shape[0]
    for step, ref in enumerate(pieces):
        offset = step if step <= count // 2 else count // 2 - step
        owner = lax.rem(place_ref[0] - offset + count, count)
        for tile in range(2):
            at = pl.multiple_of((owner * 2 + tile) * LANES, LANES)
            for ch in range(channels):
                out_ref[ch, :, pl.ds(at, LANES)] = ref[ch, tile]


def in_vmem(count):
    return [pl.BlockSpec(memory_space=VMEM)] * count


def in_smem(count):
    return [pl.BlockSpec(memory_space=pltpu.SMEM)] * count


def shape(*dims):
    return jax.ShapeDtypeStruct(dims, F32)


def ring(axis, by):
    count = lax.axis_size(axis)
    return [(i, (i + by) % count) for i in range(count)]


def per_device(volume, colour_coef, opacity_coef, light_dir, light_colour):
    slabs, bands = lax.axis_size("depth"), lax.axis_size("height")
    cells, rows, width = volume.shape
    tiles = width // LANES
    slab, band = lax.axis_index("depth"), lax.axis_index("height")
    limit = pltpu.CompilerParams(vmem_limit_bytes=56 << 20)
    field = volume.reshape(cells, rows, tiles, LANES).transpose(0, 2, 1, 3)

    low = lax.ppermute(field[cells - 3 :], "depth", ring("depth", 1))
    high = lax.ppermute(field[:3], "depth", ring("depth", -1))
    down, up = pl.pallas_call(
        pack_rows,
        out_shape=[shape(3, tiles, cells, LANES)] * 2,
        in_specs=in_vmem(1),
        out_specs=in_vmem(2),
        compiler_params=limit,
        name="pack_rows",
    )(field)
    top = lax.ppermute(down, "height", ring("height", 1))
    bottom = lax.ppermute(up, "height", ring("height", -1))
    corner_down, corner_up = pl.pallas_call(
        pack_corners,
        out_shape=[shape(tiles, rows, LANES)] * 2,
        in_specs=in_vmem(2),
        out_specs=in_vmem(2),
        compiler_params=limit,
        name="pack_corners",
    )(low, high)
    top_corner = lax.ppermute(corner_down, "height", ring("height", 1))
    bottom_corner = lax.ppermute(corner_up, "height", ring("height", -1))

    edges = jnp.stack([slab > 0, slab < slabs - 1, band > 0, band < bands - 1]).astype(F32)
    partial = pl.pallas_call(
        functools.partial(render, alpha_top=2.0 / (cells * slabs)),
        out_shape=shape(slabs, 13, tiles // slabs, rows, LANES),
        in_specs=in_smem(5) + in_vmem(7),
        out_specs=pl.BlockSpec(memory_space=VMEM),
        scratch_shapes=[
            VMEM((cells + 6, tiles, 2, rows, LANES), F32),
            VMEM((cells + 4, tiles, 2, rows, LANES), F32),
            VMEM((cells + 2, tiles, 2, rows, LANES), F32),
            VMEM((tiles, 2, rows, LANES), F32),
        ],
        compiler_params=limit,
        name="render",
    )(
        edges,
        colour_coef,
        opacity_coef,
        light_dir,
        light_colour,
        field,
        low,
        high,
        top,
        bottom,
        top_corner,
        bottom_corner,
    )
    exchanged = lax.all_to_all(partial, "depth", 0, 0, tiled=True)
    own = pl.pallas_call(
        fold,
        out_shape=shape(13, tiles // slabs, rows, LANES),
        in_specs=in_vmem(1),
        out_specs=pl.BlockSpec(memory_space=VMEM),
        compiler_params=limit,
        name="fold",
    )(exchanged)
    from_below, from_above = [own], [own]
    for _ in range(slabs // 2):
        from_below.append(lax.ppermute(from_below[-1], "depth", ring("depth", 1)))
        from_above.append(lax.ppermute(from_above[-1], "depth", ring("depth", -1)))
    pieces = from_below + from_above[1 : slabs // 2]
    return pl.pallas_call(
        spread,
        out_shape=shape(13, rows, width),
        in_specs=in_smem(1) + in_vmem(slabs),
        out_specs=pl.BlockSpec(memory_space=VMEM),
        compiler_params=limit,
        name="spread",
    )(slab[None], *pieces)


def solution(mesh):
    placed = (P("depth", "height", None), P(), P(), P(), P())
    return jax.shard_map(
        per_device, mesh=mesh, in_specs=placed, out_specs=P(None, "height", None), check_vma=False
    )
```

```python
import functools

import jax
import jax.numpy as jnp
from jax import lax
from jax.experimental import pallas as pl
from jax.experimental.pallas import tpu as pltpu
from jax.sharding import PartitionSpec as P

VMEM = pltpu.VMEM
DMA = pltpu.SemaphoreType.DMA
F32 = jnp.float32
LANES = 128
ROWS = 8
BAND = 8
OWN = 4


def inverse_of(q):
    return pltpu.reciprocal(q, approx=True)


def flux(d):
    return d * inverse_of(d * d + 1.0)


def pack(vol_ref, down_ref, up_ref, first_ref, last_ref, held, down, up, in_sem, edge_sem, out_sem):
    cells, tiles = vol_ref.shape[0], vol_ref.shape[1]
    groups = cells // 8
    loads = [
        pltpu.make_async_copy(vol_ref.at[pl.ds(8 * g, 8)], held.at[pl.ds(8 * g, 8)], in_sem.at[g])
        for g in range(groups)
    ]
    edges = [
        pltpu.make_async_copy(vol_ref.at[pl.ds(0, 3)], first_ref, edge_sem.at[0]),
        pltpu.make_async_copy(vol_ref.at[pl.ds(cells - 3, 3)], last_ref, edge_sem.at[1]),
    ]
    for copy in loads + edges:
        copy.start()
    stores = []
    for g in range(groups):
        loads[g].wait()
        for k in range(8):
            z = 8 * g + k
            for tile in range(tiles):
                up[tile, 3 * z : 3 * z + 3, :] = held[z, tile, 0:3, :]
                down[tile, 3 * z : 3 * z + 3, :] = held[z, tile, 5:8, :]
        part = pl.ds(24 * g, 24)
        for i, (ref, out_ref) in enumerate(((down, down_ref), (up, up_ref))):
            copy = pltpu.make_async_copy(
                ref.at[:, part, :], out_ref.at[:, part, :], out_sem.at[2 * g + i]
            )
            copy.start()
            stores.append(copy)
    for copy in stores + edges:
        copy.wait()


CORNERS = ((0, 1, 0), (0, 0, 0), (0, 1, 1), (1, 0, 0), (1, 1, 0), (1, 0, 1))


def pack_corners(low_ref, high_ref, down_ref, up_ref, near, sem):
    tiles = low_ref.shape[1]
    copies = [
        pltpu.make_async_copy(low_ref.at[pl.ds(1, 2)], near.at[0], sem.at[0]),
        pltpu.make_async_copy(high_ref.at[pl.ds(0, 2)], near.at[1], sem.at[1]),
    ]
    for copy in copies:
        copy.start()
    for copy in copies:
        copy.wait()
    zero = jnp.zeros((2, LANES), F32)
    for tile in range(tiles):
        for slot, (side, plane, depth) in enumerate(CORNERS):
            up_ref[tile, slot : slot + 1, :] = near[side, plane, tile, depth : depth + 1, :]
            down_ref[tile, slot : slot + 1, :] = near[side, plane, tile, 7 - depth : 8 - depth, :]
        up_ref[tile, 6:8, :] = zero
        down_ref[tile, 6:8, :] = zero


def beside(src, base, z, parity, nexts, befores):
    tiles = src.shape[1]
    lane = lax.broadcasted_iota(jnp.int32, (ROWS, LANES), 1)
    for part in range(2):
        rows = pl.ds(base + 8 * part, 8)
        now = src[z, 0, rows, :]
        lowered, raised = pltpu.roll(now, LANES - 1, 1), pltpu.roll(now, 1, 1)
        earlier = 0.0
        for tile in range(tiles):
            if tile + 1 < tiles:
                later = src[z, tile + 1, rows, :]
                later_lowered = pltpu.roll(later, LANES - 1, 1)
                later_raised = pltpu.roll(later, 1, 1)
            else:
                later_lowered, later_raised = 0.0, None
            nexts[parity, tile, part] = jnp.where(lane == LANES - 1, later_lowered, lowered)
            befores[parity, tile, part] = jnp.where(lane == 0, earlier, raised)
            earlier, lowered, raised = raised, later_lowered, later_raised


def diffuse_plane(src, base, z, parity, nexts, befores, held, dst, out, rims):
    tiles = src.shape[1]
    sub = lax.broadcasted_iota(jnp.int32, (ROWS, LANES), 0)
    for tile in range(tiles):
        below = None
        for part in range(2):
            first = base + 8 * part
            u = src[z, tile, pl.ds(first, 8), :]
            across = flux(nexts[parity, tile, part] - u) + flux(befores[parity, tile, part] - u)
            if first + 9 <= src.shape[2]:
                above = src[z, tile, pl.ds(first + 1, 8), :]
            else:
                above = pltpu.roll(u, ROWS - 1, 0)
            up = flux(above - u)
            turned = pltpu.roll(up, 1, 0)
            along = up - (turned if part == 0 else jnp.where(sub == 0, below, turned))
            below = turned
            ahead = flux(src[z + 1, tile, pl.ds(first, 8), :] - u)
            total = (across + along) + (ahead - held[tile, part])
            held[tile, part] = ahead
            dst[out, tile, pl.ds(8 * part, 8), :] = (u + 0.12 * total) * rims[part]


def width_slope(field, z, slope):
    tiles = field.shape[1]
    lane = lax.broadcasted_iota(jnp.int32, (ROWS, LANES), 1)
    rows = pl.ds(OWN, 8)
    now = field[z, 0, rows, :]
    lowered, raised = pltpu.roll(now, LANES - 1, 1), pltpu.roll(now, 1, 1)
    earlier = 0.0
    for tile in range(tiles):
        if tile + 1 < tiles:
            later = field[z, tile + 1, rows, :]
            later_lowered, later_raised = pltpu.roll(later, LANES - 1, 1), pltpu.roll(later, 1, 1)
        else:
            later_lowered, later_raised = 0.0, None
        slope[z, tile] = jnp.where(lane == LANES - 1, later_lowered, lowered) - jnp.where(
            lane == 0, earlier, raised
        )
        earlier, lowered, raised = raised, later_lowered, later_raised


def diffuse(src, base, dst, planes, nexts, befores, held, rims, slope=None):
    for tile in range(src.shape[1]):
        for part in range(2):
            rows = pl.ds(base + 8 * part, 8)
            held[tile, part] = flux(src[1, tile, rows, :] - src[0, tile, rows, :])
    beside(src, base, 1, 1, nexts, befores)

    def pair(g, carry):
        for k in range(2):
            z = 2 * g + k + 1
            beside(src, base, z + 1, k, nexts, befores)
            diffuse_plane(src, base, z, 1 - k, nexts, befores, held, dst, z - 1, rims)
            if slope is not None:
                width_slope(dst, jnp.maximum(z - 3, 0), slope)
        return carry

    lax.fori_loop(0, planes // 2, pair, 0)
    if slope is not None:
        width_slope(dst, planes - 2, slope)


def render(
    edge_ref,
    colour_ref,
    opacity_ref,
    dir_ref,
    light_ref,
    vol_ref,
    low_ref,
    high_ref,
    top_ref,
    bottom_ref,
    top_corner_ref,
    bottom_corner_ref,
    out_ref,
    field,
    once,
    twice,
    slope,
    nexts,
    befores,
    held,
    rows_in,
    corners_in,
    sem,
    alpha_top,
):
    cells, tiles = vol_ref.shape[0], vol_ref.shape[1]
    own = pl.ds(BAND, 8)
    copies = [
        pltpu.make_async_copy(low_ref, field.at[pl.ds(0, 3), :, own, :], sem.at[0]),
        pltpu.make_async_copy(high_ref, field.at[pl.ds(cells + 3, 3), :, own, :], sem.at[1]),
        pltpu.make_async_copy(top_corner_ref, corners_in.at[0], sem.at[2]),
        pltpu.make_async_copy(bottom_corner_ref, corners_in.at[1], sem.at[3]),
        pltpu.make_async_copy(top_ref, rows_in.at[0], sem.at[4]),
        pltpu.make_async_copy(bottom_ref, rows_in.at[1], sem.at[5]),
        pltpu.make_async_copy(vol_ref, field.at[pl.ds(3, cells), :, own, :], sem.at[6]),
    ]
    for copy in copies:
        copy.start()

    sub = lax.broadcasted_iota(jnp.int32, (ROWS, LANES), 0)
    keep_low, keep_high = edge_ref[0], edge_ref[1]
    keep_top, keep_bottom = edge_ref[2], edge_ref[3]
    rims = (
        jnp.where(sub < OWN, jnp.full((ROWS, LANES), keep_top), 1.0),
        jnp.where(sub >= OWN, jnp.full((ROWS, LANES), keep_bottom), 1.0),
    )

    zero = jnp.zeros((ROWS, LANES), F32)
    for k in range(3):
        for tile in range(tiles):
            for plane in (k, cells + 3 + k):
                field[plane, tile, 0:8, :] = zero
                field[plane, tile, 16:24, :] = zero
    for copy in copies[:4]:
        copy.wait()
    for k in range(3):
        for tile in range(tiles):
            field[k, tile, own, :] = field[k, tile, own, :] * keep_low
            field[cells + 3 + k, tile, own, :] = field[cells + 3 + k, tile, own, :] * keep_high
    for tile in range(tiles):
        for slot, (side, plane, away) in enumerate(CORNERS):
            at = (cells + 3 if side else 1) + plane
            keep = keep_high if side else keep_low
            field[at, tile, 7 - away : 8 - away, :] = corners_in[0, tile, slot : slot + 1, :] * (
                keep * keep_top
            )
            field[at, tile, 16 + away : 17 + away, :] = corners_in[
                1, tile, slot : slot + 1, :
            ] * (keep * keep_bottom)
    copies[4].wait()
    copies[5].wait()

    def rims_in(g, carry):
        at = pl.multiple_of(24 * g, 24)
        for tile in range(tiles):
            for k in range(8):
                field[8 * g + k + 3, tile, 5:8, :] = (
                    rows_in[0, tile, pl.ds(at + 3 * k, 3), :] * keep_top
                )
                field[8 * g + k + 3, tile, 16:19, :] = (
                    rows_in[1, tile, pl.ds(at + 3 * k, 3), :] * keep_bottom
                )
        return carry

    lax.fori_loop(0, cells // 8, rims_in, 0)
    copies[6].wait()

    diffuse(field, OWN, once, cells + 4, nexts, befores, held, rims)
    for k in range(2):
        for tile in range(tiles):
            for rows in (slice(0, 8), slice(8, 16)):
                once[k, tile, rows, :] = once[k, tile, rows, :] * keep_low
                once[cells + 2 + k, tile, rows, :] = once[cells + 2 + k, tile, rows, :] * keep_high
    diffuse(once, 0, twice, cells + 2, nexts, befores, held, rims, slope)
    own = pl.ds(OWN, 8)
    for tile in range(tiles):
        twice[0, tile, own, :] = twice[0, tile, own, :] * keep_low
        twice[cells + 1, tile, own, :] = twice[cells + 1, tile, own, :] * keep_high

    colour = [[colour_ref[c, j] for j in range(4)] for c in range(3)]
    opac = [opacity_ref[j] for j in range(4)]
    light = [[0.5 * dir_ref[l, d] for d in range(3)] for l in range(4)]

    def poly(c, v):
        return ((c[3] * v + c[2]) * v + c[1]) * v + c[0]

    def column(tile, carry):
        def cell(z, state):
            through, sums, base_sums = state
            v = twice[z + 1, tile, own, :]
            g_z = twice[z + 2, tile, own, :] - twice[z, tile, own, :]
            g_h = twice[z + 1, tile, pl.ds(OWN + 1, 8), :] - twice[z + 1, tile, pl.ds(OWN - 1, 8), :]
            g_w = slope[z + 1, tile]
            inverse = lax.rsqrt(0.25 * (g_z * g_z + g_h * g_h + g_w * g_w) + 1.0)
            p = poly(opac, v)
            s = p * p
            opacity = (alpha_top * s) * inverse_of(1.0 + s)
            weight = through * opacity
            through = through - weight
            half = 0.5 * weight
            shaded = [half + half * jnp.tanh(poly(colour[c], v)) for c in range(3)]
            base_sums = [base_sums[c] + shaded[c] for c in range(3)]
            tilted = [inverse * shaded[c] for c in range(3)]
            new = []
            for l in range(4):
                facing = jnp.abs(g_z * light[l][0] + g_h * light[l][1] + g_w * light[l][2])
                for c in range(3):
                    new.append(sums[3 * l + c] + facing * tilted[c])
            return through, new, base_sums

        state = (jnp.ones((ROWS, LANES), F32), [zero] * 12, [zero] * 3)

        def group(g, state):
            for k in range(4):
                state = cell(g * 4 + k, state)
            return state

        through, sums, base_sums = lax.fori_loop(0, cells // 4, group, state)
        for l in range(4):
            for c in range(3):
                out_ref[tile // 2, 3 * l + c, tile % 2] = light_ref[l, c] * (
                    0.2 * base_sums[c] + sums[3 * l + c]
                )
        out_ref[tile // 2, 12, tile % 2] = 1.0 - through
        return carry

    lax.fori_loop(0, tiles, column, 0)


def fold(parts_ref, out_ref):
    slabs, channels = parts_ref.shape[0], parts_ref.shape[1]
    for tile in range(parts_ref.shape[2]):
        through = 1.0 - parts_ref[0, 12, tile]
        total = [parts_ref[0, ch, tile] for ch in range(channels)]
        for slab in range(1, slabs):
            total = [total[ch] + through * parts_ref[slab, ch, tile] for ch in range(channels)]
            through = through * (1.0 - parts_ref[slab, 12, tile])
        for ch in range(channels):
            out_ref[ch, tile] = total[ch]


def spread(place_ref, *refs):
    pieces, out_ref, sem = refs[:-2], refs[-2], refs[-1]
    count = len(pieces)
    tiles = out_ref.shape[1] // count
    copies = []
    for step, ref in enumerate(pieces):
        offset = step if step <= count // 2 else count // 2 - step
        owner = lax.rem(place_ref[0] - offset + count, count)
        copies.append(
            pltpu.make_async_copy(ref, out_ref.at[:, pl.ds(owner * tiles, tiles)], sem.at[step])
        )
    for copy in copies:
        copy.start()
    for copy in copies:
        copy.wait()


def in_vmem(count):
    return [pl.BlockSpec(memory_space=VMEM)] * count


def in_smem(count):
    return [pl.BlockSpec(memory_space=pltpu.SMEM)] * count


def anywhere(count):
    return [pl.BlockSpec(memory_space=pl.ANY)] * count


def shape(*dims):
    return jax.ShapeDtypeStruct(dims, F32)


def ring(axis, by):
    count = lax.axis_size(axis)
    return [(i, (i + by) % count) for i in range(count)]


def per_device(volume, colour_coef, opacity_coef, light_dir, light_colour):
    slabs, bands = lax.axis_size("depth"), lax.axis_size("height")
    cells, rows, width = volume.shape
    tiles = width // LANES
    slab, band = lax.axis_index("depth"), lax.axis_index("height")
    limit = pltpu.CompilerParams(vmem_limit_bytes=58 << 20)
    field = volume.reshape(cells, rows, tiles, LANES).transpose(0, 2, 1, 3)

    down, up, first, last = pl.pallas_call(
        pack,
        out_shape=[shape(tiles, 3 * cells, LANES)] * 2 + [shape(3, tiles, rows, LANES)] * 2,
        in_specs=anywhere(1),
        out_specs=anywhere(4),
        scratch_shapes=[
            VMEM((cells, tiles, rows, LANES), F32),
            VMEM((tiles, 3 * cells, LANES), F32),
            VMEM((tiles, 3 * cells, LANES), F32),
            DMA((cells // 8,)),
            DMA((2,)),
            DMA((cells // 4,)),
        ],
        compiler_params=limit,
        name="pack",
    )(field)
    top = lax.ppermute(down, "height", ring("height", 1))
    bottom = lax.ppermute(up, "height", ring("height", -1))
    low = lax.ppermute(last, "depth", ring("depth", 1))
    high = lax.ppermute(first, "depth", ring("depth", -1))
    corner_down, corner_up = pl.pallas_call(
        pack_corners,
        out_shape=[shape(tiles, rows, LANES)] * 2,
        in_specs=anywhere(2),
        out_specs=in_vmem(2),
        scratch_shapes=[VMEM((2, 2, tiles, rows, LANES), F32), DMA((2,))],
        compiler_params=limit,
        name="pack_corners",
    )(low, high)
    top_corner = lax.ppermute(corner_down, "height", ring("height", 1))
    bottom_corner = lax.ppermute(corner_up, "height", ring("height", -1))

    edges = jnp.stack([slab > 0, slab < slabs - 1, band > 0, band < bands - 1]).astype(F32)
    partial = pl.pallas_call(
        functools.partial(render, alpha_top=2.0 / (cells * slabs)),
        out_shape=shape(slabs, 13, tiles // slabs, rows, LANES),
        in_specs=in_smem(5) + anywhere(7),
        out_specs=pl.BlockSpec(memory_space=VMEM),
        scratch_shapes=[
            VMEM((cells + 6, tiles, 24, LANES), F32),
            VMEM((cells + 4, tiles, 16, LANES), F32),
            VMEM((cells + 2, tiles, 16, LANES), F32),
            VMEM((cells + 1, tiles, rows, LANES), F32),
            VMEM((2, tiles, 2, rows, LANES), F32),
            VMEM((2, tiles, 2, rows, LANES), F32),
            VMEM((tiles, 2, rows, LANES), F32),
            VMEM((2, tiles, 3 * cells, LANES), F32),
            VMEM((2, tiles, rows, LANES), F32),
            DMA((7,)),
        ],
        compiler_params=limit,
        name="render",
    )(
        edges,
        colour_coef,
        opacity_coef,
        light_dir,
        light_colour,
        field,
        low,
        high,
        top,
        bottom,
        top_corner,
        bottom_corner,
    )
    exchanged = lax.all_to_all(partial, "depth", 0, 0, tiled=True)
    own = pl.pallas_call(
        fold,
        out_shape=shape(13, tiles // slabs, rows, LANES),
        in_specs=in_vmem(1),
        out_specs=pl.BlockSpec(memory_space=VMEM),
        compiler_params=limit,
        name="fold",
    )(exchanged)
    from_below, from_above = [own], [own]
    for _ in range(slabs // 2):
        from_below.append(lax.ppermute(from_below[-1], "depth", ring("depth", 1)))
        from_above.append(lax.ppermute(from_above[-1], "depth", ring("depth", -1)))
    pieces = from_below + from_above[1 : slabs // 2]
    image = pl.pallas_call(
        spread,
        out_shape=shape(13, tiles, rows, LANES),
        in_specs=in_smem(1) + anywhere(slabs),
        out_specs=pl.BlockSpec(memory_space=pl.ANY),
        scratch_shapes=[DMA((slabs,))],
        compiler_params=limit,
        name="spread",
    )(slab[None], *pieces)
    return image.transpose(0, 2, 1, 3).reshape(13, rows, width)


def solution(mesh):
    placed = (P("depth", "height", None), P(), P(), P(), P())
    return jax.shard_map(
        per_device, mesh=mesh, in_specs=placed, out_specs=P(None, "height", None), check_vma=False
    )
```

```python
import functools

import jax
import jax.numpy as jnp
from jax import lax
from jax.experimental import pallas as pl
from jax.experimental.pallas import tpu as pltpu
from jax.sharding import PartitionSpec as P

VMEM = pltpu.VMEM
DMA = pltpu.SemaphoreType.DMA
F32 = jnp.float32
LANES = 128
ROWS = 8
BAND = 8
OWN = 4


def inverse_of(q):
    return pltpu.reciprocal(q, approx=True)


def flux(d):
    return d * inverse_of(d * d + 1.0)


def pack(vol_ref, *refs):
    down_refs, up_refs, first_ref, last_ref = refs[0:2], refs[2:4], refs[4], refs[5]
    held, down, up, in_sem, edge_sem, out_sem = refs[6:]
    cells, tiles = vol_ref.shape[0], vol_ref.shape[1]
    groups = cells // 8
    loads = [
        pltpu.make_async_copy(vol_ref.at[pl.ds(8 * g, 8)], held.at[pl.ds(8 * g, 8)], in_sem.at[g])
        for g in range(groups)
    ]
    edges = [
        pltpu.make_async_copy(held.at[pl.ds(0, 3)], first_ref, edge_sem.at[0]),
        pltpu.make_async_copy(held.at[pl.ds(cells - 3, 3)], last_ref, edge_sem.at[1]),
    ]
    for copy in loads:
        copy.start()
    stores = []
    for g in range(groups):
        loads[g].wait()
        if g == 0:
            edges[0].start()
        if g == groups - 1:
            edges[1].start()
        for k in range(8):
            z = 8 * g + k
            for tile in range(tiles):
                up[tile, 3 * z : 3 * z + 3, :] = held[z, tile, 0:3, :]
                down[tile, 3 * z : 3 * z + 3, :] = held[z, tile, 5:8, :]
        part = pl.ds(24 * g, 24)
        for half in range(2):
            for ref, out_refs in ((down, down_refs), (up, up_refs)):
                count = out_refs[half].shape[0]
                copy = pltpu.make_async_copy(
                    ref.at[pl.ds(half * (tiles - count), count), part, :],
                    out_refs[half].at[:, part, :],
                    out_sem.at[len(stores)],
                )
                copy.start()
                stores.append(copy)
    for copy in stores + edges:
        copy.wait()


CORNERS = ((0, 1, 0), (0, 0, 0), (0, 1, 1), (1, 0, 0), (1, 1, 0), (1, 0, 1))


def pack_corners(low_ref, high_ref, down_ref, up_ref, near, sem):
    tiles = low_ref.shape[1]
    copies = [
        pltpu.make_async_copy(low_ref.at[pl.ds(1, 2)], near.at[0], sem.at[0]),
        pltpu.make_async_copy(high_ref.at[pl.ds(0, 2)], near.at[1], sem.at[1]),
    ]
    for copy in copies:
        copy.start()
    for copy in copies:
        copy.wait()
    zero = jnp.zeros((2, LANES), F32)
    for tile in range(tiles):
        for slot, (side, plane, depth) in enumerate(CORNERS):
            up_ref[tile, slot : slot + 1, :] = near[side, plane, tile, depth : depth + 1, :]
            down_ref[tile, slot : slot + 1, :] = near[side, plane, tile, 7 - depth : 8 - depth, :]
        up_ref[tile, 6:8, :] = zero
        down_ref[tile, 6:8, :] = zero


def beside(src, base, z, parity, nexts, befores):
    tiles = src.shape[1]
    lane = lax.broadcasted_iota(jnp.int32, (ROWS, LANES), 1)
    for part in range(2):
        rows = pl.ds(base + 8 * part, 8)
        now = src[z, 0, rows, :]
        lowered, raised = pltpu.roll(now, LANES - 1, 1), pltpu.roll(now, 1, 1)
        earlier = 0.0
        for tile in range(tiles):
            if tile + 1 < tiles:
                later = src[z, tile + 1, rows, :]
                later_lowered = pltpu.roll(later, LANES - 1, 1)
                later_raised = pltpu.roll(later, 1, 1)
            else:
                later_lowered, later_raised = 0.0, None
            nexts[parity, tile, part] = jnp.where(lane == LANES - 1, later_lowered, lowered)
            befores[parity, tile, part] = jnp.where(lane == 0, earlier, raised)
            earlier, lowered, raised = raised, later_lowered, later_raised


def diffuse_plane(src, base, z, parity, nexts, befores, held, dst, out, rims):
    tiles = src.shape[1]
    sub = lax.broadcasted_iota(jnp.int32, (ROWS, LANES), 0)
    for tile in range(tiles):
        below = None
        for part in range(2):
            first = base + 8 * part
            u = src[z, tile, pl.ds(first, 8), :]
            across = flux(nexts[parity, tile, part] - u) + flux(befores[parity, tile, part] - u)
            if first + 9 <= src.shape[2]:
                above = src[z, tile, pl.ds(first + 1, 8), :]
            else:
                above = pltpu.roll(u, ROWS - 1, 0)
            up = flux(above - u)
            turned = pltpu.roll(up, 1, 0)
            along = up - (turned if part == 0 else jnp.where(sub == 0, below, turned))
            below = turned
            ahead = flux(src[z + 1, tile, pl.ds(first, 8), :] - u)
            total = (across + along) + (ahead - held[tile, part])
            held[tile, part] = ahead
            dst[out, tile, pl.ds(8 * part, 8), :] = (u + 0.12 * total) * rims[part]


def width_slope(field, z, slope):
    tiles = field.shape[1]
    lane = lax.broadcasted_iota(jnp.int32, (ROWS, LANES), 1)
    rows = pl.ds(OWN, 8)
    now = field[z, 0, rows, :]
    lowered, raised = pltpu.roll(now, LANES - 1, 1), pltpu.roll(now, 1, 1)
    earlier = 0.0
    for tile in range(tiles):
        if tile + 1 < tiles:
            later = field[z, tile + 1, rows, :]
            later_lowered, later_raised = pltpu.roll(later, LANES - 1, 1), pltpu.roll(later, 1, 1)
        else:
            later_lowered, later_raised = 0.0, None
        slope[z, tile] = jnp.where(lane == LANES - 1, later_lowered, lowered) - jnp.where(
            lane == 0, earlier, raised
        )
        earlier, lowered, raised = raised, later_lowered, later_raised


def diffuse(src, base, dst, planes, nexts, befores, held, rims, slope=None):
    for tile in range(src.shape[1]):
        for part in range(2):
            rows = pl.ds(base + 8 * part, 8)
            held[tile, part] = flux(src[1, tile, rows, :] - src[0, tile, rows, :])
    beside(src, base, 1, 1, nexts, befores)

    def pair(g, carry):
        for k in range(2):
            z = 2 * g + k + 1
            beside(src, base, z + 1, k, nexts, befores)
            diffuse_plane(src, base, z, 1 - k, nexts, befores, held, dst, z - 1, rims)
            if slope is not None:
                width_slope(dst, jnp.maximum(z - 3, 0), slope)
        return carry

    lax.fori_loop(0, planes // 2, pair, 0)
    if slope is not None:
        width_slope(dst, planes - 2, slope)


def render(
    edge_ref,
    colour_ref,
    opacity_ref,
    dir_ref,
    light_ref,
    vol_ref,
    low_ref,
    high_ref,
    top_ref,
    bottom_ref,
    top_corner_ref,
    bottom_corner_ref,
    out_ref,
    field,
    once,
    twice,
    slope,
    nexts,
    befores,
    held,
    rows_in,
    corners_in,
    sem,
    alpha_top,
    half,
):
    cells, tiles = vol_ref.shape[0], top_ref.shape[0]
    start = half * (vol_ref.shape[1] - tiles)
    own, part = pl.ds(BAND, 8), pl.ds(start, tiles)
    low, high = field.at[pl.ds(0, 3), :, own, :], field.at[pl.ds(cells + 3, 3), :, own, :]
    copies = [
        pltpu.make_async_copy(low_ref.at[:, part], low, sem.at[0]),
        pltpu.make_async_copy(high_ref.at[:, part], high, sem.at[1]),
        pltpu.make_async_copy(top_corner_ref.at[part], corners_in.at[0], sem.at[2]),
        pltpu.make_async_copy(bottom_corner_ref.at[part], corners_in.at[1], sem.at[3]),
        pltpu.make_async_copy(top_ref, rows_in.at[0], sem.at[4]),
        pltpu.make_async_copy(bottom_ref, rows_in.at[1], sem.at[5]),
        pltpu.make_async_copy(
            vol_ref.at[:, part], field.at[pl.ds(3, cells), :, own, :], sem.at[6]
        ),
    ]
    for copy in copies:
        copy.start()

    sub = lax.broadcasted_iota(jnp.int32, (ROWS, LANES), 0)
    keep_low, keep_high = edge_ref[0], edge_ref[1]
    keep_top, keep_bottom = edge_ref[2], edge_ref[3]
    rims = (
        jnp.where(sub < OWN, jnp.full((ROWS, LANES), keep_top), 1.0),
        jnp.where(sub >= OWN, jnp.full((ROWS, LANES), keep_bottom), 1.0),
    )

    zero = jnp.zeros((ROWS, LANES), F32)
    for k in range(3):
        for tile in range(tiles):
            for plane in (k, cells + 3 + k):
                field[plane, tile, 0:8, :] = zero
                field[plane, tile, 16:24, :] = zero
    for copy in copies[:4]:
        copy.wait()
    for k in range(3):
        for tile in range(tiles):
            field[k, tile, own, :] = field[k, tile, own, :] * keep_low
            field[cells + 3 + k, tile, own, :] = field[cells + 3 + k, tile, own, :] * keep_high
    for tile in range(tiles):
        for slot, (side, plane, away) in enumerate(CORNERS):
            at = (cells + 3 if side else 1) + plane
            keep = keep_high if side else keep_low
            field[at, tile, 7 - away : 8 - away, :] = corners_in[0, tile, slot : slot + 1, :] * (
                keep * keep_top
            )
            field[at, tile, 16 + away : 17 + away, :] = corners_in[
                1, tile, slot : slot + 1, :
            ] * (keep * keep_bottom)
    copies[4].wait()
    copies[5].wait()

    def rims_in(g, carry):
        at = pl.multiple_of(24 * g, 24)
        for tile in range(tiles):
            for k in range(8):
                field[8 * g + k + 3, tile, 5:8, :] = (
                    rows_in[0, tile, pl.ds(at + 3 * k, 3), :] * keep_top
                )
                field[8 * g + k + 3, tile, 16:19, :] = (
                    rows_in[1, tile, pl.ds(at + 3 * k, 3), :] * keep_bottom
                )
        return carry

    lax.fori_loop(0, cells // 8, rims_in, 0)
    copies[6].wait()

    diffuse(field, OWN, once, cells + 4, nexts, befores, held, rims)
    for k in range(2):
        for tile in range(tiles):
            for rows in (slice(0, 8), slice(8, 16)):
                once[k, tile, rows, :] = once[k, tile, rows, :] * keep_low
                once[cells + 2 + k, tile, rows, :] = once[cells + 2 + k, tile, rows, :] * keep_high
    diffuse(once, 0, twice, cells + 2, nexts, befores, held, rims, slope)
    own = pl.ds(OWN, 8)
    for tile in range(tiles):
        twice[0, tile, own, :] = twice[0, tile, own, :] * keep_low
        twice[cells + 1, tile, own, :] = twice[cells + 1, tile, own, :] * keep_high

    colour = [[colour_ref[c, j] for j in range(4)] for c in range(3)]
    opac = [opacity_ref[j] for j in range(4)]
    light = [[0.5 * dir_ref[l, d] for d in range(3)] for l in range(4)]

    def poly(c, v):
        return ((c[3] * v + c[2]) * v + c[1]) * v + c[0]

    def column(piece, carry):
        tile = piece + half * (tiles - out_ref.shape[0])

        def cell(z, state):
            through, sums, base_sums = state
            v = twice[z + 1, tile, own, :]
            g_z = twice[z + 2, tile, own, :] - twice[z, tile, own, :]
            g_h = twice[z + 1, tile, pl.ds(OWN + 1, 8), :] - twice[z + 1, tile, pl.ds(OWN - 1, 8), :]
            g_w = slope[z + 1, tile]
            inverse = lax.rsqrt(0.25 * (g_z * g_z + g_h * g_h + g_w * g_w) + 1.0)
            p = poly(opac, v)
            s = p * p
            opacity = (alpha_top * s) * inverse_of(1.0 + s)
            weight = through * opacity
            through = through - weight
            half = 0.5 * weight
            shaded = [half + half * jnp.tanh(poly(colour[c], v)) for c in range(3)]
            base_sums = [base_sums[c] + shaded[c] for c in range(3)]
            tilted = [inverse * shaded[c] for c in range(3)]
            new = []
            for l in range(4):
                facing = jnp.abs(g_z * light[l][0] + g_h * light[l][1] + g_w * light[l][2])
                for c in range(3):
                    new.append(sums[3 * l + c] + facing * tilted[c])
            return through, new, base_sums

        state = (jnp.ones((ROWS, LANES), F32), [zero] * 12, [zero] * 3)

        def group(g, state):
            for k in range(4):
                state = cell(g * 4 + k, state)
            return state

        through, sums, base_sums = lax.fori_loop(0, cells // 4, group, state)
        for l in range(4):
            for c in range(3):
                out_ref[piece, 3 * l + c] = light_ref[l, c] * (
                    0.2 * base_sums[c] + sums[3 * l + c]
                )
        out_ref[piece, 12] = 1.0 - through
        return carry

    lax.fori_loop(0, out_ref.shape[0], column, 0)


def fold(*refs):
    out_ref = refs[-1]
    for half, parts_ref in enumerate(refs[:-1]):
        slabs, channels = parts_ref.shape[0], parts_ref.shape[1]
        through = 1.0 - parts_ref[0, 12]
        total = [parts_ref[0, ch] for ch in range(channels)]
        for slab in range(1, slabs):
            total = [total[ch] + through * parts_ref[slab, ch] for ch in range(channels)]
            through = through * (1.0 - parts_ref[slab, 12])
        for ch in range(channels):
            out_ref[half, ch] = total[ch]


def spread(place_ref, *refs):
    pieces, out_ref, sem = refs[:-2], refs[-2], refs[-1]
    count = len(pieces)
    copies = []
    for step, ref in enumerate(pieces):
        offset = step if step <= count // 2 else count // 2 - step
        owner = lax.rem(place_ref[0] - offset + count, count)
        for half in range(2):
            copies.append(
                pltpu.make_async_copy(
                    ref.at[half], out_ref.at[:, half * count + owner], sem.at[2 * step + half]
                )
            )
    for copy in copies:
        copy.start()
    for copy in copies:
        copy.wait()


def in_vmem(count):
    return [pl.BlockSpec(memory_space=VMEM)] * count


def in_smem(count):
    return [pl.BlockSpec(memory_space=pltpu.SMEM)] * count


def anywhere(count):
    return [pl.BlockSpec(memory_space=pl.ANY)] * count


def shape(*dims):
    return jax.ShapeDtypeStruct(dims, F32)


def ring(axis, by):
    count = lax.axis_size(axis)
    return [(i, (i + by) % count) for i in range(count)]


def per_device(volume, colour_coef, opacity_coef, light_dir, light_colour):
    slabs, bands = lax.axis_size("depth"), lax.axis_size("height")
    cells, rows, width = volume.shape
    tiles = width // LANES
    slab, band = lax.axis_index("depth"), lax.axis_index("height")
    limit = pltpu.CompilerParams(vmem_limit_bytes=58 << 20)
    field = volume.reshape(cells, rows, tiles, LANES).transpose(0, 2, 1, 3)

    reach = tiles // 2 + 1
    down0, down1, up0, up1, first, last = pl.pallas_call(
        pack,
        out_shape=[shape(reach, 3 * cells, LANES)] * 4 + [shape(3, tiles, rows, LANES)] * 2,
        in_specs=anywhere(1),
        out_specs=anywhere(6),
        scratch_shapes=[
            VMEM((cells, tiles, rows, LANES), F32),
            VMEM((tiles, 3 * cells, LANES), F32),
            VMEM((tiles, 3 * cells, LANES), F32),
            DMA((cells // 8,)),
            DMA((2,)),
            DMA((cells // 2,)),
        ],
        compiler_params=limit,
        name="pack",
    )(field)
    low = lax.ppermute(last, "depth", ring("depth", 1))
    high = lax.ppermute(first, "depth", ring("depth", -1))
    tops = [lax.ppermute(down, "height", ring("height", 1)) for down in (down0, down1)]
    bottoms = [lax.ppermute(up, "height", ring("height", -1)) for up in (up0, up1)]
    corner_down, corner_up = pl.pallas_call(
        pack_corners,
        out_shape=[shape(tiles, rows, LANES)] * 2,
        in_specs=anywhere(2),
        out_specs=in_vmem(2),
        scratch_shapes=[VMEM((2, 2, tiles, rows, LANES), F32), DMA((2,))],
        compiler_params=limit,
        name="pack_corners",
    )(low, high)
    top_corner = lax.ppermute(corner_down, "height", ring("height", 1))
    bottom_corner = lax.ppermute(corner_up, "height", ring("height", -1))

    edges = jnp.stack([slab > 0, slab < slabs - 1, band > 0, band < bands - 1]).astype(F32)
    exchanged = []
    for half in range(2):
        partial = pl.pallas_call(
            functools.partial(render, alpha_top=2.0 / (cells * slabs), half=half),
            out_shape=shape(slabs, 13, rows, LANES),
            in_specs=in_smem(5) + anywhere(7),
            out_specs=pl.BlockSpec(memory_space=VMEM),
            scratch_shapes=[
                VMEM((cells + 6, reach, 24, LANES), F32),
                VMEM((cells + 4, reach, 16, LANES), F32),
                VMEM((cells + 2, reach, 16, LANES), F32),
                VMEM((cells + 1, reach, rows, LANES), F32),
                VMEM((2, reach, 2, rows, LANES), F32),
                VMEM((2, reach, 2, rows, LANES), F32),
                VMEM((reach, 2, rows, LANES), F32),
                VMEM((2, reach, 3 * cells, LANES), F32),
                VMEM((2, reach, rows, LANES), F32),
                DMA((7,)),
            ],
            compiler_params=limit,
            cost_estimate=pl.CostEstimate(
                flops=400_000_000, bytes_accessed=40_000_000, transcendentals=4_000_000
            ),
            name="render",
        )(
            edges,
            colour_coef,
            opacity_coef,
            light_dir,
            light_colour,
            field,
            low,
            high,
            tops[half],
            bottoms[half],
            top_corner,
            bottom_corner,
        )
        exchanged.append(lax.all_to_all(partial, "depth", 0, 0, tiled=True))
    own = pl.pallas_call(
        fold,
        out_shape=shape(2, 13, rows, LANES),
        in_specs=in_vmem(2),
        out_specs=pl.BlockSpec(memory_space=VMEM),
        compiler_params=limit,
        name="fold",
    )(*exchanged)
    from_below, from_above = [own], [own]
    for _ in range(slabs // 2):
        from_below.append(lax.ppermute(from_below[-1], "depth", ring("depth", 1)))
        from_above.append(lax.ppermute(from_above[-1], "depth", ring("depth", -1)))
    pieces = from_below + from_above[1 : slabs // 2]
    image = pl.pallas_call(
        spread,
        out_shape=shape(13, tiles, rows, LANES),
        in_specs=in_smem(1) + in_vmem(slabs),
        out_specs=pl.BlockSpec(memory_space=pl.ANY),
        scratch_shapes=[DMA((2 * slabs,))],
        compiler_params=limit,
        name="spread",
    )(slab[None], *pieces)
    return image.transpose(0, 2, 1, 3).reshape(13, rows, width)


def solution(mesh):
    placed = (P("depth", "height", None), P(), P(), P(), P())
    return jax.shard_map(
        per_device, mesh=mesh, in_specs=placed, out_specs=P(None, "height", None), check_vma=False
    )
```

```python
import functools

import jax
import jax.numpy as jnp
from jax import lax
from jax.experimental import pallas as pl
from jax.experimental.pallas import tpu as pltpu
from jax.sharding import PartitionSpec as P

VMEM = pltpu.VMEM
DMA = pltpu.SemaphoreType.DMA
F32 = jnp.float32
LANES = 128
ROWS = 8
BAND = 8
OWN = 4


def inverse_of(q):
    return pltpu.reciprocal(q, approx=True)


def flux(d):
    return d * inverse_of(d * d + 1.0)


CORNERS = ((0, 0), (1, 0), (0, 1))


def pack(vol_ref, down_ref, up_ref, first_ref, last_ref, *refs):
    corner_refs = refs[0:4]
    held, down, up, corners, in_sem, edge_sem, out_sem = refs[4:]
    cells, tiles = vol_ref.shape[0], vol_ref.shape[1]
    groups = cells // 8
    order = [0, groups - 1] + list(range(1, groups - 1))
    loads = {
        g: pltpu.make_async_copy(
            vol_ref.at[pl.ds(8 * g, 8)], held.at[pl.ds(8 * g, 8)], in_sem.at[g]
        )
        for g in order
    }
    edges = [
        pltpu.make_async_copy(held.at[pl.ds(0, 3)], first_ref, edge_sem.at[0]),
        pltpu.make_async_copy(held.at[pl.ds(cells - 3, 3)], last_ref, edge_sem.at[1]),
    ]
    edges += [
        pltpu.make_async_copy(corners.at[i], corner_refs[i], edge_sem.at[2 + i]) for i in range(4)
    ]
    for g in order:
        loads[g].start()
    stores = []
    for g in order:
        loads[g].wait()
        for k in range(8):
            z = 8 * g + k
            for tile in range(tiles):
                up[tile, 3 * z : 3 * z + 3, :] = held[z, tile, 0:3, :]
                down[tile, 3 * z : 3 * z + 3, :] = held[z, tile, 5:8, :]
        part = pl.ds(24 * g, 24)
        for i, (ref, out_ref) in enumerate(((down, down_ref), (up, up_ref))):
            copy = pltpu.make_async_copy(
                ref.at[:, part, :], out_ref.at[:, part, :], out_sem.at[2 * g + i]
            )
            copy.start()
            stores.append(copy)
        if g == groups - 1:
            for i, (z_far, row_far) in enumerate(((1, 1), (1, 0), (0, 1), (0, 0))):
                for tile in range(tiles):
                    for slot, (depth, row) in enumerate(CORNERS):
                        z = cells - 1 - depth if z_far else depth
                        r = ROWS - 1 - row if row_far else row
                        corners[i, tile, slot : slot + 1, :] = held[z, tile, r : r + 1, :]
                    corners[i, tile, 3:8, :] = jnp.zeros((5, LANES), F32)
            for copy in edges:
                copy.start()
    for copy in stores + edges:
        copy.wait()


def beside(src, base, z, parity, nexts, befores):
    tiles = src.shape[1]
    lane = lax.broadcasted_iota(jnp.int32, (ROWS, LANES), 1)
    for part in range(2):
        rows = pl.ds(base + 8 * part, 8)
        now = src[z, 0, rows, :]
        lowered, raised = pltpu.roll(now, LANES - 1, 1), pltpu.roll(now, 1, 1)
        earlier = 0.0
        for tile in range(tiles):
            if tile + 1 < tiles:
                later = src[z, tile + 1, rows, :]
                later_lowered = pltpu.roll(later, LANES - 1, 1)
                later_raised = pltpu.roll(later, 1, 1)
            else:
                later_lowered, later_raised = 0.0, None
            nexts[parity, tile, part] = jnp.where(lane == LANES - 1, later_lowered, lowered)
            befores[parity, tile, part] = jnp.where(lane == 0, earlier, raised)
            earlier, lowered, raised = raised, later_lowered, later_raised


def diffuse_plane(src, base, z, parity, nexts, befores, held, dst, out, rims):
    tiles = src.shape[1]
    sub = lax.broadcasted_iota(jnp.int32, (ROWS, LANES), 0)
    for tile in range(tiles):
        below = None
        for part in range(2):
            first = base + 8 * part
            u = src[z, tile, pl.ds(first, 8), :]
            across = flux(nexts[parity, tile, part] - u) + flux(befores[parity, tile, part] - u)
            if first + 9 <= src.shape[2]:
                above = src[z, tile, pl.ds(first + 1, 8), :]
            else:
                above = pltpu.roll(u, ROWS - 1, 0)
            up = flux(above - u)
            turned = pltpu.roll(up, 1, 0)
            along = up - (turned if part == 0 else jnp.where(sub == 0, below, turned))
            below = turned
            ahead = flux(src[z + 1, tile, pl.ds(first, 8), :] - u)
            total = (across + along) + (ahead - held[tile, part])
            held[tile, part] = ahead
            dst[out, tile, pl.ds(8 * part, 8), :] = (u + 0.12 * total) * rims[part]


def width_slope(field, z, slope):
    tiles = field.shape[1]
    lane = lax.broadcasted_iota(jnp.int32, (ROWS, LANES), 1)
    rows = pl.ds(OWN, 8)
    now = field[z, 0, rows, :]
    lowered, raised = pltpu.roll(now, LANES - 1, 1), pltpu.roll(now, 1, 1)
    earlier = 0.0
    for tile in range(tiles):
        if tile + 1 < tiles:
            later = field[z, tile + 1, rows, :]
            later_lowered, later_raised = pltpu.roll(later, LANES - 1, 1), pltpu.roll(later, 1, 1)
        else:
            later_lowered, later_raised = 0.0, None
        slope[z, tile] = jnp.where(lane == LANES - 1, later_lowered, lowered) - jnp.where(
            lane == 0, earlier, raised
        )
        earlier, lowered, raised = raised, later_lowered, later_raised


def diffuse(src, base, dst, planes, nexts, befores, held, rims, slope=None):
    for tile in range(src.shape[1]):
        for part in range(2):
            rows = pl.ds(base + 8 * part, 8)
            held[tile, part] = flux(src[1, tile, rows, :] - src[0, tile, rows, :])
    beside(src, base, 1, 1, nexts, befores)

    def pair(g, carry):
        for k in range(2):
            z = 2 * g + k + 1
            beside(src, base, z + 1, k, nexts, befores)
            diffuse_plane(src, base, z, 1 - k, nexts, befores, held, dst, z - 1, rims)
            if slope is not None:
                width_slope(dst, jnp.maximum(z - 3, 0), slope)
        return carry

    lax.fori_loop(0, planes // 2, pair, 0)
    if slope is not None:
        width_slope(dst, planes - 2, slope)


def render(
    edge_ref,
    colour_ref,
    opacity_ref,
    dir_ref,
    light_ref,
    vol_ref,
    low_ref,
    high_ref,
    top_ref,
    bottom_ref,
    low_top_ref,
    low_bottom_ref,
    high_top_ref,
    high_bottom_ref,
    out_ref,
    twice_ref,
    slope_ref,
    field,
    once,
    twice,
    slope,
    nexts,
    befores,
    held,
    rows_in,
    corners_in,
    sem,
    later_sem,
    alpha_top,
):
    cells, tiles = vol_ref.shape[0], vol_ref.shape[1]
    own = pl.ds(BAND, 8)
    copies = [
        pltpu.make_async_copy(low_ref, field.at[pl.ds(0, 3), :, own, :], sem.at[0]),
        pltpu.make_async_copy(high_ref, field.at[pl.ds(cells + 3, 3), :, own, :], sem.at[1]),
        pltpu.make_async_copy(low_top_ref, corners_in.at[0], sem.at[2]),
        pltpu.make_async_copy(low_bottom_ref, corners_in.at[1], sem.at[3]),
        pltpu.make_async_copy(high_top_ref, corners_in.at[2], sem.at[4]),
        pltpu.make_async_copy(high_bottom_ref, corners_in.at[3], sem.at[5]),
        pltpu.make_async_copy(top_ref, rows_in.at[0], sem.at[6]),
        pltpu.make_async_copy(bottom_ref, rows_in.at[1], sem.at[7]),
        pltpu.make_async_copy(vol_ref, field.at[pl.ds(3, cells), :, own, :], sem.at[8]),
    ]
    for copy in copies:
        copy.start()

    sub = lax.broadcasted_iota(jnp.int32, (ROWS, LANES), 0)
    keep_low, keep_high = edge_ref[0], edge_ref[1]
    keep_top, keep_bottom = edge_ref[2], edge_ref[3]
    rims = (
        jnp.where(sub < OWN, jnp.full((ROWS, LANES), keep_top), 1.0),
        jnp.where(sub >= OWN, jnp.full((ROWS, LANES), keep_bottom), 1.0),
    )

    zero = jnp.zeros((ROWS, LANES), F32)
    for k in range(3):
        for tile in range(tiles):
            for plane in (k, cells + 3 + k):
                field[plane, tile, 0:8, :] = zero
                field[plane, tile, 16:24, :] = zero
    for copy in copies[:6]:
        copy.wait()
    for k in range(3):
        for tile in range(tiles):
            field[k, tile, own, :] = field[k, tile, own, :] * keep_low
            field[cells + 3 + k, tile, own, :] = field[cells + 3 + k, tile, own, :] * keep_high
    for i in range(4):
        keep = (keep_high if i // 2 else keep_low) * (keep_bottom if i % 2 else keep_top)
        for tile in range(tiles):
            for slot, (depth, row) in enumerate(CORNERS):
                at = cells + 3 + depth if i // 2 else 2 - depth
                r = 16 + row if i % 2 else 7 - row
                field[at, tile, r : r + 1, :] = corners_in[i, tile, slot : slot + 1, :] * keep
    copies[6].wait()
    copies[7].wait()

    def rims_in(g, carry):
        at = pl.multiple_of(24 * g, 24)
        for tile in range(tiles):
            for k in range(8):
                field[8 * g + k + 3, tile, 5:8, :] = (
                    rows_in[0, tile, pl.ds(at + 3 * k, 3), :] * keep_top
                )
                field[8 * g + k + 3, tile, 16:19, :] = (
                    rows_in[1, tile, pl.ds(at + 3 * k, 3), :] * keep_bottom
                )
        return carry

    lax.fori_loop(0, cells // 8, rims_in, 0)
    copies[8].wait()

    diffuse(field, OWN, once, cells + 4, nexts, befores, held, rims)
    for k in range(2):
        for tile in range(tiles):
            for rows in (slice(0, 8), slice(8, 16)):
                once[k, tile, rows, :] = once[k, tile, rows, :] * keep_low
                once[cells + 2 + k, tile, rows, :] = once[cells + 2 + k, tile, rows, :] * keep_high
    diffuse(once, 0, twice, cells + 2, nexts, befores, held, rims, slope)
    own = pl.ds(OWN, 8)
    for tile in range(tiles):
        twice[0, tile, own, :] = twice[0, tile, own, :] * keep_low
        twice[cells + 1, tile, own, :] = twice[cells + 1, tile, own, :] * keep_high

    half = out_ref.shape[0]
    later = [
        pltpu.make_async_copy(twice.at[:, pl.ds(half, half)], twice_ref, later_sem.at[0]),
        pltpu.make_async_copy(slope.at[:, pl.ds(half, half)], slope_ref, later_sem.at[1]),
    ]
    for copy in later:
        copy.start()
    shade(colour_ref, opacity_ref, dir_ref, light_ref, twice, slope, out_ref, alpha_top)
    for copy in later:
        copy.wait()


def render_rest(
    colour_ref,
    opacity_ref,
    dir_ref,
    light_ref,
    twice_ref,
    slope_ref,
    out_ref,
    twice,
    slope,
    sem,
    alpha_top,
):
    def load(tile):
        return [
            pltpu.make_async_copy(twice_ref.at[:, tile], twice.at[:, tile], sem.at[0, tile]),
            pltpu.make_async_copy(slope_ref.at[:, tile], slope.at[:, tile], sem.at[1, tile]),
        ]

    for tile in range(out_ref.shape[0]):
        for copy in load(tile):
            copy.start()

    def ready(tile):
        for copy in load(tile):
            copy.wait()

    shade(colour_ref, opacity_ref, dir_ref, light_ref, twice, slope, out_ref, alpha_top, ready)


def shade(
    colour_ref, opacity_ref, dir_ref, light_ref, twice, slope, out_ref, alpha_top, ready=None
):
    cells = slope.shape[0] - 1
    own = pl.ds(OWN, 8)
    zero = jnp.zeros((ROWS, LANES), F32)
    colour = [[colour_ref[c, j] for j in range(4)] for c in range(3)]
    opac = [opacity_ref[j] for j in range(4)]
    light = [[0.5 * dir_ref[l, d] for d in range(3)] for l in range(4)]

    def poly(c, v):
        return ((c[3] * v + c[2]) * v + c[1]) * v + c[0]

    def column(tile, carry):
        if ready is not None:
            ready(tile)

        def cell(z, state):
            through, sums, base_sums = state
            v = twice[z + 1, tile, own, :]
            g_z = twice[z + 2, tile, own, :] - twice[z, tile, own, :]
            g_h = twice[z + 1, tile, pl.ds(OWN + 1, 8), :] - twice[z + 1, tile, pl.ds(OWN - 1, 8), :]
            g_w = slope[z + 1, tile]
            inverse = lax.rsqrt(0.25 * (g_z * g_z + g_h * g_h + g_w * g_w) + 1.0)
            p = poly(opac, v)
            s = p * p
            opacity = (alpha_top * s) * inverse_of(1.0 + s)
            weight = through * opacity
            through = through - weight
            half = 0.5 * weight
            shaded = [half + half * jnp.tanh(poly(colour[c], v)) for c in range(3)]
            base_sums = [base_sums[c] + shaded[c] for c in range(3)]
            tilted = [inverse * shaded[c] for c in range(3)]
            new = []
            for l in range(4):
                facing = jnp.abs(g_z * light[l][0] + g_h * light[l][1] + g_w * light[l][2])
                for c in range(3):
                    new.append(sums[3 * l + c] + facing * tilted[c])
            return through, new, base_sums

        state = (jnp.ones((ROWS, LANES), F32), [zero] * 12, [zero] * 3)

        def group(g, state):
            for k in range(8):
                state = cell(g * 8 + k, state)
            return state

        through, sums, base_sums = lax.fori_loop(0, cells // 8, group, state)
        for l in range(4):
            for c in range(3):
                out_ref[tile, 3 * l + c] = light_ref[l, c] * (
                    0.2 * base_sums[c] + sums[3 * l + c]
                )
        out_ref[tile, 12] = 1.0 - through
        return carry

    lax.fori_loop(0, out_ref.shape[0], column, 0)


def fold(parts_ref, *refs):
    if len(refs) > 1:
        first_ref, both_ref = refs
        both_ref[0] = first_ref[...]
        out_ref = both_ref.at[1]
    else:
        (out_ref,) = refs
    slabs, channels = parts_ref.shape[0], parts_ref.shape[1]
    through = 1.0 - parts_ref[0, 12]
    total = [parts_ref[0, ch] for ch in range(channels)]
    for slab in range(1, slabs):
        total = [total[ch] + through * parts_ref[slab, ch] for ch in range(channels)]
        through = through * (1.0 - parts_ref[slab, 12])
    for ch in range(channels):
        out_ref[ch] = total[ch]


def spread(count, offsets, place_ref, *refs):
    pieces, out_ref, sem = refs[: len(offsets)], refs[-2], refs[-1]
    copies = []
    for i, ref in enumerate(pieces):
        owner = lax.rem(place_ref[0] - offsets[i] + count, count)
        for half in range(2):
            copies.append(
                pltpu.make_async_copy(
                    ref.at[half], out_ref.at[:, half * count + owner], sem.at[2 * i + half]
                )
            )
    for copy in copies:
        copy.start()
    for copy in copies:
        copy.wait()


def in_vmem(count):
    return [pl.BlockSpec(memory_space=VMEM)] * count


def in_smem(count):
    return [pl.BlockSpec(memory_space=pltpu.SMEM)] * count


def anywhere(count):
    return [pl.BlockSpec(memory_space=pl.ANY)] * count


def shape(*dims):
    return jax.ShapeDtypeStruct(dims, F32)


def ring(axis, by):
    count = lax.axis_size(axis)
    return [(i, (i + by) % count) for i in range(count)]


def per_device(volume, colour_coef, opacity_coef, light_dir, light_colour):
    slabs, bands = lax.axis_size("depth"), lax.axis_size("height")
    cells, rows, width = volume.shape
    tiles = width // LANES
    slab, band = lax.axis_index("depth"), lax.axis_index("height")
    limit = pltpu.CompilerParams(vmem_limit_bytes=58 << 20)
    field = volume.reshape(cells, rows, tiles, LANES).transpose(0, 2, 1, 3)

    packed = pl.pallas_call(
        pack,
        out_shape=[shape(tiles, 3 * cells, LANES)] * 2
        + [shape(3, tiles, rows, LANES)] * 2
        + [shape(tiles, rows, LANES)] * 4,
        in_specs=anywhere(1),
        out_specs=anywhere(8),
        scratch_shapes=[
            VMEM((cells, tiles, rows, LANES), F32),
            VMEM((tiles, 3 * cells, LANES), F32),
            VMEM((tiles, 3 * cells, LANES), F32),
            VMEM((4, tiles, rows, LANES), F32),
            DMA((cells // 8,)),
            DMA((6,)),
            DMA((cells // 4,)),
        ],
        compiler_params=limit,
        name="pack",
    )(field)
    down, up, first, last = packed[:4]
    top = lax.ppermute(down, "height", ring("height", 1))
    bottom = lax.ppermute(up, "height", ring("height", -1))
    low = lax.ppermute(last, "depth", ring("depth", 1))
    high = lax.ppermute(first, "depth", ring("depth", -1))
    corners = []
    for i, (dz, dh) in enumerate(((1, 1), (1, -1), (-1, 1), (-1, -1))):
        pairs = [
            (z * bands + h, (z + dz) % slabs * bands + (h + dh) % bands)
            for z in range(slabs)
            for h in range(bands)
        ]
        corners.append(lax.ppermute(packed[4 + i], ("depth", "height"), pairs))

    edges = jnp.stack([slab > 0, slab < slabs - 1, band > 0, band < bands - 1]).astype(F32)
    half = tiles // 2
    alpha_top = 2.0 / (cells * slabs)
    partial, twice, slope = pl.pallas_call(
        functools.partial(render, alpha_top=alpha_top),
        out_shape=[
            shape(half, 13, rows, LANES),
            shape(cells + 2, half, 16, LANES),
            shape(cells + 1, half, rows, LANES),
        ],
        in_specs=in_smem(5) + anywhere(9),
        out_specs=in_vmem(1) + anywhere(2),
        scratch_shapes=[
            VMEM((cells + 6, tiles, 24, LANES), F32),
            VMEM((cells + 4, tiles, 16, LANES), F32),
            VMEM((cells + 2, tiles, 16, LANES), F32),
            VMEM((cells + 1, tiles, rows, LANES), F32),
            VMEM((2, tiles, 2, rows, LANES), F32),
            VMEM((2, tiles, 2, rows, LANES), F32),
            VMEM((tiles, 2, rows, LANES), F32),
            VMEM((2, tiles, 3 * cells, LANES), F32),
            VMEM((4, tiles, rows, LANES), F32),
            DMA((9,)),
            DMA((2,)),
        ],
        compiler_params=limit,
        cost_estimate=pl.CostEstimate(
            flops=400_000_000, bytes_accessed=40_000_000, transcendentals=4_000_000
        ),
        name="render",
    )(
        edges,
        colour_coef,
        opacity_coef,
        light_dir,
        light_colour,
        field,
        low,
        high,
        top,
        bottom,
        *corners,
    )
    partial_rest = pl.pallas_call(
        functools.partial(render_rest, alpha_top=alpha_top),
        out_shape=shape(half, 13, rows, LANES),
        in_specs=in_smem(4) + anywhere(2),
        out_specs=pl.BlockSpec(memory_space=VMEM),
        scratch_shapes=[
            VMEM((cells + 2, half, 16, LANES), F32),
            VMEM((cells + 1, half, rows, LANES), F32),
            DMA((2, half)),
        ],
        compiler_params=limit,
        cost_estimate=pl.CostEstimate(
            flops=50_000_000, bytes_accessed=10_000_000, transcendentals=1_000_000
        ),
        name="render_rest",
    )(colour_coef, opacity_coef, light_dir, light_colour, twice, slope)
    count = slabs // 2
    own = []
    for value in (partial, partial_rest):
        exchanged = lax.all_to_all(value, "depth", 0, 0, tiled=True)
        image_shape = (2,) * len(own) + (13, rows, LANES)
        own = [
            pl.pallas_call(
                fold,
                out_shape=shape(*image_shape),
                in_specs=in_vmem(1 + len(own)),
                out_specs=pl.BlockSpec(memory_space=VMEM),
                compiler_params=limit,
                cost_estimate=pl.CostEstimate(
                    flops=10_000_000, bytes_accessed=2_000_000, transcendentals=0
                ),
                name="fold",
            )(exchanged, *own)
        ]
    (both,) = own
    from_below, from_above = [both], [both]
    for _ in range(count):
        from_below.append(lax.ppermute(from_below[-1], "depth", ring("depth", 1)))
        from_above.append(lax.ppermute(from_above[-1], "depth", ring("depth", -1)))
    pieces = from_below + from_above[1:count]
    image = pl.pallas_call(
        functools.partial(spread, slabs, [k for k in range(count + 1)] + [-k for k in range(1, count)]),
        out_shape=shape(13, tiles, rows, LANES),
        in_specs=in_smem(1) + in_vmem(slabs),
        out_specs=pl.BlockSpec(memory_space=pl.ANY),
        scratch_shapes=[DMA((2 * slabs,))],
        compiler_params=limit,
        name="spread",
    )(slab[None], *pieces)
    return image.transpose(0, 2, 1, 3).reshape(13, rows, width)


def solution(mesh):
    placed = (P("depth", "height", None), P(), P(), P(), P())
    return jax.shard_map(
        per_device, mesh=mesh, in_specs=placed, out_specs=P(None, "height", None), check_vma=False
    )
```

```python
import functools

import jax
import jax.numpy as jnp
from jax import lax
from jax.experimental import pallas as pl
from jax.experimental.pallas import tpu as pltpu
from jax.sharding import PartitionSpec as P

VMEM = pltpu.VMEM
DMA = pltpu.SemaphoreType.DMA
F32 = jnp.float32
LANES = 128
ROWS = 8
BAND = 8
OWN = 4


def inverse_of(q):
    return pltpu.reciprocal(q, approx=True)


def flux(d):
    return d * inverse_of(d * d + 1.0)


def pack(vol_ref, down_ref, up_ref, first_ref, last_ref, held, down, up, in_sem, edge_sem, out_sem):
    cells, tiles = vol_ref.shape[0], vol_ref.shape[1]
    groups = cells // 8
    loads = [
        pltpu.make_async_copy(vol_ref.at[pl.ds(8 * g, 8)], held.at[pl.ds(8 * g, 8)], in_sem.at[g])
        for g in range(groups)
    ]
    edges = [
        pltpu.make_async_copy(held.at[pl.ds(0, 3)], first_ref, edge_sem.at[0]),
        pltpu.make_async_copy(held.at[pl.ds(cells - 3, 3)], last_ref, edge_sem.at[1]),
    ]
    for copy in loads:
        copy.start()
    stores = []
    for g in range(groups):
        loads[g].wait()
        if g == 0:
            edges[0].start()
        if g == groups - 1:
            edges[1].start()
        for k in range(8):
            z = 8 * g + k
            for tile in range(tiles):
                up[tile, 3 * z : 3 * z + 3, :] = held[z, tile, 0:3, :]
                down[tile, 3 * z : 3 * z + 3, :] = held[z, tile, 5:8, :]
        part = pl.ds(24 * g, 24)
        for i, (ref, out_ref) in enumerate(((down, down_ref), (up, up_ref))):
            copy = pltpu.make_async_copy(
                ref.at[:, part, :], out_ref.at[:, part, :], out_sem.at[2 * g + i]
            )
            copy.start()
            stores.append(copy)
    for copy in stores + edges:
        copy.wait()


CORNERS = ((0, 1, 0), (0, 0, 0), (0, 1, 1), (1, 0, 0), (1, 1, 0), (1, 0, 1))


def pack_corners(low_ref, high_ref, down_ref, up_ref, near, sem):
    tiles = low_ref.shape[1]
    copies = [
        pltpu.make_async_copy(low_ref.at[pl.ds(1, 2)], near.at[0], sem.at[0]),
        pltpu.make_async_copy(high_ref.at[pl.ds(0, 2)], near.at[1], sem.at[1]),
    ]
    for copy in copies:
        copy.start()
    for copy in copies:
        copy.wait()
    zero = jnp.zeros((2, LANES), F32)
    for tile in range(tiles):
        for slot, (side, plane, depth) in enumerate(CORNERS):
            up_ref[tile, slot : slot + 1, :] = near[side, plane, tile, depth : depth + 1, :]
            down_ref[tile, slot : slot + 1, :] = near[side, plane, tile, 7 - depth : 8 - depth, :]
        up_ref[tile, 6:8, :] = zero
        down_ref[tile, 6:8, :] = zero


def beside(src, base, z, parity, nexts, befores):
    tiles = src.shape[1]
    lane = lax.broadcasted_iota(jnp.int32, (ROWS, LANES), 1)
    for part in range(2):
        rows = pl.ds(base + 8 * part, 8)
        now = src[z, 0, rows, :]
        lowered, raised = pltpu.roll(now, LANES - 1, 1), pltpu.roll(now, 1, 1)
        earlier = 0.0
        for tile in range(tiles):
            if tile + 1 < tiles:
                later = src[z, tile + 1, rows, :]
                later_lowered = pltpu.roll(later, LANES - 1, 1)
                later_raised = pltpu.roll(later, 1, 1)
            else:
                later_lowered, later_raised = 0.0, None
            nexts[parity, tile, part] = jnp.where(lane == LANES - 1, later_lowered, lowered)
            befores[parity, tile, part] = jnp.where(lane == 0, earlier, raised)
            earlier, lowered, raised = raised, later_lowered, later_raised


def diffuse_plane(src, base, z, parity, nexts, befores, held, dst, out, rims):
    tiles = src.shape[1]
    sub = lax.broadcasted_iota(jnp.int32, (ROWS, LANES), 0)
    for tile in range(tiles):
        below = None
        for part in range(2):
            first = base + 8 * part
            u = src[z, tile, pl.ds(first, 8), :]
            across = flux(nexts[parity, tile, part] - u) + flux(befores[parity, tile, part] - u)
            if first + 9 <= src.shape[2]:
                above = src[z, tile, pl.ds(first + 1, 8), :]
            else:
                above = pltpu.roll(u, ROWS - 1, 0)
            up = flux(above - u)
            turned = pltpu.roll(up, 1, 0)
            along = up - (turned if part == 0 else jnp.where(sub == 0, below, turned))
            below = turned
            ahead = flux(src[z + 1, tile, pl.ds(first, 8), :] - u)
            total = (across + along) + (ahead - held[tile, part])
            held[tile, part] = ahead
            dst[out, tile, pl.ds(8 * part, 8), :] = (u + 0.12 * total) * rims[part]


def width_slope(field, z, slope):
    tiles = field.shape[1]
    lane = lax.broadcasted_iota(jnp.int32, (ROWS, LANES), 1)
    rows = pl.ds(OWN, 8)
    now = field[z, 0, rows, :]
    lowered, raised = pltpu.roll(now, LANES - 1, 1), pltpu.roll(now, 1, 1)
    earlier = 0.0
    for tile in range(tiles):
        if tile + 1 < tiles:
            later = field[z, tile + 1, rows, :]
            later_lowered, later_raised = pltpu.roll(later, LANES - 1, 1), pltpu.roll(later, 1, 1)
        else:
            later_lowered, later_raised = 0.0, None
        slope[z, tile] = jnp.where(lane == LANES - 1, later_lowered, lowered) - jnp.where(
            lane == 0, earlier, raised
        )
        earlier, lowered, raised = raised, later_lowered, later_raised


def diffuse(src, base, dst, planes, nexts, befores, held, rims, slope=None):
    for tile in range(src.shape[1]):
        for part in range(2):
            rows = pl.ds(base + 8 * part, 8)
            held[tile, part] = flux(src[1, tile, rows, :] - src[0, tile, rows, :])
    beside(src, base, 1, 1, nexts, befores)

    def pair(g, carry):
        for k in range(2):
            z = 2 * g + k + 1
            beside(src, base, z + 1, k, nexts, befores)
            diffuse_plane(src, base, z, 1 - k, nexts, befores, held, dst, z - 1, rims)
            if slope is not None:
                width_slope(dst, jnp.maximum(z - 3, 0), slope)
        return carry

    lax.fori_loop(0, planes // 2, pair, 0)
    if slope is not None:
        width_slope(dst, planes - 2, slope)


def render(
    edge_ref,
    colour_ref,
    opacity_ref,
    dir_ref,
    light_ref,
    vol_ref,
    low_ref,
    high_ref,
    top_ref,
    bottom_ref,
    top_corner_ref,
    bottom_corner_ref,
    out_ref,
    field,
    once,
    twice,
    slope,
    nexts,
    befores,
    held,
    rows_in,
    corners_in,
    sem,
    alpha_top,
):
    cells, tiles = vol_ref.shape[0], vol_ref.shape[1]
    own = pl.ds(BAND, 8)
    copies = [
        pltpu.make_async_copy(low_ref, field.at[pl.ds(0, 3), :, own, :], sem.at[0]),
        pltpu.make_async_copy(high_ref, field.at[pl.ds(cells + 3, 3), :, own, :], sem.at[1]),
        pltpu.make_async_copy(top_corner_ref, corners_in.at[0], sem.at[2]),
        pltpu.make_async_copy(bottom_corner_ref, corners_in.at[1], sem.at[3]),
        pltpu.make_async_copy(top_ref, rows_in.at[0], sem.at[4]),
        pltpu.make_async_copy(bottom_ref, rows_in.at[1], sem.at[5]),
        pltpu.make_async_copy(vol_ref, field.at[pl.ds(3, cells), :, own, :], sem.at[6]),
    ]
    for copy in copies:
        copy.start()

    sub = lax.broadcasted_iota(jnp.int32, (ROWS, LANES), 0)
    keep_low, keep_high = edge_ref[0], edge_ref[1]
    keep_top, keep_bottom = edge_ref[2], edge_ref[3]
    rims = (
        jnp.where(sub < OWN, jnp.full((ROWS, LANES), keep_top), 1.0),
        jnp.where(sub >= OWN, jnp.full((ROWS, LANES), keep_bottom), 1.0),
    )

    zero = jnp.zeros((ROWS, LANES), F32)
    for k in range(3):
        for tile in range(tiles):
            for plane in (k, cells + 3 + k):
                field[plane, tile, 0:8, :] = zero
                field[plane, tile, 16:24, :] = zero
    for copy in copies[:4]:
        copy.wait()
    for k in range(3):
        for tile in range(tiles):
            field[k, tile, own, :] = field[k, tile, own, :] * keep_low
            field[cells + 3 + k, tile, own, :] = field[cells + 3 + k, tile, own, :] * keep_high
    for tile in range(tiles):
        for slot, (side, plane, away) in enumerate(CORNERS):
            at = (cells + 3 if side else 1) + plane
            keep = keep_high if side else keep_low
            field[at, tile, 7 - away : 8 - away, :] = corners_in[0, tile, slot : slot + 1, :] * (
                keep * keep_top
            )
            field[at, tile, 16 + away : 17 + away, :] = corners_in[
                1, tile, slot : slot + 1, :
            ] * (keep * keep_bottom)
    copies[4].wait()
    copies[5].wait()

    def rims_in(g, carry):
        at = pl.multiple_of(24 * g, 24)
        for tile in range(tiles):
            for k in range(8):
                field[8 * g + k + 3, tile, 5:8, :] = (
                    rows_in[0, tile, pl.ds(at + 3 * k, 3), :] * keep_top
                )
                field[8 * g + k + 3, tile, 16:19, :] = (
                    rows_in[1, tile, pl.ds(at + 3 * k, 3), :] * keep_bottom
                )
        return carry

    lax.fori_loop(0, cells // 8, rims_in, 0)
    copies[6].wait()

    diffuse(field, OWN, once, cells + 4, nexts, befores, held, rims)
    for k in range(2):
        for tile in range(tiles):
            for rows in (slice(0, 8), slice(8, 16)):
                once[k, tile, rows, :] = once[k, tile, rows, :] * keep_low
                once[cells + 2 + k, tile, rows, :] = once[cells + 2 + k, tile, rows, :] * keep_high
    diffuse(once, 0, twice, cells + 2, nexts, befores, held, rims, slope)
    own = pl.ds(OWN, 8)
    for tile in range(tiles):
        twice[0, tile, own, :] = twice[0, tile, own, :] * keep_low
        twice[cells + 1, tile, own, :] = twice[cells + 1, tile, own, :] * keep_high

    colour = [[colour_ref[c, j] for j in range(4)] for c in range(3)]
    opac = [opacity_ref[j] for j in range(4)]
    light = [[0.5 * dir_ref[l, d] for d in range(3)] for l in range(4)]

    def poly(c, v):
        return ((c[3] * v + c[2]) * v + c[1]) * v + c[0]

    def column(tile, carry):
        def cell(z, state):
            through, sums, base_sums = state
            v = twice[z + 1, tile, own, :]
            g_z = twice[z + 2, tile, own, :] - twice[z, tile, own, :]
            g_h = twice[z + 1, tile, pl.ds(OWN + 1, 8), :] - twice[z + 1, tile, pl.ds(OWN - 1, 8), :]
            g_w = slope[z + 1, tile]
            inverse = lax.rsqrt(0.25 * (g_z * g_z + g_h * g_h + g_w * g_w) + 1.0)
            p = poly(opac, v)
            s = p * p
            opacity = (alpha_top * s) * inverse_of(1.0 + s)
            weight = through * opacity
            through = through - weight
            half = 0.5 * weight
            shaded = [half + half * jnp.tanh(poly(colour[c], v)) for c in range(3)]
            base_sums = [base_sums[c] + shaded[c] for c in range(3)]
            tilted = [inverse * shaded[c] for c in range(3)]
            new = []
            for l in range(4):
                facing = jnp.abs(g_z * light[l][0] + g_h * light[l][1] + g_w * light[l][2])
                for c in range(3):
                    new.append(sums[3 * l + c] + facing * tilted[c])
            return through, new, base_sums

        state = (jnp.ones((ROWS, LANES), F32), [zero] * 12, [zero] * 3)

        def group(g, state):
            for k in range(8):
                state = cell(g * 8 + k, state)
            return state

        through, sums, base_sums = lax.fori_loop(0, cells // 8, group, state)
        for l in range(4):
            for c in range(3):
                out_ref[tile // 2, 3 * l + c, tile % 2] = light_ref[l, c] * (
                    0.2 * base_sums[c] + sums[3 * l + c]
                )
        out_ref[tile // 2, 12, tile % 2] = 1.0 - through
        return carry

    lax.fori_loop(0, tiles, column, 0)


def fold(parts_ref, out_ref):
    slabs, channels = parts_ref.shape[0], parts_ref.shape[1]
    for tile in range(parts_ref.shape[2]):
        through = 1.0 - parts_ref[0, 12, tile]
        total = [parts_ref[0, ch, tile] for ch in range(channels)]
        for slab in range(1, slabs):
            total = [total[ch] + through * parts_ref[slab, ch, tile] for ch in range(channels)]
            through = through * (1.0 - parts_ref[slab, 12, tile])
        for ch in range(channels):
            out_ref[ch, tile] = total[ch]


def spread(count, offsets, place_ref, *refs):
    pieces, out_ref, sem = refs[: len(offsets)], refs[-2], refs[-1]
    tiles = out_ref.shape[1] // count
    copies = []
    for i, ref in enumerate(pieces):
        owner = lax.rem(place_ref[0] - offsets[i] + count, count)
        copies.append(
            pltpu.make_async_copy(ref, out_ref.at[:, pl.ds(owner * tiles, tiles)], sem.at[i])
        )
    for copy in copies:
        copy.start()
    for copy in copies:
        copy.wait()


def in_vmem(count):
    return [pl.BlockSpec(memory_space=VMEM)] * count


def in_smem(count):
    return [pl.BlockSpec(memory_space=pltpu.SMEM)] * count


def anywhere(count):
    return [pl.BlockSpec(memory_space=pl.ANY)] * count


def shape(*dims):
    return jax.ShapeDtypeStruct(dims, F32)


def ring(axis, by):
    count = lax.axis_size(axis)
    return [(i, (i + by) % count) for i in range(count)]


def per_device(volume, colour_coef, opacity_coef, light_dir, light_colour):
    slabs, bands = lax.axis_size("depth"), lax.axis_size("height")
    cells, rows, width = volume.shape
    tiles = width // LANES
    slab, band = lax.axis_index("depth"), lax.axis_index("height")
    limit = pltpu.CompilerParams(vmem_limit_bytes=63 << 20)
    field = volume.reshape(cells, rows, tiles, LANES).transpose(0, 2, 1, 3)

    down, up, first, last = pl.pallas_call(
        pack,
        out_shape=[shape(tiles, 3 * cells, LANES)] * 2 + [shape(3, tiles, rows, LANES)] * 2,
        in_specs=anywhere(1),
        out_specs=anywhere(4),
        scratch_shapes=[
            VMEM((cells, tiles, rows, LANES), F32),
            VMEM((tiles, 3 * cells, LANES), F32),
            VMEM((tiles, 3 * cells, LANES), F32),
            DMA((cells // 8,)),
            DMA((2,)),
            DMA((cells // 4,)),
        ],
        compiler_params=limit,
        name="pack",
    )(field)
    low = lax.ppermute(last, "depth", ring("depth", 1))
    high = lax.ppermute(first, "depth", ring("depth", -1))
    top = lax.ppermute(down, "height", ring("height", 1))
    bottom = lax.ppermute(up, "height", ring("height", -1))
    corner_down, corner_up = pl.pallas_call(
        pack_corners,
        out_shape=[shape(tiles, rows, LANES)] * 2,
        in_specs=anywhere(2),
        out_specs=in_vmem(2),
        scratch_shapes=[VMEM((2, 2, tiles, rows, LANES), F32), DMA((2,))],
        compiler_params=limit,
        cost_estimate=pl.CostEstimate(
            flops=400_000_000, bytes_accessed=80_000_000, transcendentals=0
        ),
        name="pack_corners",
    )(low, high)
    top_corner = lax.ppermute(corner_down, "height", ring("height", 1))
    bottom_corner = lax.ppermute(corner_up, "height", ring("height", -1))

    edges = jnp.stack([slab > 0, slab < slabs - 1, band > 0, band < bands - 1]).astype(F32)
    partial = pl.pallas_call(
        functools.partial(render, alpha_top=2.0 / (cells * slabs)),
        out_shape=shape(slabs, 13, tiles // slabs, rows, LANES),
        in_specs=in_smem(5) + anywhere(7),
        out_specs=pl.BlockSpec(memory_space=VMEM),
        scratch_shapes=[
            VMEM((cells + 6, tiles, 24, LANES), F32),
            VMEM((cells + 4, tiles, 16, LANES), F32),
            VMEM((cells + 2, tiles, 16, LANES), F32),
            VMEM((cells + 1, tiles, rows, LANES), F32),
            VMEM((2, tiles, 2, rows, LANES), F32),
            VMEM((2, tiles, 2, rows, LANES), F32),
            VMEM((tiles, 2, rows, LANES), F32),
            VMEM((2, tiles, 3 * cells, LANES), F32),
            VMEM((2, tiles, rows, LANES), F32),
            DMA((7,)),
        ],
        compiler_params=limit,
        name="render",
    )(
        edges,
        colour_coef,
        opacity_coef,
        light_dir,
        light_colour,
        field,
        low,
        high,
        top,
        bottom,
        top_corner,
        bottom_corner,
    )
    exchanged = lax.all_to_all(partial, "depth", 0, 0, tiled=True)
    own = pl.pallas_call(
        fold,
        out_shape=shape(13, tiles // slabs, rows, LANES),
        in_specs=in_vmem(1),
        out_specs=pl.BlockSpec(memory_space=VMEM),
        compiler_params=limit,
        name="fold",
    )(exchanged)
    from_below, from_above = [own], [own]
    for _ in range(slabs // 2):
        from_below.append(lax.ppermute(from_below[-1], "depth", ring("depth", 1)))
        from_above.append(lax.ppermute(from_above[-1], "depth", ring("depth", -1)))
    count = slabs // 2
    early = list(range(1 - count // 2, 1 + count // 2))
    late = [k for k in range(1 - count, 1 + count) if k not in early]
    image = []
    for offsets in (early, late):
        aliases = {1 + len(offsets): 0} if image else {}
        image = [
            pl.pallas_call(
                functools.partial(spread, slabs, offsets),
                out_shape=shape(13, tiles, rows, LANES),
                in_specs=in_smem(1) + in_vmem(len(offsets)) + anywhere(len(image)),
                out_specs=pl.BlockSpec(memory_space=pl.ANY),
                scratch_shapes=[DMA((len(offsets),))],
                input_output_aliases=aliases,
                compiler_params=limit,
                name="spread",
            )(
                slab[None],
                *[from_below[k] if k >= 0 else from_above[-k] for k in offsets],
                *image,
            )
        ]
    (image,) = image
    return image.transpose(0, 2, 1, 3).reshape(13, rows, width)


def solution(mesh):
    placed = (P("depth", "height", None), P(), P(), P(), P())
    return jax.shard_map(
        per_device, mesh=mesh, in_specs=placed, out_specs=P(None, "height", None), check_vma=False
    )
```

```python
import functools

import jax
import jax.numpy as jnp
from jax import lax
from jax.experimental import pallas as pl
from jax.experimental.pallas import tpu as pltpu
from jax.sharding import PartitionSpec as P

VMEM = pltpu.VMEM
DMA = pltpu.SemaphoreType.DMA
F32 = jnp.float32
LANES = 128
ROWS = 8
BAND = 8
OWN = 4


def inverse_of(q):
    return pltpu.reciprocal(q, approx=True)


def flux(d):
    return d * inverse_of(d * d + 1.0)


def pack(vol_ref, down_ref, up_ref, first_ref, last_ref, held, down, up, in_sem, edge_sem, out_sem):
    cells, tiles = vol_ref.shape[0], vol_ref.shape[1]
    groups = cells // 8
    loads = [
        pltpu.make_async_copy(vol_ref.at[pl.ds(8 * g, 8)], held.at[pl.ds(8 * g, 8)], in_sem.at[g])
        for g in range(groups)
    ]
    edges = [
        pltpu.make_async_copy(held.at[pl.ds(0, 3)], first_ref, edge_sem.at[0]),
        pltpu.make_async_copy(held.at[pl.ds(cells - 3, 3)], last_ref, edge_sem.at[1]),
    ]
    for copy in loads:
        copy.start()
    stores = []
    for g in range(groups):
        loads[g].wait()
        if g == 0:
            edges[0].start()
        if g == groups - 1:
            edges[1].start()
        for k in range(8):
            z = 8 * g + k
            for tile in range(tiles):
                up[tile, 3 * z : 3 * z + 3, :] = held[z, tile, 0:3, :]
                down[tile, 3 * z : 3 * z + 3, :] = held[z, tile, 5:8, :]
        part = pl.ds(24 * g, 24)
        for i, (ref, out_ref) in enumerate(((down, down_ref), (up, up_ref))):
            copy = pltpu.make_async_copy(
                ref.at[:, part, :], out_ref.at[:, part, :], out_sem.at[2 * g + i]
            )
            copy.start()
            stores.append(copy)
    for copy in stores + edges:
        copy.wait()


CORNERS = ((0, 1, 0), (0, 0, 0), (0, 1, 1), (1, 0, 0), (1, 1, 0), (1, 0, 1))


def pack_corners(low_ref, high_ref, down_ref, up_ref, near, sem):
    tiles = low_ref.shape[1]
    copies = [
        pltpu.make_async_copy(low_ref.at[pl.ds(1, 2)], near.at[0], sem.at[0]),
        pltpu.make_async_copy(high_ref.at[pl.ds(0, 2)], near.at[1], sem.at[1]),
    ]
    for copy in copies:
        copy.start()
    for copy in copies:
        copy.wait()
    zero = jnp.zeros((2, LANES), F32)
    for tile in range(tiles):
        for slot, (side, plane, depth) in enumerate(CORNERS):
            up_ref[tile, slot : slot + 1, :] = near[side, plane, tile, depth : depth + 1, :]
            down_ref[tile, slot : slot + 1, :] = near[side, plane, tile, 7 - depth : 8 - depth, :]
        up_ref[tile, 6:8, :] = zero
        down_ref[tile, 6:8, :] = zero


def beside(src, base, z, parity, nexts, befores):
    tiles = src.shape[1]
    lane = lax.broadcasted_iota(jnp.int32, (ROWS, LANES), 1)
    for part in range(2):
        rows = pl.ds(base + 8 * part, 8)
        now = src[z, 0, rows, :]
        lowered, raised = pltpu.roll(now, LANES - 1, 1), pltpu.roll(now, 1, 1)
        earlier = 0.0
        for tile in range(tiles):
            if tile + 1 < tiles:
                later = src[z, tile + 1, rows, :]
                later_lowered = pltpu.roll(later, LANES - 1, 1)
                later_raised = pltpu.roll(later, 1, 1)
            else:
                later_lowered, later_raised = 0.0, None
            nexts[parity, tile, part] = jnp.where(lane == LANES - 1, later_lowered, lowered)
            befores[parity, tile, part] = jnp.where(lane == 0, earlier, raised)
            earlier, lowered, raised = raised, later_lowered, later_raised


def diffuse_plane(src, base, z, parity, nexts, befores, held, dst, out, rims):
    tiles = src.shape[1]
    sub = lax.broadcasted_iota(jnp.int32, (ROWS, LANES), 0)
    for tile in range(tiles):
        below = None
        for part in range(2):
            first = base + 8 * part
            u = src[z, tile, pl.ds(first, 8), :]
            across = flux(nexts[parity, tile, part] - u) + flux(befores[parity, tile, part] - u)
            if first + 9 <= src.shape[2]:
                above = src[z, tile, pl.ds(first + 1, 8), :]
            else:
                above = pltpu.roll(u, ROWS - 1, 0)
            up = flux(above - u)
            turned = pltpu.roll(up, 1, 0)
            along = up - (turned if part == 0 else jnp.where(sub == 0, below, turned))
            below = turned
            ahead = flux(src[z + 1, tile, pl.ds(first, 8), :] - u)
            total = (across + along) + (ahead - held[tile, part])
            held[tile, part] = ahead
            dst[out, tile, pl.ds(8 * part, 8), :] = (u + 0.12 * total) * rims[part]


def width_slope(field, z, slope):
    tiles = field.shape[1]
    lane = lax.broadcasted_iota(jnp.int32, (ROWS, LANES), 1)
    rows = pl.ds(OWN, 8)
    now = field[z, 0, rows, :]
    lowered, raised = pltpu.roll(now, LANES - 1, 1), pltpu.roll(now, 1, 1)
    earlier = 0.0
    for tile in range(tiles):
        if tile + 1 < tiles:
            later = field[z, tile + 1, rows, :]
            later_lowered, later_raised = pltpu.roll(later, LANES - 1, 1), pltpu.roll(later, 1, 1)
        else:
            later_lowered, later_raised = 0.0, None
        slope[z, tile] = jnp.where(lane == LANES - 1, later_lowered, lowered) - jnp.where(
            lane == 0, earlier, raised
        )
        earlier, lowered, raised = raised, later_lowered, later_raised


def diffuse(src, base, dst, planes, nexts, befores, held, rims, slope=None):
    for tile in range(src.shape[1]):
        for part in range(2):
            rows = pl.ds(base + 8 * part, 8)
            held[tile, part] = flux(src[1, tile, rows, :] - src[0, tile, rows, :])
    beside(src, base, 1, 1, nexts, befores)

    def pair(g, carry):
        for k in range(2):
            z = 2 * g + k + 1
            beside(src, base, z + 1, k, nexts, befores)
            diffuse_plane(src, base, z, 1 - k, nexts, befores, held, dst, z - 1, rims)
            if slope is not None:
                width_slope(dst, jnp.maximum(z - 3, 0), slope)
        return carry

    lax.fori_loop(0, planes // 2, pair, 0)
    if slope is not None:
        width_slope(dst, planes - 2, slope)


SHIFTS = (4, 3, 5, 2, 6, 1, 7, 0)
FAR = 3


def render(
    edge_ref,
    tile_ref,
    colour_ref,
    opacity_ref,
    dir_ref,
    light_ref,
    vol_ref,
    low_ref,
    high_ref,
    top_ref,
    bottom_ref,
    top_corner_ref,
    bottom_corner_ref,
    *refs,
    alpha_top,
):
    out_refs, twice_ref, slope_ref = refs[:FAR], refs[FAR], refs[FAR + 1]
    (field, once, twice, slope, nexts, befores, held, rows_in, corners_in, images) = refs[FAR + 2 : -3]
    sem, later_sem, out_sem = refs[-3:]
    cells, tiles = vol_ref.shape[0], vol_ref.shape[1]
    own = pl.ds(BAND, 8)
    copies = [
        pltpu.make_async_copy(low_ref, field.at[pl.ds(0, 3), :, own, :], sem.at[0]),
        pltpu.make_async_copy(high_ref, field.at[pl.ds(cells + 3, 3), :, own, :], sem.at[1]),
        pltpu.make_async_copy(top_corner_ref, corners_in.at[0], sem.at[2]),
        pltpu.make_async_copy(bottom_corner_ref, corners_in.at[1], sem.at[3]),
        pltpu.make_async_copy(top_ref, rows_in.at[0], sem.at[4]),
        pltpu.make_async_copy(bottom_ref, rows_in.at[1], sem.at[5]),
        pltpu.make_async_copy(vol_ref, field.at[pl.ds(3, cells), :, own, :], sem.at[6]),
    ]
    for copy in copies:
        copy.start()

    sub = lax.broadcasted_iota(jnp.int32, (ROWS, LANES), 0)
    keep_low, keep_high = edge_ref[0], edge_ref[1]
    keep_top, keep_bottom = edge_ref[2], edge_ref[3]
    rims = (
        jnp.where(sub < OWN, jnp.full((ROWS, LANES), keep_top), 1.0),
        jnp.where(sub >= OWN, jnp.full((ROWS, LANES), keep_bottom), 1.0),
    )

    zero = jnp.zeros((ROWS, LANES), F32)
    for k in range(3):
        for tile in range(tiles):
            for plane in (k, cells + 3 + k):
                field[plane, tile, 0:8, :] = zero
                field[plane, tile, 16:24, :] = zero
    for copy in copies[:4]:
        copy.wait()
    for k in range(3):
        for tile in range(tiles):
            field[k, tile, own, :] = field[k, tile, own, :] * keep_low
            field[cells + 3 + k, tile, own, :] = field[cells + 3 + k, tile, own, :] * keep_high
    for tile in range(tiles):
        for slot, (side, plane, away) in enumerate(CORNERS):
            at = (cells + 3 if side else 1) + plane
            keep = keep_high if side else keep_low
            field[at, tile, 7 - away : 8 - away, :] = corners_in[0, tile, slot : slot + 1, :] * (
                keep * keep_top
            )
            field[at, tile, 16 + away : 17 + away, :] = corners_in[
                1, tile, slot : slot + 1, :
            ] * (keep * keep_bottom)
    copies[4].wait()
    copies[5].wait()

    def rims_in(g, carry):
        at = pl.multiple_of(24 * g, 24)
        for tile in range(tiles):
            for k in range(8):
                field[8 * g + k + 3, tile, 5:8, :] = (
                    rows_in[0, tile, pl.ds(at + 3 * k, 3), :] * keep_top
                )
                field[8 * g + k + 3, tile, 16:19, :] = (
                    rows_in[1, tile, pl.ds(at + 3 * k, 3), :] * keep_bottom
                )
        return carry

    lax.fori_loop(0, cells // 8, rims_in, 0)
    copies[6].wait()

    diffuse(field, OWN, once, cells + 4, nexts, befores, held, rims)
    for k in range(2):
        for tile in range(tiles):
            for rows in (slice(0, 8), slice(8, 16)):
                once[k, tile, rows, :] = once[k, tile, rows, :] * keep_low
                once[cells + 2 + k, tile, rows, :] = once[cells + 2 + k, tile, rows, :] * keep_high
    diffuse(once, 0, twice, cells + 2, nexts, befores, held, rims, slope)
    own = pl.ds(OWN, 8)
    for tile in range(tiles):
        twice[0, tile, own, :] = twice[0, tile, own, :] * keep_low
        twice[cells + 1, tile, own, :] = twice[cells + 1, tile, own, :] * keep_high

    each = tiles // len(SHIFTS)
    ahead = FAR * each
    later = []
    for k in range(tiles - ahead):
        tile = tile_ref[ahead + k]
        later += [
            pltpu.make_async_copy(twice.at[:, tile], twice_ref.at[k], later_sem.at[0, k]),
            pltpu.make_async_copy(slope.at[:, tile], slope_ref.at[k], later_sem.at[1, k]),
        ]
    for copy in later:
        copy.start()

    def smooth(k, z, row):
        return twice[z, tile_ref[k], pl.ds(row, 8), :]

    def across(k, z):
        return slope[z, tile_ref[k]]

    coefs = (colour_ref, opacity_ref, dir_ref, light_ref)
    shade(coefs, cells, ahead, smooth, across, images, alpha_top)
    send(images, out_refs, out_sem)
    for copy in later:
        copy.wait()


def render_rest(colour_ref, opacity_ref, dir_ref, light_ref, twice_ref, slope_ref, *refs, alpha_top):
    out_refs, (twice, slope, images, sem, out_sem) = refs[:-5], refs[-5:]
    count, cells = slope.shape[0], slope.shape[1] - 1

    def load(k):
        return [
            pltpu.make_async_copy(twice_ref.at[k], twice.at[k], sem.at[0, k]),
            pltpu.make_async_copy(slope_ref.at[k], slope.at[k], sem.at[1, k]),
        ]

    for k in range(count):
        for copy in load(k):
            copy.start()

    def ready(k):
        for copy in load(k):
            copy.wait()

    def smooth(k, z, row):
        return twice[k, z, pl.ds(row, 8), :]

    def across(k, z):
        return slope[k, z]

    coefs = (colour_ref, opacity_ref, dir_ref, light_ref)
    shade(coefs, cells, count, smooth, across, images, alpha_top, ready)
    send(images, out_refs, out_sem)


def send(images, out_refs, sem):
    copies = [
        pltpu.make_async_copy(images.at[k], ref, sem.at[k]) for k, ref in enumerate(out_refs)
    ]
    for copy in copies:
        copy.start()
    for copy in copies:
        copy.wait()


def shade(coefs, cells, count, smooth, across, images, alpha_top, ready=None):
    colour_ref, opacity_ref, dir_ref, light_ref = coefs
    each = images.shape[2]
    zero = jnp.zeros((ROWS, LANES), F32)
    colour = [[colour_ref[c, j] for j in range(4)] for c in range(3)]
    opac = [opacity_ref[j] for j in range(4)]
    light = [[0.5 * dir_ref[l, d] for d in range(3)] for l in range(4)]

    def poly(c, v):
        return ((c[3] * v + c[2]) * v + c[1]) * v + c[0]

    def column(k, carry):
        if ready is not None:
            ready(k)

        def cell(z, state):
            through, sums, base_sums = state
            v = smooth(k, z + 1, OWN)
            g_z = smooth(k, z + 2, OWN) - smooth(k, z, OWN)
            g_h = smooth(k, z + 1, OWN + 1) - smooth(k, z + 1, OWN - 1)
            g_w = across(k, z + 1)
            inverse = lax.rsqrt(0.25 * (g_z * g_z + g_h * g_h + g_w * g_w) + 1.0)
            p = poly(opac, v)
            s = p * p
            opacity = (alpha_top * s) * inverse_of(1.0 + s)
            weight = through * opacity
            through = through - weight
            half = 0.5 * weight
            shaded = [half + half * jnp.tanh(poly(colour[c], v)) for c in range(3)]
            base_sums = [base_sums[c] + shaded[c] for c in range(3)]
            tilted = [inverse * shaded[c] for c in range(3)]
            new = []
            for l in range(4):
                facing = jnp.abs(g_z * light[l][0] + g_h * light[l][1] + g_w * light[l][2])
                for c in range(3):
                    new.append(sums[3 * l + c] + facing * tilted[c])
            return through, new, base_sums

        state = (jnp.ones((ROWS, LANES), F32), [zero] * 12, [zero] * 3)

        def group(g, state):
            for i in range(8):
                state = cell(g * 8 + i, state)
            return state

        through, sums, base_sums = lax.fori_loop(0, cells // 8, group, state)
        for l in range(4):
            for c in range(3):
                images[k // each, 3 * l + c, k % each] = light_ref[l, c] * (
                    0.2 * base_sums[c] + sums[3 * l + c]
                )
        images[k // each, 12, k % each] = 1.0 - through
        return carry

    lax.fori_loop(0, count, column, 0)


def fold(place_ref, *refs):
    pieces, (out_ref, parts, sem) = refs[:-3], refs[-3:]
    slabs, channels = parts.shape[0], parts.shape[1]
    copies = []
    for i, ref in enumerate(pieces):
        slab = lax.rem(place_ref[0] - SHIFTS[i] + slabs, slabs)
        copies.append(pltpu.make_async_copy(ref, parts.at[slab], sem.at[i]))
    for copy in copies:
        copy.start()
    for copy in copies:
        copy.wait()
    for tile in range(parts.shape[2]):
        through = 1.0 - parts[0, 12, tile]
        total = [parts[0, ch, tile] for ch in range(channels)]
        for slab in range(1, slabs):
            total = [total[ch] + through * parts[slab, ch, tile] for ch in range(channels)]
            through = through * (1.0 - parts[slab, 12, tile])
        for ch in range(channels):
            out_ref[ch, tile] = total[ch]


def spread(count, offsets, place_ref, *refs):
    pieces, out_ref, sem = refs[: len(offsets)], refs[-2], refs[-1]
    tiles = out_ref.shape[1] // count
    copies = []
    for i, ref in enumerate(pieces):
        owner = lax.rem(place_ref[0] - offsets[i] + count, count)
        copies.append(
            pltpu.make_async_copy(ref, out_ref.at[:, pl.ds(owner * tiles, tiles)], sem.at[i])
        )
    for copy in copies:
        copy.start()
    for copy in copies:
        copy.wait()


def in_vmem(count):
    return [pl.BlockSpec(memory_space=VMEM)] * count


def in_smem(count):
    return [pl.BlockSpec(memory_space=pltpu.SMEM)] * count


def anywhere(count):
    return [pl.BlockSpec(memory_space=pl.ANY)] * count


def shape(*dims):
    return jax.ShapeDtypeStruct(dims, F32)


def ring(axis, by):
    count = lax.axis_size(axis)
    return [(i, (i + by) % count) for i in range(count)]


def per_device(volume, colour_coef, opacity_coef, light_dir, light_colour):
    slabs, bands = lax.axis_size("depth"), lax.axis_size("height")
    cells, rows, width = volume.shape
    tiles = width // LANES
    slab, band = lax.axis_index("depth"), lax.axis_index("height")
    limit = pltpu.CompilerParams(vmem_limit_bytes=63 << 20)
    field = volume.reshape(cells, rows, tiles, LANES).transpose(0, 2, 1, 3)

    down, up, first, last = pl.pallas_call(
        pack,
        out_shape=[shape(tiles, 3 * cells, LANES)] * 2 + [shape(3, tiles, rows, LANES)] * 2,
        in_specs=anywhere(1),
        out_specs=anywhere(4),
        scratch_shapes=[
            VMEM((cells, tiles, rows, LANES), F32),
            VMEM((tiles, 3 * cells, LANES), F32),
            VMEM((tiles, 3 * cells, LANES), F32),
            DMA((cells // 8,)),
            DMA((2,)),
            DMA((cells // 4,)),
        ],
        compiler_params=limit,
        name="pack",
    )(field)
    low = lax.ppermute(last, "depth", ring("depth", 1))
    high = lax.ppermute(first, "depth", ring("depth", -1))
    top = lax.ppermute(down, "height", ring("height", 1))
    bottom = lax.ppermute(up, "height", ring("height", -1))
    corner_down, corner_up = pl.pallas_call(
        pack_corners,
        out_shape=[shape(tiles, rows, LANES)] * 2,
        in_specs=anywhere(2),
        out_specs=in_vmem(2),
        scratch_shapes=[VMEM((2, 2, tiles, rows, LANES), F32), DMA((2,))],
        compiler_params=limit,
        cost_estimate=pl.CostEstimate(
            flops=400_000_000, bytes_accessed=80_000_000, transcendentals=0
        ),
        name="pack_corners",
    )(low, high)
    top_corner = lax.ppermute(corner_down, "height", ring("height", 1))
    bottom_corner = lax.ppermute(corner_up, "height", ring("height", -1))

    edges = jnp.stack([slab > 0, slab < slabs - 1, band > 0, band < bands - 1]).astype(F32)
    each = tiles // slabs
    rest = tiles - FAR * each
    alpha_top = 2.0 / (cells * slabs)
    piece = shape(13, each, rows, LANES)
    order = [(slab + by) % slabs * each + k for by in SHIFTS for k in range(each)]
    *pieces, twice, slope = pl.pallas_call(
        functools.partial(render, alpha_top=alpha_top),
        out_shape=[piece] * FAR
        + [shape(rest, cells + 2, 16, LANES), shape(rest, cells + 1, rows, LANES)],
        in_specs=in_smem(6) + anywhere(7),
        out_specs=anywhere(FAR + 2),
        scratch_shapes=[
            VMEM((cells + 6, tiles, 24, LANES), F32),
            VMEM((cells + 4, tiles, 16, LANES), F32),
            VMEM((cells + 2, tiles, 16, LANES), F32),
            VMEM((cells + 1, tiles, rows, LANES), F32),
            VMEM((2, tiles, 2, rows, LANES), F32),
            VMEM((2, tiles, 2, rows, LANES), F32),
            VMEM((tiles, 2, rows, LANES), F32),
            VMEM((2, tiles, 3 * cells, LANES), F32),
            VMEM((2, tiles, rows, LANES), F32),
            VMEM((FAR, 13, each, rows, LANES), F32),
            DMA((7,)),
            DMA((2, rest)),
            DMA((FAR,)),
        ],
        compiler_params=limit,
        name="render",
    )(
        edges,
        jnp.stack(order).astype(jnp.int32),
        colour_coef,
        opacity_coef,
        light_dir,
        light_colour,
        field,
        low,
        high,
        top,
        bottom,
        top_corner,
        bottom_corner,
    )
    pieces += pl.pallas_call(
        functools.partial(render_rest, alpha_top=alpha_top),
        out_shape=[piece] * (slabs - FAR),
        in_specs=in_smem(4) + anywhere(2),
        out_specs=anywhere(slabs - FAR),
        scratch_shapes=[
            VMEM((rest, cells + 2, 16, LANES), F32),
            VMEM((rest, cells + 1, rows, LANES), F32),
            VMEM((slabs - FAR, 13, each, rows, LANES), F32),
            DMA((2, rest)),
            DMA((slabs - FAR,)),
        ],
        compiler_params=limit,
        cost_estimate=pl.CostEstimate(
            flops=50_000_000, bytes_accessed=20_000_000, transcendentals=1_000_000
        ),
        name="render_rest",
    )(colour_coef, opacity_coef, light_dir, light_colour, twice, slope)
    arrived = [
        lax.ppermute(value, "depth", ring("depth", by)) if by else value
        for value, by in zip(pieces, SHIFTS)
    ]
    own = pl.pallas_call(
        fold,
        out_shape=piece,
        in_specs=in_smem(1) + anywhere(slabs),
        out_specs=pl.BlockSpec(memory_space=VMEM),
        scratch_shapes=[VMEM((slabs, 13, each, rows, LANES), F32), DMA((slabs,))],
        compiler_params=limit,
        name="fold",
    )(slab[None], *arrived)
    from_below, from_above = [own], [own]
    for _ in range(slabs // 2):
        from_below.append(lax.ppermute(from_below[-1], "depth", ring("depth", 1)))
        from_above.append(lax.ppermute(from_above[-1], "depth", ring("depth", -1)))
    count = slabs // 2
    early = list(range(1 - count // 2, 1 + count // 2))
    late = [k for k in range(1 - count, 1 + count) if k not in early]
    image = []
    for offsets in (early, late):
        aliases = {1 + len(offsets): 0} if image else {}
        image = [
            pl.pallas_call(
                functools.partial(spread, slabs, offsets),
                out_shape=shape(13, tiles, rows, LANES),
                in_specs=in_smem(1) + in_vmem(len(offsets)) + anywhere(len(image)),
                out_specs=pl.BlockSpec(memory_space=pl.ANY),
                scratch_shapes=[DMA((len(offsets),))],
                input_output_aliases=aliases,
                compiler_params=limit,
                name="spread",
            )(
                slab[None],
                *[from_below[k] if k >= 0 else from_above[-k] for k in offsets],
                *image,
            )
        ]
    (image,) = image
    return image.transpose(0, 2, 1, 3).reshape(13, rows, width)


def solution(mesh):
    placed = (P("depth", "height", None), P(), P(), P(), P())
    return jax.shard_map(
        per_device, mesh=mesh, in_specs=placed, out_specs=P(None, "height", None), check_vma=False
    )
```

```python
import functools

import jax
import jax.numpy as jnp
from jax import lax
from jax.experimental import pallas as pl
from jax.experimental.pallas import tpu as pltpu
from jax.sharding import PartitionSpec as P

VMEM = pltpu.VMEM
DMA = pltpu.SemaphoreType.DMA
F32 = jnp.float32
LANES = 128
ROWS = 8
BAND = 8
OWN = 4


def inverse_of(q):
    return pltpu.reciprocal(q, approx=True)


def flux(d):
    return d * inverse_of(d * d + 1.0)


def pack(vol_ref, down_ref, up_ref, first_ref, last_ref, held, down, up, in_sem, edge_sem, out_sem):
    cells, tiles = vol_ref.shape[0], vol_ref.shape[1]
    groups = cells // 8
    loads = [
        pltpu.make_async_copy(vol_ref.at[pl.ds(8 * g, 8)], held.at[pl.ds(8 * g, 8)], in_sem.at[g])
        for g in range(groups)
    ]
    edges = [
        pltpu.make_async_copy(held.at[pl.ds(0, 3)], first_ref, edge_sem.at[0]),
        pltpu.make_async_copy(held.at[pl.ds(cells - 3, 3)], last_ref, edge_sem.at[1]),
    ]
    for copy in loads:
        copy.start()
    stores = []
    for g in range(groups):
        loads[g].wait()
        if g == 0:
            edges[0].start()
        if g == groups - 1:
            edges[1].start()
        for k in range(8):
            z = 8 * g + k
            for tile in range(tiles):
                up[tile, 3 * z : 3 * z + 3, :] = held[z, tile, 0:3, :]
                down[tile, 3 * z : 3 * z + 3, :] = held[z, tile, 5:8, :]
        part = pl.ds(24 * g, 24)
        for i, (ref, out_ref) in enumerate(((down, down_ref), (up, up_ref))):
            copy = pltpu.make_async_copy(
                ref.at[:, part, :], out_ref.at[:, part, :], out_sem.at[2 * g + i]
            )
            copy.start()
            stores.append(copy)
    for copy in stores + edges:
        copy.wait()


CORNERS = ((0, 1, 0), (0, 0, 0), (0, 1, 1), (1, 0, 0), (1, 1, 0), (1, 0, 1))


def pack_corners(low_ref, high_ref, down_ref, up_ref, near, sem):
    tiles = low_ref.shape[1]
    copies = [
        pltpu.make_async_copy(low_ref.at[pl.ds(1, 2)], near.at[0], sem.at[0]),
        pltpu.make_async_copy(high_ref.at[pl.ds(0, 2)], near.at[1], sem.at[1]),
    ]
    for copy in copies:
        copy.start()
    for copy in copies:
        copy.wait()
    zero = jnp.zeros((2, LANES), F32)
    for tile in range(tiles):
        for slot, (side, plane, depth) in enumerate(CORNERS):
            up_ref[tile, slot : slot + 1, :] = near[side, plane, tile, depth : depth + 1, :]
            down_ref[tile, slot : slot + 1, :] = near[side, plane, tile, 7 - depth : 8 - depth, :]
        up_ref[tile, 6:8, :] = zero
        down_ref[tile, 6:8, :] = zero


def beside(src, base, z, parity, nexts, befores):
    tiles = src.shape[1]
    lane = lax.broadcasted_iota(jnp.int32, (ROWS, LANES), 1)
    for part in range(2):
        rows = pl.ds(base + 8 * part, 8)
        now = src[z, 0, rows, :]
        lowered, raised = pltpu.roll(now, LANES - 1, 1), pltpu.roll(now, 1, 1)
        earlier = 0.0
        for tile in range(tiles):
            if tile + 1 < tiles:
                later = src[z, tile + 1, rows, :]
                later_lowered = pltpu.roll(later, LANES - 1, 1)
                later_raised = pltpu.roll(later, 1, 1)
            else:
                later_lowered, later_raised = 0.0, None
            nexts[parity, tile, part] = jnp.where(lane == LANES - 1, later_lowered, lowered)
            befores[parity, tile, part] = jnp.where(lane == 0, earlier, raised)
            earlier, lowered, raised = raised, later_lowered, later_raised


def diffuse_plane(src, base, z, parity, nexts, befores, held, dst, out, rims):
    tiles = src.shape[1]
    sub = lax.broadcasted_iota(jnp.int32, (ROWS, LANES), 0)
    for tile in range(tiles):
        below = None
        for part in range(2):
            first = base + 8 * part
            u = src[z, tile, pl.ds(first, 8), :]
            across = flux(nexts[parity, tile, part] - u) + flux(befores[parity, tile, part] - u)
            if first + 9 <= src.shape[2]:
                above = src[z, tile, pl.ds(first + 1, 8), :]
            else:
                above = pltpu.roll(u, ROWS - 1, 0)
            up = flux(above - u)
            turned = pltpu.roll(up, 1, 0)
            along = up - (turned if part == 0 else jnp.where(sub == 0, below, turned))
            below = turned
            ahead = flux(src[z + 1, tile, pl.ds(first, 8), :] - u)
            total = (across + along) + (ahead - held[tile, part])
            held[tile, part] = ahead
            dst[out, tile, pl.ds(8 * part, 8), :] = (u + 0.12 * total) * rims[part]


def width_slope(field, z, slope):
    tiles = field.shape[1]
    lane = lax.broadcasted_iota(jnp.int32, (ROWS, LANES), 1)
    rows = pl.ds(OWN, 8)
    now = field[z, 0, rows, :]
    lowered, raised = pltpu.roll(now, LANES - 1, 1), pltpu.roll(now, 1, 1)
    earlier = 0.0
    for tile in range(tiles):
        if tile + 1 < tiles:
            later = field[z, tile + 1, rows, :]
            later_lowered, later_raised = pltpu.roll(later, LANES - 1, 1), pltpu.roll(later, 1, 1)
        else:
            later_lowered, later_raised = 0.0, None
        slope[z, tile] = jnp.where(lane == LANES - 1, later_lowered, lowered) - jnp.where(
            lane == 0, earlier, raised
        )
        earlier, lowered, raised = raised, later_lowered, later_raised


def diffuse(src, base, dst, planes, nexts, befores, held, rims, slope=None):
    for tile in range(src.shape[1]):
        for part in range(2):
            rows = pl.ds(base + 8 * part, 8)
            held[tile, part] = flux(src[1, tile, rows, :] - src[0, tile, rows, :])
    beside(src, base, 1, 1, nexts, befores)

    def pair(g, carry):
        for k in range(2):
            z = 2 * g + k + 1
            beside(src, base, z + 1, k, nexts, befores)
            diffuse_plane(src, base, z, 1 - k, nexts, befores, held, dst, z - 1, rims)
            if slope is not None:
                width_slope(dst, jnp.maximum(z - 3, 0), slope)
        return carry

    lax.fori_loop(0, planes // 2, pair, 0)
    if slope is not None:
        width_slope(dst, planes - 2, slope)


SHIFTS = (4, 3, 5, 2, 6, 1, 7, 0)
FAR = 3


def render(
    edge_ref,
    tile_ref,
    colour_ref,
    opacity_ref,
    dir_ref,
    light_ref,
    vol_ref,
    low_ref,
    high_ref,
    top_ref,
    bottom_ref,
    top_corner_ref,
    bottom_corner_ref,
    *refs,
    alpha_top,
):
    out_refs, twice_ref, slope_ref = refs[:FAR], refs[FAR], refs[FAR + 1]
    (field, once, twice, slope, nexts, befores, held, rows_in, corners_in, images) = refs[FAR + 2 : -3]
    sem, later_sem, out_sem = refs[-3:]
    cells, tiles = vol_ref.shape[0], vol_ref.shape[1]
    own = pl.ds(BAND, 8)
    copies = [
        pltpu.make_async_copy(low_ref, field.at[pl.ds(0, 3), :, own, :], sem.at[0]),
        pltpu.make_async_copy(high_ref, field.at[pl.ds(cells + 3, 3), :, own, :], sem.at[1]),
        pltpu.make_async_copy(top_corner_ref, corners_in.at[0], sem.at[2]),
        pltpu.make_async_copy(bottom_corner_ref, corners_in.at[1], sem.at[3]),
        pltpu.make_async_copy(top_ref, rows_in.at[0], sem.at[4]),
        pltpu.make_async_copy(bottom_ref, rows_in.at[1], sem.at[5]),
        pltpu.make_async_copy(vol_ref, field.at[pl.ds(3, cells), :, own, :], sem.at[6]),
    ]
    for copy in copies:
        copy.start()

    sub = lax.broadcasted_iota(jnp.int32, (ROWS, LANES), 0)
    keep_low, keep_high = edge_ref[0], edge_ref[1]
    keep_top, keep_bottom = edge_ref[2], edge_ref[3]
    rims = (
        jnp.where(sub < OWN, jnp.full((ROWS, LANES), keep_top), 1.0),
        jnp.where(sub >= OWN, jnp.full((ROWS, LANES), keep_bottom), 1.0),
    )

    zero = jnp.zeros((ROWS, LANES), F32)
    for k in range(3):
        for tile in range(tiles):
            for plane in (k, cells + 3 + k):
                field[plane, tile, 0:8, :] = zero
                field[plane, tile, 16:24, :] = zero
    for copy in copies[:4]:
        copy.wait()
    for k in range(3):
        for tile in range(tiles):
            field[k, tile, own, :] = field[k, tile, own, :] * keep_low
            field[cells + 3 + k, tile, own, :] = field[cells + 3 + k, tile, own, :] * keep_high
    for tile in range(tiles):
        for slot, (side, plane, away) in enumerate(CORNERS):
            at = (cells + 3 if side else 1) + plane
            keep = keep_high if side else keep_low
            field[at, tile, 7 - away : 8 - away, :] = corners_in[0, tile, slot : slot + 1, :] * (
                keep * keep_top
            )
            field[at, tile, 16 + away : 17 + away, :] = corners_in[
                1, tile, slot : slot + 1, :
            ] * (keep * keep_bottom)
    copies[4].wait()
    copies[5].wait()

    def rims_in(g, carry):
        at = pl.multiple_of(24 * g, 24)
        for tile in range(tiles):
            for k in range(8):
                field[8 * g + k + 3, tile, 5:8, :] = (
                    rows_in[0, tile, pl.ds(at + 3 * k, 3), :] * keep_top
                )
                field[8 * g + k + 3, tile, 16:19, :] = (
                    rows_in[1, tile, pl.ds(at + 3 * k, 3), :] * keep_bottom
                )
        return carry

    lax.fori_loop(0, cells // 8, rims_in, 0)
    copies[6].wait()

    diffuse(field, OWN, once, cells + 4, nexts, befores, held, rims)
    for k in range(2):
        for tile in range(tiles):
            for rows in (slice(0, 8), slice(8, 16)):
                once[k, tile, rows, :] = once[k, tile, rows, :] * keep_low
                once[cells + 2 + k, tile, rows, :] = once[cells + 2 + k, tile, rows, :] * keep_high
    diffuse(once, 0, twice, cells + 2, nexts, befores, held, rims, slope)
    own = pl.ds(OWN, 8)
    for tile in range(tiles):
        twice[0, tile, own, :] = twice[0, tile, own, :] * keep_low
        twice[cells + 1, tile, own, :] = twice[cells + 1, tile, own, :] * keep_high

    each = tiles // len(SHIFTS)
    ahead = FAR * each
    later = []
    for k in range(tiles - ahead):
        tile = tile_ref[ahead + k]
        later += [
            pltpu.make_async_copy(twice.at[:, tile], twice_ref.at[k], later_sem.at[0, k]),
            pltpu.make_async_copy(slope.at[:, tile], slope_ref.at[k], later_sem.at[1, k]),
        ]
    for copy in later:
        copy.start()

    def smooth(k, z, row):
        return twice[z, tile_ref[k], pl.ds(row, 8), :]

    def across(k, z):
        return slope[z, tile_ref[k]]

    coefs = (colour_ref, opacity_ref, dir_ref, light_ref)
    shade(coefs, cells, ahead, smooth, across, images, alpha_top)
    send(images, out_refs, out_sem)
    for copy in later:
        copy.wait()


def render_rest(colour_ref, opacity_ref, dir_ref, light_ref, twice_ref, slope_ref, *refs, alpha_top):
    out_refs, (twice, slope, images, sem, out_sem) = refs[:-5], refs[-5:]
    count, cells = slope.shape[0], slope.shape[1] - 1

    def load(k):
        return [
            pltpu.make_async_copy(twice_ref.at[k], twice.at[k], sem.at[0, k]),
            pltpu.make_async_copy(slope_ref.at[k], slope.at[k], sem.at[1, k]),
        ]

    for k in range(count):
        for copy in load(k):
            copy.start()

    def ready(k):
        for copy in load(k):
            copy.wait()

    def smooth(k, z, row):
        return twice[k, z, pl.ds(row, 8), :]

    def across(k, z):
        return slope[k, z]

    coefs = (colour_ref, opacity_ref, dir_ref, light_ref)
    shade(coefs, cells, count, smooth, across, images, alpha_top, ready)
    send(images, out_refs, out_sem)


def send(images, out_refs, sem):
    copies = [
        pltpu.make_async_copy(images.at[k], ref, sem.at[k]) for k, ref in enumerate(out_refs)
    ]
    for copy in copies:
        copy.start()
    for copy in copies:
        copy.wait()


def shade(coefs, cells, count, smooth, across, images, alpha_top, ready=None):
    colour_ref, opacity_ref, dir_ref, light_ref = coefs
    each = images.shape[2]
    zero = jnp.zeros((ROWS, LANES), F32)
    colour = [[colour_ref[c, j] for j in range(4)] for c in range(3)]
    opac = [opacity_ref[j] for j in range(4)]
    light = [[0.5 * dir_ref[l, d] for d in range(3)] for l in range(4)]

    def poly(c, v):
        return ((c[3] * v + c[2]) * v + c[1]) * v + c[0]

    def column(k, carry):
        if ready is not None:
            ready(k)

        def cell(z, state):
            through, sums, base_sums = state
            v = smooth(k, z + 1, OWN)
            g_z = smooth(k, z + 2, OWN) - smooth(k, z, OWN)
            g_h = smooth(k, z + 1, OWN + 1) - smooth(k, z + 1, OWN - 1)
            g_w = across(k, z + 1)
            inverse = lax.rsqrt(0.25 * (g_z * g_z + g_h * g_h + g_w * g_w) + 1.0)
            p = poly(opac, v)
            s = p * p
            opacity = (alpha_top * s) * inverse_of(1.0 + s)
            weight = through * opacity
            through = through - weight
            half = 0.5 * weight
            shaded = [half + half * jnp.tanh(poly(colour[c], v)) for c in range(3)]
            base_sums = [base_sums[c] + shaded[c] for c in range(3)]
            tilted = [inverse * shaded[c] for c in range(3)]
            new = []
            for l in range(4):
                facing = jnp.abs(g_z * light[l][0] + g_h * light[l][1] + g_w * light[l][2])
                for c in range(3):
                    new.append(sums[3 * l + c] + facing * tilted[c])
            return through, new, base_sums

        state = (jnp.ones((ROWS, LANES), F32), [zero] * 12, [zero] * 3)

        def group(g, state):
            for i in range(8):
                state = cell(g * 8 + i, state)
            return state

        through, sums, base_sums = lax.fori_loop(0, cells // 8, group, state)
        for l in range(4):
            for c in range(3):
                images[k // each, 3 * l + c, k % each] = light_ref[l, c] * (
                    0.2 * base_sums[c] + sums[3 * l + c]
                )
        images[k // each, 12, k % each] = 1.0 - through
        return carry

    lax.fori_loop(0, count, column, 0)


def fold(place_ref, *refs):
    pieces, (out_ref, parts, sem) = refs[:-3], refs[-3:]
    slabs, channels = parts.shape[0], parts.shape[1]
    copies = []
    for i, ref in enumerate(pieces):
        slab = lax.rem(place_ref[0] - SHIFTS[i] + slabs, slabs)
        copies.append(pltpu.make_async_copy(ref, parts.at[slab], sem.at[i]))
    for copy in copies:
        copy.start()
    for copy in copies:
        copy.wait()
    for tile in range(parts.shape[2]):
        through = 1.0 - parts[0, 12, tile]
        total = [parts[0, ch, tile] for ch in range(channels)]
        for slab in range(1, slabs):
            total = [total[ch] + through * parts[slab, ch, tile] for ch in range(channels)]
            through = through * (1.0 - parts[slab, 12, tile])
        for ch in range(channels):
            out_ref[ch, tile] = total[ch]


def spread(count, offsets, place_ref, *refs):
    pieces, out_ref, sem = refs[: len(offsets)], refs[-2], refs[-1]
    tiles = out_ref.shape[1] // count
    copies = []
    for i, ref in enumerate(pieces):
        owner = lax.rem(place_ref[0] - offsets[i] + count, count)
        copies.append(
            pltpu.make_async_copy(ref, out_ref.at[:, pl.ds(owner * tiles, tiles)], sem.at[i])
        )
    for copy in copies:
        copy.start()
    for copy in copies:
        copy.wait()


def in_vmem(count):
    return [pl.BlockSpec(memory_space=VMEM)] * count


def in_smem(count):
    return [pl.BlockSpec(memory_space=pltpu.SMEM)] * count


def anywhere(count):
    return [pl.BlockSpec(memory_space=pl.ANY)] * count


def shape(*dims):
    return jax.ShapeDtypeStruct(dims, F32)


def ring(axis, by):
    count = lax.axis_size(axis)
    return [(i, (i + by) % count) for i in range(count)]


def per_device(volume, colour_coef, opacity_coef, light_dir, light_colour):
    slabs, bands = lax.axis_size("depth"), lax.axis_size("height")
    cells, rows, width = volume.shape
    tiles = width // LANES
    slab, band = lax.axis_index("depth"), lax.axis_index("height")
    limit = pltpu.CompilerParams(vmem_limit_bytes=63 << 20)
    field = volume.reshape(cells, rows, tiles, LANES).transpose(0, 2, 1, 3)

    down, up, first, last = pl.pallas_call(
        pack,
        out_shape=[shape(tiles, 3 * cells, LANES)] * 2 + [shape(3, tiles, rows, LANES)] * 2,
        in_specs=anywhere(1),
        out_specs=anywhere(4),
        scratch_shapes=[
            VMEM((cells, tiles, rows, LANES), F32),
            VMEM((tiles, 3 * cells, LANES), F32),
            VMEM((tiles, 3 * cells, LANES), F32),
            DMA((cells // 8,)),
            DMA((2,)),
            DMA((cells // 4,)),
        ],
        compiler_params=limit,
        name="pack",
    )(field)
    low = lax.ppermute(last, "depth", ring("depth", 1))
    high = lax.ppermute(first, "depth", ring("depth", -1))
    top = lax.ppermute(down, "height", ring("height", 1))
    bottom = lax.ppermute(up, "height", ring("height", -1))
    corner_down, corner_up = pl.pallas_call(
        pack_corners,
        out_shape=[shape(tiles, rows, LANES)] * 2,
        in_specs=anywhere(2),
        out_specs=in_vmem(2),
        scratch_shapes=[VMEM((2, 2, tiles, rows, LANES), F32), DMA((2,))],
        compiler_params=limit,
        cost_estimate=pl.CostEstimate(
            flops=400_000_000, bytes_accessed=80_000_000, transcendentals=0
        ),
        name="pack_corners",
    )(low, high)
    top_corner = lax.ppermute(corner_down, "height", ring("height", 1))
    bottom_corner = lax.ppermute(corner_up, "height", ring("height", -1))

    edges = jnp.stack([slab > 0, slab < slabs - 1, band > 0, band < bands - 1]).astype(F32)
    each = tiles // slabs
    rest = tiles - FAR * each
    alpha_top = 2.0 / (cells * slabs)
    piece = shape(13, each, rows, LANES)
    order = [(slab + by) % slabs * each + k for by in SHIFTS for k in range(each)]
    *pieces, twice, slope = pl.pallas_call(
        functools.partial(render, alpha_top=alpha_top),
        out_shape=[piece] * FAR
        + [shape(rest, cells + 2, 16, LANES), shape(rest, cells + 1, rows, LANES)],
        in_specs=in_smem(6) + anywhere(7),
        out_specs=anywhere(FAR + 2),
        scratch_shapes=[
            VMEM((cells + 6, tiles, 24, LANES), F32),
            VMEM((cells + 4, tiles, 16, LANES), F32),
            VMEM((cells + 2, tiles, 16, LANES), F32),
            VMEM((cells + 1, tiles, rows, LANES), F32),
            VMEM((2, tiles, 2, rows, LANES), F32),
            VMEM((2, tiles, 2, rows, LANES), F32),
            VMEM((tiles, 2, rows, LANES), F32),
            VMEM((2, tiles, 3 * cells, LANES), F32),
            VMEM((2, tiles, rows, LANES), F32),
            VMEM((FAR, 13, each, rows, LANES), F32),
            DMA((7,)),
            DMA((2, rest)),
            DMA((FAR,)),
        ],
        compiler_params=limit,
        name="render",
    )(
        edges,
        jnp.stack(order).astype(jnp.int32),
        colour_coef,
        opacity_coef,
        light_dir,
        light_colour,
        field,
        low,
        high,
        top,
        bottom,
        top_corner,
        bottom_corner,
    )
    pieces += pl.pallas_call(
        functools.partial(render_rest, alpha_top=alpha_top),
        out_shape=[piece] * (slabs - FAR),
        in_specs=in_smem(4) + anywhere(2),
        out_specs=anywhere(slabs - FAR),
        scratch_shapes=[
            VMEM((rest, cells + 2, 16, LANES), F32),
            VMEM((rest, cells + 1, rows, LANES), F32),
            VMEM((slabs - FAR, 13, each, rows, LANES), F32),
            DMA((2, rest)),
            DMA((slabs - FAR,)),
        ],
        compiler_params=limit,
        cost_estimate=pl.CostEstimate(
            flops=50_000_000, bytes_accessed=20_000_000, transcendentals=1_000_000
        ),
        name="render_rest",
    )(colour_coef, opacity_coef, light_dir, light_colour, twice, slope)
    arrived = [
        lax.ppermute(value, "depth", ring("depth", by)) if by else value
        for value, by in zip(pieces, SHIFTS)
    ]
    own = pl.pallas_call(
        fold,
        out_shape=piece,
        in_specs=in_smem(1) + anywhere(slabs),
        out_specs=pl.BlockSpec(memory_space=VMEM),
        scratch_shapes=[VMEM((slabs, 13, each, rows, LANES), F32), DMA((slabs,))],
        compiler_params=limit,
        name="fold",
    )(slab[None], *arrived)
    known = {0: own}
    for by in (1, -1, 2, -2):
        known[by] = lax.ppermute(own, "depth", ring("depth", by))
    early = list(known)
    for held, by in ((2, 1), (-2, -1), (2, 2)):
        known[held + by] = lax.ppermute(known[held], "depth", ring("depth", by))
    late = [by for by in known if by not in early]
    image = []
    for offsets in (early, late):
        aliases = {1 + len(offsets): 0} if image else {}
        image = [
            pl.pallas_call(
                functools.partial(spread, slabs, offsets),
                out_shape=shape(13, tiles, rows, LANES),
                in_specs=in_smem(1) + in_vmem(len(offsets)) + anywhere(len(image)),
                out_specs=pl.BlockSpec(memory_space=pl.ANY),
                scratch_shapes=[DMA((len(offsets),))],
                input_output_aliases=aliases,
                compiler_params=limit,
                name="spread",
            )(
                slab[None],
                *[known[by] for by in offsets],
                *image,
            )
        ]
    (image,) = image
    return image.transpose(0, 2, 1, 3).reshape(13, rows, width)


def solution(mesh):
    placed = (P("depth", "height", None), P(), P(), P(), P())
    return jax.shard_map(
        per_device, mesh=mesh, in_specs=placed, out_specs=P(None, "height", None), check_vma=False
    )
```

```python
import functools

import jax
import jax.numpy as jnp
from jax import lax
from jax.experimental import pallas as pl
from jax.experimental.pallas import tpu as pltpu
from jax.sharding import PartitionSpec as P

VMEM = pltpu.VMEM
DMA = pltpu.SemaphoreType.DMA
F32 = jnp.float32
LANES = 128
ROWS = 8
BAND = 8
OWN = 4


def inverse_of(q):
    return pltpu.reciprocal(q, approx=True)


def flux(d):
    return d * inverse_of(d * d + 1.0)


def pack(vol_ref, down_ref, up_ref, first_ref, last_ref, held, down, up, in_sem, edge_sem, out_sem):
    cells, tiles = vol_ref.shape[0], vol_ref.shape[1]
    groups = cells // 8
    loads = [
        pltpu.make_async_copy(vol_ref.at[pl.ds(8 * g, 8)], held.at[pl.ds(8 * g, 8)], in_sem.at[g])
        for g in range(groups)
    ]
    edges = [
        pltpu.make_async_copy(held.at[pl.ds(0, 3)], first_ref, edge_sem.at[0]),
        pltpu.make_async_copy(held.at[pl.ds(cells - 3, 3)], last_ref, edge_sem.at[1]),
    ]
    for copy in loads:
        copy.start()
    stores = []
    for g in range(groups):
        loads[g].wait()
        if g == 0:
            edges[0].start()
        if g == groups - 1:
            edges[1].start()
        for k in range(8):
            z = 8 * g + k
            for tile in range(tiles):
                up[tile, 3 * z : 3 * z + 3, :] = held[z, tile, 0:3, :]
                down[tile, 3 * z : 3 * z + 3, :] = held[z, tile, 5:8, :]
        part = pl.ds(24 * g, 24)
        for i, (ref, out_ref) in enumerate(((down, down_ref), (up, up_ref))):
            copy = pltpu.make_async_copy(
                ref.at[:, part, :], out_ref.at[:, part, :], out_sem.at[2 * g + i]
            )
            copy.start()
            stores.append(copy)
    for copy in stores + edges:
        copy.wait()


CORNERS = ((0, 1, 0), (0, 0, 0), (0, 1, 1), (1, 0, 0), (1, 1, 0), (1, 0, 1))


def pack_corners(low_ref, high_ref, down_ref, up_ref, near, sem):
    tiles = low_ref.shape[1]
    copies = [
        pltpu.make_async_copy(low_ref.at[pl.ds(1, 2)], near.at[0], sem.at[0]),
        pltpu.make_async_copy(high_ref.at[pl.ds(0, 2)], near.at[1], sem.at[1]),
    ]
    for copy in copies:
        copy.start()
    for copy in copies:
        copy.wait()
    zero = jnp.zeros((2, LANES), F32)
    for tile in range(tiles):
        for slot, (side, plane, depth) in enumerate(CORNERS):
            up_ref[tile, slot : slot + 1, :] = near[side, plane, tile, depth : depth + 1, :]
            down_ref[tile, slot : slot + 1, :] = near[side, plane, tile, 7 - depth : 8 - depth, :]
        up_ref[tile, 6:8, :] = zero
        down_ref[tile, 6:8, :] = zero


def beside(src, base, z, parity, nexts):
    tiles = src.shape[1]
    lane = lax.broadcasted_iota(jnp.int32, (ROWS, LANES), 1)
    for part in range(2):
        rows = pl.ds(base + 8 * part, 8)
        turned = [pltpu.roll(src[z, tile, rows, :], LANES - 1, 1) for tile in range(tiles)]
        for tile in range(tiles):
            later = turned[tile + 1] if tile + 1 < tiles else 0.0
            nexts[parity, tile, part] = jnp.where(lane == LANES - 1, later, turned[tile])


def width_flux(src, base, z, parity, nexts, nets):
    tiles = src.shape[1]
    lane = lax.broadcasted_iota(jnp.int32, (ROWS, LANES), 1)
    for part in range(2):
        rows = pl.ds(base + 8 * part, 8)
        earlier = None
        for tile in range(tiles):
            u = src[z, tile, rows, :]
            across = flux(nexts[parity, tile, part] - u)
            turned = pltpu.roll(across, 1, 1)
            behind = flux(u) if earlier is None else earlier
            nets[parity, tile, part] = across - jnp.where(lane == 0, behind, turned)
            earlier = turned


def diffuse_plane(src, base, z, parity, nets, held, dst, out, rims):
    tiles = src.shape[1]
    sub = lax.broadcasted_iota(jnp.int32, (ROWS, LANES), 0)
    for tile in range(tiles):
        below = None
        for part in range(2):
            first = base + 8 * part
            u = src[z, tile, pl.ds(first, 8), :]
            if first + 9 <= src.shape[2]:
                above = src[z, tile, pl.ds(first + 1, 8), :]
            else:
                above = pltpu.roll(u, ROWS - 1, 0)
            up = flux(above - u)
            turned = pltpu.roll(up, 1, 0)
            along = up - (turned if part == 0 else jnp.where(sub == 0, below, turned))
            below = turned
            ahead = flux(src[z + 1, tile, pl.ds(first, 8), :] - u)
            total = (nets[parity, tile, part] + along) + (ahead - held[tile, part])
            held[tile, part] = ahead
            dst[out, tile, pl.ds(8 * part, 8), :] = (u + 0.12 * total) * rims[part]


def width_slope(field, z, slope):
    tiles = field.shape[1]
    lane = lax.broadcasted_iota(jnp.int32, (ROWS, LANES), 1)
    rows = pl.ds(OWN, 8)
    now = field[z, 0, rows, :]
    lowered, raised = pltpu.roll(now, LANES - 1, 1), pltpu.roll(now, 1, 1)
    earlier = 0.0
    for tile in range(tiles):
        if tile + 1 < tiles:
            later = field[z, tile + 1, rows, :]
            later_lowered, later_raised = pltpu.roll(later, LANES - 1, 1), pltpu.roll(later, 1, 1)
        else:
            later_lowered, later_raised = 0.0, None
        slope[z, tile] = jnp.where(lane == LANES - 1, later_lowered, lowered) - jnp.where(
            lane == 0, earlier, raised
        )
        earlier, lowered, raised = raised, later_lowered, later_raised


def diffuse(src, base, dst, planes, nexts, nets, held, rims, slope=None):
    for tile in range(src.shape[1]):
        for part in range(2):
            rows = pl.ds(base + 8 * part, 8)
            held[tile, part] = flux(src[1, tile, rows, :] - src[0, tile, rows, :])
    beside(src, base, 1, 1, nexts)
    width_flux(src, base, 1, 1, nexts, nets)
    beside(src, base, 2, 0, nexts)

    def pair(g, carry):
        for k in range(2):
            z = 2 * g + k + 1
            beside(src, base, jnp.minimum(z + 2, planes + 1), 1 - k, nexts)
            width_flux(src, base, z + 1, k, nexts, nets)
            diffuse_plane(src, base, z, 1 - k, nets, held, dst, z - 1, rims)
            if slope is not None:
                width_slope(dst, jnp.maximum(z - 3, 0), slope)
        return carry

    lax.fori_loop(0, planes // 2, pair, 0)
    if slope is not None:
        width_slope(dst, planes - 2, slope)


SHIFTS = (4, 3, 5, 2, 6, 1, 7, 0)
FAR = 3


def render(
    edge_ref,
    tile_ref,
    colour_ref,
    opacity_ref,
    dir_ref,
    light_ref,
    vol_ref,
    low_ref,
    high_ref,
    top_ref,
    bottom_ref,
    top_corner_ref,
    bottom_corner_ref,
    *refs,
    alpha_top,
):
    out_refs, twice_ref, slope_ref = refs[:FAR], refs[FAR], refs[FAR + 1]
    (field, once, twice, slope, nexts, nets, held, rows_in, corners_in, images) = refs[FAR + 2 : -3]
    sem, later_sem, out_sem = refs[-3:]
    cells, tiles = vol_ref.shape[0], vol_ref.shape[1]
    own = pl.ds(BAND, 8)
    copies = [
        pltpu.make_async_copy(low_ref, field.at[pl.ds(0, 3), :, own, :], sem.at[0]),
        pltpu.make_async_copy(high_ref, field.at[pl.ds(cells + 3, 3), :, own, :], sem.at[1]),
        pltpu.make_async_copy(top_corner_ref, corners_in.at[0], sem.at[2]),
        pltpu.make_async_copy(bottom_corner_ref, corners_in.at[1], sem.at[3]),
        pltpu.make_async_copy(top_ref, rows_in.at[0], sem.at[4]),
        pltpu.make_async_copy(bottom_ref, rows_in.at[1], sem.at[5]),
        pltpu.make_async_copy(vol_ref, field.at[pl.ds(3, cells), :, own, :], sem.at[6]),
    ]
    for copy in copies:
        copy.start()

    sub = lax.broadcasted_iota(jnp.int32, (ROWS, LANES), 0)
    keep_low, keep_high = edge_ref[0], edge_ref[1]
    keep_top, keep_bottom = edge_ref[2], edge_ref[3]
    rims = (
        jnp.where(sub < OWN, jnp.full((ROWS, LANES), keep_top), 1.0),
        jnp.where(sub >= OWN, jnp.full((ROWS, LANES), keep_bottom), 1.0),
    )

    zero = jnp.zeros((ROWS, LANES), F32)
    for k in range(3):
        for tile in range(tiles):
            for plane in (k, cells + 3 + k):
                field[plane, tile, 0:8, :] = zero
                field[plane, tile, 16:24, :] = zero
    for copy in copies[:4]:
        copy.wait()
    for k in range(3):
        for tile in range(tiles):
            field[k, tile, own, :] = field[k, tile, own, :] * keep_low
            field[cells + 3 + k, tile, own, :] = field[cells + 3 + k, tile, own, :] * keep_high
    for tile in range(tiles):
        for slot, (side, plane, away) in enumerate(CORNERS):
            at = (cells + 3 if side else 1) + plane
            keep = keep_high if side else keep_low
            field[at, tile, 7 - away : 8 - away, :] = corners_in[0, tile, slot : slot + 1, :] * (
                keep * keep_top
            )
            field[at, tile, 16 + away : 17 + away, :] = corners_in[
                1, tile, slot : slot + 1, :
            ] * (keep * keep_bottom)
    copies[4].wait()
    copies[5].wait()

    def rims_in(g, carry):
        at = pl.multiple_of(24 * g, 24)
        for tile in range(tiles):
            for k in range(8):
                field[8 * g + k + 3, tile, 5:8, :] = (
                    rows_in[0, tile, pl.ds(at + 3 * k, 3), :] * keep_top
                )
                field[8 * g + k + 3, tile, 16:19, :] = (
                    rows_in[1, tile, pl.ds(at + 3 * k, 3), :] * keep_bottom
                )
        return carry

    lax.fori_loop(0, cells // 8, rims_in, 0)
    copies[6].wait()

    diffuse(field, OWN, once, cells + 4, nexts, nets, held, rims)
    for k in range(2):
        for tile in range(tiles):
            for rows in (slice(0, 8), slice(8, 16)):
                once[k, tile, rows, :] = once[k, tile, rows, :] * keep_low
                once[cells + 2 + k, tile, rows, :] = once[cells + 2 + k, tile, rows, :] * keep_high
    diffuse(once, 0, twice, cells + 2, nexts, nets, held, rims, slope)
    own = pl.ds(OWN, 8)
    for tile in range(tiles):
        twice[0, tile, own, :] = twice[0, tile, own, :] * keep_low
        twice[cells + 1, tile, own, :] = twice[cells + 1, tile, own, :] * keep_high

    each = tiles // len(SHIFTS)
    ahead = FAR * each
    later = []
    for k in range(tiles - ahead):
        tile = tile_ref[ahead + k]
        later += [
            pltpu.make_async_copy(twice.at[:, tile], twice_ref.at[k], later_sem.at[0, k]),
            pltpu.make_async_copy(slope.at[:, tile], slope_ref.at[k], later_sem.at[1, k]),
        ]
    for copy in later:
        copy.start()

    def smooth(k, z, row):
        return twice[z, tile_ref[k], pl.ds(row, 8), :]

    def across(k, z):
        return slope[z, tile_ref[k]]

    coefs = (colour_ref, opacity_ref, dir_ref, light_ref)
    shade(coefs, cells, ahead, smooth, across, images, alpha_top)
    send(images, out_refs, out_sem)
    for copy in later:
        copy.wait()


def render_rest(colour_ref, opacity_ref, dir_ref, light_ref, twice_ref, slope_ref, *refs, alpha_top):
    out_refs, (twice, slope, images, sem, out_sem) = refs[:-5], refs[-5:]
    count, cells = slope.shape[0], slope.shape[1] - 1

    def load(k):
        return [
            pltpu.make_async_copy(twice_ref.at[k], twice.at[k], sem.at[0, k]),
            pltpu.make_async_copy(slope_ref.at[k], slope.at[k], sem.at[1, k]),
        ]

    for k in range(count):
        for copy in load(k):
            copy.start()

    def ready(k):
        for copy in load(k):
            copy.wait()

    def smooth(k, z, row):
        return twice[k, z, pl.ds(row, 8), :]

    def across(k, z):
        return slope[k, z]

    coefs = (colour_ref, opacity_ref, dir_ref, light_ref)
    shade(coefs, cells, count, smooth, across, images, alpha_top, ready)
    send(images, out_refs, out_sem)


def send(images, out_refs, sem):
    copies = [
        pltpu.make_async_copy(images.at[k], ref, sem.at[k]) for k, ref in enumerate(out_refs)
    ]
    for copy in copies:
        copy.start()
    for copy in copies:
        copy.wait()


def shade(coefs, cells, count, smooth, across, images, alpha_top, ready=None):
    colour_ref, opacity_ref, dir_ref, light_ref = coefs
    each = images.shape[2]
    zero = jnp.zeros((ROWS, LANES), F32)
    colour = [[colour_ref[c, j] for j in range(4)] for c in range(3)]
    opac = [opacity_ref[j] for j in range(4)]
    light = [[0.5 * dir_ref[l, d] for d in range(3)] for l in range(4)]

    def poly(c, v):
        return ((c[3] * v + c[2]) * v + c[1]) * v + c[0]

    def column(k, carry):
        if ready is not None:
            ready(k)

        def cell(z, state):
            through, sums, base_sums = state
            v = smooth(k, z + 1, OWN)
            g_z = smooth(k, z + 2, OWN) - smooth(k, z, OWN)
            g_h = smooth(k, z + 1, OWN + 1) - smooth(k, z + 1, OWN - 1)
            g_w = across(k, z + 1)
            inverse = lax.rsqrt(0.25 * (g_z * g_z + g_h * g_h + g_w * g_w) + 1.0)
            p = poly(opac, v)
            s = p * p
            opacity = (alpha_top * s) * inverse_of(1.0 + s)
            weight = through * opacity
            through = through - weight
            half = 0.5 * weight
            shaded = [half + half * jnp.tanh(poly(colour[c], v)) for c in range(3)]
            base_sums = [base_sums[c] + shaded[c] for c in range(3)]
            tilted = [inverse * shaded[c] for c in range(3)]
            new = []
            for l in range(4):
                facing = jnp.abs(g_z * light[l][0] + g_h * light[l][1] + g_w * light[l][2])
                for c in range(3):
                    new.append(sums[3 * l + c] + facing * tilted[c])
            return through, new, base_sums

        state = (jnp.ones((ROWS, LANES), F32), [zero] * 12, [zero] * 3)

        def group(g, state):
            for i in range(8):
                state = cell(g * 8 + i, state)
            return state

        through, sums, base_sums = lax.fori_loop(0, cells // 8, group, state)
        for l in range(4):
            for c in range(3):
                images[k // each, 3 * l + c, k % each] = light_ref[l, c] * (
                    0.2 * base_sums[c] + sums[3 * l + c]
                )
        images[k // each, 12, k % each] = 1.0 - through
        return carry

    lax.fori_loop(0, count, column, 0)


def fold(place_ref, *refs):
    pieces, (out_ref, parts, sem) = refs[:-3], refs[-3:]
    slabs, channels = parts.shape[0], parts.shape[1]
    copies = []
    for i, ref in enumerate(pieces):
        slab = lax.rem(place_ref[0] - SHIFTS[i] + slabs, slabs)
        copies.append(pltpu.make_async_copy(ref, parts.at[slab], sem.at[i]))
    for copy in copies:
        copy.start()
    for copy in copies:
        copy.wait()
    for tile in range(parts.shape[2]):
        through = 1.0 - parts[0, 12, tile]
        total = [parts[0, ch, tile] for ch in range(channels)]
        for slab in range(1, slabs):
            total = [total[ch] + through * parts[slab, ch, tile] for ch in range(channels)]
            through = through * (1.0 - parts[slab, 12, tile])
        for ch in range(channels):
            out_ref[ch, tile] = total[ch]


def spread(offsets, place_ref, *refs):
    pieces, out_ref, sem = refs[:-2], refs[-2], refs[-1]
    count = len(pieces)
    tiles = out_ref.shape[1] // count
    copies = []
    for i, ref in enumerate(pieces):
        owner = lax.rem(place_ref[0] - offsets[i] + count, count)
        copies.append(
            pltpu.make_async_copy(ref, out_ref.at[:, pl.ds(owner * tiles, tiles)], sem.at[i])
        )
    for copy in copies:
        copy.start()
    for copy in copies:
        copy.wait()


def in_vmem(count):
    return [pl.BlockSpec(memory_space=VMEM)] * count


def in_smem(count):
    return [pl.BlockSpec(memory_space=pltpu.SMEM)] * count


def anywhere(count):
    return [pl.BlockSpec(memory_space=pl.ANY)] * count


def shape(*dims):
    return jax.ShapeDtypeStruct(dims, F32)


def ring(axis, by):
    count = lax.axis_size(axis)
    return [(i, (i + by) % count) for i in range(count)]


def per_device(volume, colour_coef, opacity_coef, light_dir, light_colour):
    slabs, bands = lax.axis_size("depth"), lax.axis_size("height")
    cells, rows, width = volume.shape
    tiles = width // LANES
    slab, band = lax.axis_index("depth"), lax.axis_index("height")
    limit = pltpu.CompilerParams(vmem_limit_bytes=63 << 20)
    field = volume.reshape(cells, rows, tiles, LANES).transpose(0, 2, 1, 3)

    down, up, first, last = pl.pallas_call(
        pack,
        out_shape=[shape(tiles, 3 * cells, LANES)] * 2 + [shape(3, tiles, rows, LANES)] * 2,
        in_specs=anywhere(1),
        out_specs=anywhere(4),
        scratch_shapes=[
            VMEM((cells, tiles, rows, LANES), F32),
            VMEM((tiles, 3 * cells, LANES), F32),
            VMEM((tiles, 3 * cells, LANES), F32),
            DMA((cells // 8,)),
            DMA((2,)),
            DMA((cells // 4,)),
        ],
        compiler_params=limit,
        name="pack",
    )(field)
    low = lax.ppermute(last, "depth", ring("depth", 1))
    high = lax.ppermute(first, "depth", ring("depth", -1))
    top = lax.ppermute(down, "height", ring("height", 1))
    bottom = lax.ppermute(up, "height", ring("height", -1))
    corner_down, corner_up = pl.pallas_call(
        pack_corners,
        out_shape=[shape(tiles, rows, LANES)] * 2,
        in_specs=anywhere(2),
        out_specs=in_vmem(2),
        scratch_shapes=[VMEM((2, 2, tiles, rows, LANES), F32), DMA((2,))],
        compiler_params=limit,
        cost_estimate=pl.CostEstimate(
            flops=400_000_000, bytes_accessed=80_000_000, transcendentals=0
        ),
        name="pack_corners",
    )(low, high)
    top_corner = lax.ppermute(corner_down, "height", ring("height", 1))
    bottom_corner = lax.ppermute(corner_up, "height", ring("height", -1))

    edges = jnp.stack([slab > 0, slab < slabs - 1, band > 0, band < bands - 1]).astype(F32)
    each = tiles // slabs
    rest = tiles - FAR * each
    alpha_top = 2.0 / (cells * slabs)
    piece = shape(13, each, rows, LANES)
    order = [(slab + by) % slabs * each + k for by in SHIFTS for k in range(each)]
    *pieces, twice, slope = pl.pallas_call(
        functools.partial(render, alpha_top=alpha_top),
        out_shape=[piece] * FAR
        + [shape(rest, cells + 2, 16, LANES), shape(rest, cells + 1, rows, LANES)],
        in_specs=in_smem(6) + anywhere(7),
        out_specs=anywhere(FAR + 2),
        scratch_shapes=[
            VMEM((cells + 6, tiles, 24, LANES), F32),
            VMEM((cells + 4, tiles, 16, LANES), F32),
            VMEM((cells + 2, tiles, 16, LANES), F32),
            VMEM((cells + 1, tiles, rows, LANES), F32),
            VMEM((2, tiles, 2, rows, LANES), F32),
            VMEM((2, tiles, 2, rows, LANES), F32),
            VMEM((tiles, 2, rows, LANES), F32),
            VMEM((2, tiles, 3 * cells, LANES), F32),
            VMEM((2, tiles, rows, LANES), F32),
            VMEM((FAR, 13, each, rows, LANES), F32),
            DMA((7,)),
            DMA((2, rest)),
            DMA((FAR,)),
        ],
        compiler_params=limit,
        name="render",
    )(
        edges,
        jnp.stack(order).astype(jnp.int32),
        colour_coef,
        opacity_coef,
        light_dir,
        light_colour,
        field,
        low,
        high,
        top,
        bottom,
        top_corner,
        bottom_corner,
    )
    pieces += pl.pallas_call(
        functools.partial(render_rest, alpha_top=alpha_top),
        out_shape=[piece] * (slabs - FAR),
        in_specs=in_smem(4) + anywhere(2),
        out_specs=anywhere(slabs - FAR),
        scratch_shapes=[
            VMEM((rest, cells + 2, 16, LANES), F32),
            VMEM((rest, cells + 1, rows, LANES), F32),
            VMEM((slabs - FAR, 13, each, rows, LANES), F32),
            DMA((2, rest)),
            DMA((slabs - FAR,)),
        ],
        compiler_params=limit,
        cost_estimate=pl.CostEstimate(
            flops=50_000_000, bytes_accessed=20_000_000, transcendentals=1_000_000
        ),
        name="render_rest",
    )(colour_coef, opacity_coef, light_dir, light_colour, twice, slope)
    arrived = [
        lax.ppermute(value, "depth", ring("depth", by)) if by else value
        for value, by in zip(pieces, SHIFTS)
    ]
    own = pl.pallas_call(
        fold,
        out_shape=piece,
        in_specs=in_smem(1) + anywhere(slabs),
        out_specs=pl.BlockSpec(memory_space=VMEM),
        scratch_shapes=[VMEM((slabs, 13, each, rows, LANES), F32), DMA((slabs,))],
        compiler_params=limit,
        name="fold",
    )(slab[None], *arrived)
    known = {0: own}
    for by in (1, -1, 2, -2):
        known[by] = lax.ppermute(own, "depth", ring("depth", by))
    for held, by in ((2, 1), (-2, -1), (2, 2)):
        known[held + by] = lax.ppermute(known[held], "depth", ring("depth", by))
    image = pl.pallas_call(
        functools.partial(spread, list(known)),
        out_shape=shape(13, tiles, rows, LANES),
        in_specs=in_smem(1) + anywhere(slabs),
        out_specs=pl.BlockSpec(memory_space=VMEM),
        scratch_shapes=[DMA((slabs,))],
        compiler_params=limit,
        name="spread",
    )(slab[None], *known.values())
    return image.transpose(0, 2, 1, 3).reshape(13, rows, width)


def solution(mesh):
    placed = (P("depth", "height", None), P(), P(), P(), P())
    return jax.shard_map(
        per_device, mesh=mesh, in_specs=placed, out_specs=P(None, "height", None), check_vma=False
    )
```

```python
import functools

import jax
import jax.numpy as jnp
from jax import lax
from jax.experimental import pallas as pl
from jax.experimental.pallas import tpu as pltpu
from jax.sharding import PartitionSpec as P

VMEM = pltpu.VMEM
DMA = pltpu.SemaphoreType.DMA
F32 = jnp.float32
LANES = 128
ROWS = 8
BAND = 8
OWN = 4


def inverse_of(q):
    return pltpu.reciprocal(q, approx=True)


def flux(d):
    return d * inverse_of(d * d + 1.0)


def pack(vol_ref, down_ref, up_ref, first_ref, last_ref, held, down, up, in_sem, edge_sem, out_sem):
    cells, tiles = vol_ref.shape[0], vol_ref.shape[1]
    groups = cells // 8
    loads = [
        pltpu.make_async_copy(vol_ref.at[pl.ds(8 * g, 8)], held.at[pl.ds(8 * g, 8)], in_sem.at[g])
        for g in range(groups)
    ]
    edges = [
        pltpu.make_async_copy(held.at[pl.ds(0, 3)], first_ref, edge_sem.at[0]),
        pltpu.make_async_copy(held.at[pl.ds(cells - 3, 3)], last_ref, edge_sem.at[1]),
    ]
    for copy in loads:
        copy.start()
    stores = []
    for g in range(groups):
        loads[g].wait()
        if g == 0:
            edges[0].start()
        if g == groups - 1:
            edges[1].start()
        for k in range(8):
            z = 8 * g + k
            for tile in range(tiles):
                up[tile, 3 * z : 3 * z + 3, :] = held[z, tile, 0:3, :]
                down[tile, 3 * z : 3 * z + 3, :] = held[z, tile, 5:8, :]
        part = pl.ds(24 * g, 24)
        for i, (ref, out_ref) in enumerate(((down, down_ref), (up, up_ref))):
            copy = pltpu.make_async_copy(
                ref.at[:, part, :], out_ref.at[:, part, :], out_sem.at[2 * g + i]
            )
            copy.start()
            stores.append(copy)
    for copy in stores + edges:
        copy.wait()


CORNERS = ((0, 1, 0), (0, 0, 0), (0, 1, 1), (1, 0, 0), (1, 1, 0), (1, 0, 1))


def pack_corners(low_ref, high_ref, down_ref, up_ref, near, sem):
    tiles = low_ref.shape[1]
    copies = [
        pltpu.make_async_copy(low_ref.at[pl.ds(1, 2)], near.at[0], sem.at[0]),
        pltpu.make_async_copy(high_ref.at[pl.ds(0, 2)], near.at[1], sem.at[1]),
    ]
    for copy in copies:
        copy.start()
    for copy in copies:
        copy.wait()
    zero = jnp.zeros((2, LANES), F32)
    for tile in range(tiles):
        for slot, (side, plane, depth) in enumerate(CORNERS):
            up_ref[tile, slot : slot + 1, :] = near[side, plane, tile, depth : depth + 1, :]
            down_ref[tile, slot : slot + 1, :] = near[side, plane, tile, 7 - depth : 8 - depth, :]
        up_ref[tile, 6:8, :] = zero
        down_ref[tile, 6:8, :] = zero


def beside(src, base, z, parity, nexts):
    tiles = src.shape[1]
    lane = lax.broadcasted_iota(jnp.int32, (ROWS, LANES), 1)
    for part in range(2):
        rows = pl.ds(base + 8 * part, 8)
        turned = [pltpu.roll(src[z, tile, rows, :], LANES - 1, 1) for tile in range(tiles)]
        for tile in range(tiles):
            later = turned[tile + 1] if tile + 1 < tiles else 0.0
            nexts[parity, tile, part] = jnp.where(lane == LANES - 1, later, turned[tile])


def width_flux(src, base, z, parity, nexts, nets):
    tiles = src.shape[1]
    lane = lax.broadcasted_iota(jnp.int32, (ROWS, LANES), 1)
    for part in range(2):
        rows = pl.ds(base + 8 * part, 8)
        earlier = None
        for tile in range(tiles):
            u = src[z, tile, rows, :]
            across = flux(nexts[parity, tile, part] - u)
            turned = pltpu.roll(across, 1, 1)
            behind = flux(u) if earlier is None else earlier
            nets[parity, tile, part] = across - jnp.where(lane == 0, behind, turned)
            earlier = turned


def diffuse_plane(src, base, z, parity, nets, held, dst, out, rims):
    tiles = src.shape[1]
    sub = lax.broadcasted_iota(jnp.int32, (ROWS, LANES), 0)
    for tile in range(tiles):
        below = None
        for part in range(2):
            first = base + 8 * part
            u = src[z, tile, pl.ds(first, 8), :]
            if first + 9 <= src.shape[2]:
                above = src[z, tile, pl.ds(first + 1, 8), :]
            else:
                above = pltpu.roll(u, ROWS - 1, 0)
            up = flux(above - u)
            turned = pltpu.roll(up, 1, 0)
            along = up - (turned if part == 0 else jnp.where(sub == 0, below, turned))
            below = turned
            ahead = flux(src[z + 1, tile, pl.ds(first, 8), :] - u)
            total = (nets[parity, tile, part] + along) + (ahead - held[tile, part])
            held[tile, part] = ahead
            dst[out, tile, pl.ds(8 * part, 8), :] = (u + 0.12 * total) * rims[part]


def width_slope(field, z, slope):
    tiles = field.shape[1]
    lane = lax.broadcasted_iota(jnp.int32, (ROWS, LANES), 1)
    rows = pl.ds(OWN, 8)
    now = field[z, 0, rows, :]
    lowered, raised = pltpu.roll(now, LANES - 1, 1), pltpu.roll(now, 1, 1)
    earlier = 0.0
    for tile in range(tiles):
        if tile + 1 < tiles:
            later = field[z, tile + 1, rows, :]
            later_lowered, later_raised = pltpu.roll(later, LANES - 1, 1), pltpu.roll(later, 1, 1)
        else:
            later_lowered, later_raised = 0.0, None
        slope[z, tile] = jnp.where(lane == LANES - 1, later_lowered, lowered) - jnp.where(
            lane == 0, earlier, raised
        )
        earlier, lowered, raised = raised, later_lowered, later_raised


def diffuse(src, base, dst, planes, nexts, nets, held, rims, slope=None):
    for tile in range(src.shape[1]):
        for part in range(2):
            rows = pl.ds(base + 8 * part, 8)
            held[tile, part] = flux(src[1, tile, rows, :] - src[0, tile, rows, :])
    beside(src, base, 1, 1, nexts)
    width_flux(src, base, 1, 1, nexts, nets)
    beside(src, base, 2, 0, nexts)

    def pair(g, carry):
        for k in range(2):
            z = 2 * g + k + 1
            beside(src, base, jnp.minimum(z + 2, planes + 1), 1 - k, nexts)
            width_flux(src, base, z + 1, k, nexts, nets)
            diffuse_plane(src, base, z, 1 - k, nets, held, dst, z - 1, rims)
            if slope is not None:
                width_slope(dst, jnp.maximum(z - 3, 0), slope)
        return carry

    lax.fori_loop(0, planes // 2, pair, 0)
    if slope is not None:
        width_slope(dst, planes - 2, slope)


SHIFTS = (4, 3, 5, 2, 6, 1, 7, 0)
FAR = 3


def render(
    edge_ref,
    tile_ref,
    colour_ref,
    opacity_ref,
    dir_ref,
    light_ref,
    vol_ref,
    low_ref,
    high_ref,
    top_ref,
    bottom_ref,
    top_corner_ref,
    bottom_corner_ref,
    *refs,
    alpha_top,
):
    out_refs, twice_ref, slope_ref = refs[:FAR], refs[FAR], refs[FAR + 1]
    (field, once, twice, slope, nexts, nets, held, rows_in, corners_in, images) = refs[FAR + 2 : -3]
    sem, later_sem, out_sem = refs[-3:]
    cells, tiles = vol_ref.shape[0], vol_ref.shape[1]
    own = pl.ds(BAND, 8)
    copies = [
        pltpu.make_async_copy(low_ref, field.at[pl.ds(0, 3), :, own, :], sem.at[0]),
        pltpu.make_async_copy(high_ref, field.at[pl.ds(cells + 3, 3), :, own, :], sem.at[1]),
        pltpu.make_async_copy(top_corner_ref, corners_in.at[0], sem.at[2]),
        pltpu.make_async_copy(bottom_corner_ref, corners_in.at[1], sem.at[3]),
        pltpu.make_async_copy(top_ref, rows_in.at[0], sem.at[4]),
        pltpu.make_async_copy(bottom_ref, rows_in.at[1], sem.at[5]),
        pltpu.make_async_copy(vol_ref, field.at[pl.ds(3, cells), :, own, :], sem.at[6]),
    ]
    for copy in copies:
        copy.start()

    sub = lax.broadcasted_iota(jnp.int32, (ROWS, LANES), 0)
    keep_low, keep_high = edge_ref[0], edge_ref[1]
    keep_top, keep_bottom = edge_ref[2], edge_ref[3]
    rims = (
        jnp.where(sub < OWN, jnp.full((ROWS, LANES), keep_top), 1.0),
        jnp.where(sub >= OWN, jnp.full((ROWS, LANES), keep_bottom), 1.0),
    )

    zero = jnp.zeros((ROWS, LANES), F32)
    for k in range(3):
        for tile in range(tiles):
            for plane in (k, cells + 3 + k):
                field[plane, tile, 0:8, :] = zero
                field[plane, tile, 16:24, :] = zero
    for copy in copies[:4]:
        copy.wait()
    for k in range(3):
        for tile in range(tiles):
            field[k, tile, own, :] = field[k, tile, own, :] * keep_low
            field[cells + 3 + k, tile, own, :] = field[cells + 3 + k, tile, own, :] * keep_high
    for tile in range(tiles):
        for slot, (side, plane, away) in enumerate(CORNERS):
            at = (cells + 3 if side else 1) + plane
            keep = keep_high if side else keep_low
            field[at, tile, 7 - away : 8 - away, :] = corners_in[0, tile, slot : slot + 1, :] * (
                keep * keep_top
            )
            field[at, tile, 16 + away : 17 + away, :] = corners_in[
                1, tile, slot : slot + 1, :
            ] * (keep * keep_bottom)
    copies[4].wait()
    copies[5].wait()

    def rims_in(g, carry):
        at = pl.multiple_of(24 * g, 24)
        for tile in range(tiles):
            for k in range(8):
                field[8 * g + k + 3, tile, 5:8, :] = (
                    rows_in[0, tile, pl.ds(at + 3 * k, 3), :] * keep_top
                )
                field[8 * g + k + 3, tile, 16:19, :] = (
                    rows_in[1, tile, pl.ds(at + 3 * k, 3), :] * keep_bottom
                )
        return carry

    lax.fori_loop(0, cells // 8, rims_in, 0)
    copies[6].wait()

    diffuse(field, OWN, once, cells + 4, nexts, nets, held, rims)
    for k in range(2):
        for tile in range(tiles):
            for rows in (slice(0, 8), slice(8, 16)):
                once[k, tile, rows, :] = once[k, tile, rows, :] * keep_low
                once[cells + 2 + k, tile, rows, :] = once[cells + 2 + k, tile, rows, :] * keep_high
    diffuse(once, 0, twice, cells + 2, nexts, nets, held, rims, slope)
    own = pl.ds(OWN, 8)
    for tile in range(tiles):
        twice[0, tile, own, :] = twice[0, tile, own, :] * keep_low
        twice[cells + 1, tile, own, :] = twice[cells + 1, tile, own, :] * keep_high

    each = tiles // len(SHIFTS)
    ahead = FAR * each
    later = []
    for k in range(tiles - ahead):
        tile = tile_ref[ahead + k]
        later += [
            pltpu.make_async_copy(twice.at[:, tile], twice_ref.at[k], later_sem.at[0, k]),
            pltpu.make_async_copy(slope.at[:, tile], slope_ref.at[k], later_sem.at[1, k]),
        ]
    for copy in later:
        copy.start()

    def smooth(k, z, row):
        return twice[z, tile_ref[k], pl.ds(row, 8), :]

    def across(k, z):
        return slope[z, tile_ref[k]]

    coefs = (colour_ref, opacity_ref, dir_ref, light_ref)
    shade(coefs, cells, ahead, smooth, across, images, out_refs, out_sem, alpha_top)
    for copy in later:
        copy.wait()


def render_rest(colour_ref, opacity_ref, dir_ref, light_ref, twice_ref, slope_ref, *refs, alpha_top):
    out_refs, (twice, slope, images, sem, out_sem) = refs[:-5], refs[-5:]
    count, cells = slope.shape[0], slope.shape[1] - 1

    def load(k):
        return [
            pltpu.make_async_copy(twice_ref.at[k], twice.at[k], sem.at[0, k]),
            pltpu.make_async_copy(slope_ref.at[k], slope.at[k], sem.at[1, k]),
        ]

    for k in range(count):
        for copy in load(k):
            copy.start()

    def ready(k):
        for copy in load(k):
            copy.wait()

    def smooth(k, z, row):
        return twice[k, z, pl.ds(row, 8), :]

    def across(k, z):
        return slope[k, z]

    coefs = (colour_ref, opacity_ref, dir_ref, light_ref)
    shade(coefs, cells, count, smooth, across, images, out_refs, out_sem, alpha_top, ready)


def shade(
    coefs, cells, count, smooth, across, images, out_refs, out_sem, alpha_top, ready=None
):
    colour_ref, opacity_ref, dir_ref, light_ref = coefs
    each = images.shape[2]
    copies = [
        pltpu.make_async_copy(images.at[i], ref, out_sem.at[i]) for i, ref in enumerate(out_refs)
    ]
    zero = jnp.zeros((ROWS, LANES), F32)
    colour = [[colour_ref[c, j] for j in range(4)] for c in range(3)]
    opac = [opacity_ref[j] for j in range(4)]
    light = [[0.5 * dir_ref[l, d] for d in range(3)] for l in range(4)]

    def poly(c, v):
        return ((c[3] * v + c[2]) * v + c[1]) * v + c[0]

    def column(k, carry):
        if ready is not None:
            ready(k)

        def cell(z, state):
            through, sums, base_sums = state
            v = smooth(k, z + 1, OWN)
            g_z = smooth(k, z + 2, OWN) - smooth(k, z, OWN)
            g_h = smooth(k, z + 1, OWN + 1) - smooth(k, z + 1, OWN - 1)
            g_w = across(k, z + 1)
            inverse = lax.rsqrt(0.25 * (g_z * g_z + g_h * g_h + g_w * g_w) + 1.0)
            p = poly(opac, v)
            s = p * p
            opacity = (alpha_top * s) * inverse_of(1.0 + s)
            weight = through * opacity
            through = through - weight
            half = 0.5 * weight
            shaded = [half + half * jnp.tanh(poly(colour[c], v)) for c in range(3)]
            base_sums = [base_sums[c] + shaded[c] for c in range(3)]
            tilted = [inverse * shaded[c] for c in range(3)]
            new = []
            for l in range(4):
                facing = jnp.abs(g_z * light[l][0] + g_h * light[l][1] + g_w * light[l][2])
                for c in range(3):
                    new.append(sums[3 * l + c] + facing * tilted[c])
            return through, new, base_sums

        state = (jnp.ones((ROWS, LANES), F32), [zero] * 12, [zero] * 3)

        def group(g, state):
            for i in range(8):
                state = cell(g * 8 + i, state)
            return state

        through, sums, base_sums = lax.fori_loop(0, cells // 8, group, state)
        for l in range(4):
            for c in range(3):
                images[k // each, 3 * l + c, k % each] = light_ref[l, c] * (
                    0.2 * base_sums[c] + sums[3 * l + c]
                )
        images[k // each, 12, k % each] = 1.0 - through
        for i, copy in enumerate(copies):
            pl.when(k == (i + 1) * each - 1)(copy.start)
        return carry

    lax.fori_loop(0, count, column, 0)
    for copy in copies:
        copy.wait()


def fold(place_ref, *refs):
    pieces, out_ref = refs[:-1], refs[-1]
    slabs = len(pieces)
    channels, tiles = out_ref.shape[0], out_ref.shape[1]
    owner = [lax.rem(place_ref[0] - by + slabs, slabs) for by in SHIFTS]
    for tile in range(tiles):
        through = [1.0 - ref[12, tile] for ref in pieces]
        weight = []
        for i in range(slabs):
            product = None
            for j in range(slabs):
                if j != i:
                    factor = jnp.where(owner[j] < owner[i], through[j], 1.0)
                    product = factor if product is None else product * factor
            weight.append(product)
        for ch in range(channels):
            out_ref[ch, tile] = sum(weight[i] * pieces[i][ch, tile] for i in range(slabs))


def spread(offsets, place_ref, *refs):
    pieces, out_ref, sem = refs[:-2], refs[-2], refs[-1]
    count = len(pieces)
    tiles = out_ref.shape[1] // count
    copies = []
    for i, ref in enumerate(pieces):
        owner = lax.rem(place_ref[0] - offsets[i] + count, count)
        copies.append(
            pltpu.make_async_copy(ref, out_ref.at[:, pl.ds(owner * tiles, tiles)], sem.at[i])
        )
    for copy in copies:
        copy.start()
    for copy in copies:
        copy.wait()


def in_vmem(count):
    return [pl.BlockSpec(memory_space=VMEM)] * count


def in_smem(count):
    return [pl.BlockSpec(memory_space=pltpu.SMEM)] * count


def anywhere(count):
    return [pl.BlockSpec(memory_space=pl.ANY)] * count


def shape(*dims):
    return jax.ShapeDtypeStruct(dims, F32)


def ring(axis, by):
    count = lax.axis_size(axis)
    return [(i, (i + by) % count) for i in range(count)]


def per_device(volume, colour_coef, opacity_coef, light_dir, light_colour):
    slabs, bands = lax.axis_size("depth"), lax.axis_size("height")
    cells, rows, width = volume.shape
    tiles = width // LANES
    slab, band = lax.axis_index("depth"), lax.axis_index("height")
    limit = pltpu.CompilerParams(vmem_limit_bytes=63 << 20)
    field = volume.reshape(cells, rows, tiles, LANES).transpose(0, 2, 1, 3)

    down, up, first, last = pl.pallas_call(
        pack,
        out_shape=[shape(tiles, 3 * cells, LANES)] * 2 + [shape(3, tiles, rows, LANES)] * 2,
        in_specs=anywhere(1),
        out_specs=anywhere(4),
        scratch_shapes=[
            VMEM((cells, tiles, rows, LANES), F32),
            VMEM((tiles, 3 * cells, LANES), F32),
            VMEM((tiles, 3 * cells, LANES), F32),
            DMA((cells // 8,)),
            DMA((2,)),
            DMA((cells // 4,)),
        ],
        compiler_params=limit,
        name="pack",
    )(field)
    low = lax.ppermute(last, "depth", ring("depth", 1))
    high = lax.ppermute(first, "depth", ring("depth", -1))
    top = lax.ppermute(down, "height", ring("height", 1))
    bottom = lax.ppermute(up, "height", ring("height", -1))
    corner_down, corner_up = pl.pallas_call(
        pack_corners,
        out_shape=[shape(tiles, rows, LANES)] * 2,
        in_specs=anywhere(2),
        out_specs=in_vmem(2),
        scratch_shapes=[VMEM((2, 2, tiles, rows, LANES), F32), DMA((2,))],
        compiler_params=limit,
        cost_estimate=pl.CostEstimate(
            flops=400_000_000, bytes_accessed=80_000_000, transcendentals=0
        ),
        name="pack_corners",
    )(low, high)
    top_corner = lax.ppermute(corner_down, "height", ring("height", 1))
    bottom_corner = lax.ppermute(corner_up, "height", ring("height", -1))

    edges = jnp.stack([slab > 0, slab < slabs - 1, band > 0, band < bands - 1]).astype(F32)
    each = tiles // slabs
    rest = tiles - FAR * each
    alpha_top = 2.0 / (cells * slabs)
    piece = shape(13, each, rows, LANES)
    order = [(slab + by) % slabs * each + k for by in SHIFTS for k in range(each)]
    *pieces, twice, slope = pl.pallas_call(
        functools.partial(render, alpha_top=alpha_top),
        out_shape=[piece] * FAR
        + [shape(rest, cells + 2, 16, LANES), shape(rest, cells + 1, rows, LANES)],
        in_specs=in_smem(6) + anywhere(7),
        out_specs=anywhere(FAR + 2),
        scratch_shapes=[
            VMEM((cells + 6, tiles, 24, LANES), F32),
            VMEM((cells + 4, tiles, 16, LANES), F32),
            VMEM((cells + 2, tiles, 16, LANES), F32),
            VMEM((cells + 1, tiles, rows, LANES), F32),
            VMEM((2, tiles, 2, rows, LANES), F32),
            VMEM((2, tiles, 2, rows, LANES), F32),
            VMEM((tiles, 2, rows, LANES), F32),
            VMEM((2, tiles, 3 * cells, LANES), F32),
            VMEM((2, tiles, rows, LANES), F32),
            VMEM((FAR, 13, each, rows, LANES), F32),
            DMA((7,)),
            DMA((2, rest)),
            DMA((FAR,)),
        ],
        compiler_params=limit,
        name="render",
    )(
        edges,
        jnp.stack(order).astype(jnp.int32),
        colour_coef,
        opacity_coef,
        light_dir,
        light_colour,
        field,
        low,
        high,
        top,
        bottom,
        top_corner,
        bottom_corner,
    )
    pieces += pl.pallas_call(
        functools.partial(render_rest, alpha_top=alpha_top),
        out_shape=[piece] * (slabs - FAR),
        in_specs=in_smem(4) + anywhere(2),
        out_specs=anywhere(slabs - FAR),
        scratch_shapes=[
            VMEM((rest, cells + 2, 16, LANES), F32),
            VMEM((rest, cells + 1, rows, LANES), F32),
            VMEM((slabs - FAR, 13, each, rows, LANES), F32),
            DMA((2, rest)),
            DMA((slabs - FAR,)),
        ],
        compiler_params=limit,
        cost_estimate=pl.CostEstimate(
            flops=50_000_000, bytes_accessed=20_000_000, transcendentals=1_000_000
        ),
        name="render_rest",
    )(colour_coef, opacity_coef, light_dir, light_colour, twice, slope)
    arrived = [
        lax.ppermute(value, "depth", ring("depth", by)) if by else value
        for value, by in zip(pieces, SHIFTS)
    ]
    own = pl.pallas_call(
        fold,
        out_shape=piece,
        in_specs=in_smem(1) + in_vmem(slabs),
        out_specs=pl.BlockSpec(memory_space=VMEM),
        compiler_params=limit,
        name="fold",
    )(slab[None], *arrived)
    known = {0: own}
    for by in (1, -1, 2, -2):
        known[by] = lax.ppermute(own, "depth", ring("depth", by))
    for held, by in ((2, 1), (-2, -1), (2, 2)):
        known[held + by] = lax.ppermute(known[held], "depth", ring("depth", by))
    image = pl.pallas_call(
        functools.partial(spread, list(known)),
        out_shape=shape(13, tiles, rows, LANES),
        in_specs=in_smem(1) + anywhere(slabs),
        out_specs=pl.BlockSpec(memory_space=VMEM),
        scratch_shapes=[DMA((slabs,))],
        compiler_params=limit,
        name="spread",
    )(slab[None], *known.values())
    return image.transpose(0, 2, 1, 3).reshape(13, rows, width)


def solution(mesh):
    placed = (P("depth", "height", None), P(), P(), P(), P())
    return jax.shard_map(
        per_device, mesh=mesh, in_specs=placed, out_specs=P(None, "height", None), check_vma=False
    )
```

```python
import functools

import jax
import jax.numpy as jnp
from jax import lax
from jax.experimental import pallas as pl
from jax.experimental.pallas import tpu as pltpu
from jax.sharding import PartitionSpec as P

VMEM = pltpu.VMEM
DMA = pltpu.SemaphoreType.DMA
F32 = jnp.float32
LANES = 128
ROWS = 8
BAND = 8
OWN = 4


def inverse_of(q):
    return pltpu.reciprocal(q, approx=True)


def flux(d):
    return d * inverse_of(d * d + 1.0)


def pack(vol_ref, down_ref, up_ref, first_ref, last_ref, held, down, up, in_sem, edge_sem, out_sem):
    cells, tiles = vol_ref.shape[0], vol_ref.shape[1]
    groups = cells // 8
    loads = [
        pltpu.make_async_copy(vol_ref.at[pl.ds(8 * g, 8)], held.at[pl.ds(8 * g, 8)], in_sem.at[g])
        for g in range(groups)
    ]
    edges = [
        pltpu.make_async_copy(held.at[pl.ds(0, 3)], first_ref, edge_sem.at[0]),
        pltpu.make_async_copy(held.at[pl.ds(cells - 3, 3)], last_ref, edge_sem.at[1]),
    ]
    for copy in loads:
        copy.start()
    stores = []
    for g in range(groups):
        loads[g].wait()
        if g == 0:
            edges[0].start()
        if g == groups - 1:
            edges[1].start()
        for k in range(8):
            z = 8 * g + k
            for tile in range(tiles):
                up[tile, 3 * z : 3 * z + 3, :] = held[z, tile, 0:3, :]
                down[tile, 3 * z : 3 * z + 3, :] = held[z, tile, 5:8, :]
        part = pl.ds(24 * g, 24)
        for i, (ref, out_ref) in enumerate(((down, down_ref), (up, up_ref))):
            copy = pltpu.make_async_copy(
                ref.at[:, part, :], out_ref.at[:, part, :], out_sem.at[2 * g + i]
            )
            copy.start()
            stores.append(copy)
    for copy in stores + edges:
        copy.wait()


CORNERS = ((0, 1, 0), (0, 0, 0), (0, 1, 1), (1, 0, 0), (1, 1, 0), (1, 0, 1))


def pack_corners(low_ref, high_ref, down_ref, up_ref, near, sem):
    tiles = low_ref.shape[1]
    copies = [
        pltpu.make_async_copy(low_ref.at[pl.ds(1, 2)], near.at[0], sem.at[0]),
        pltpu.make_async_copy(high_ref.at[pl.ds(0, 2)], near.at[1], sem.at[1]),
    ]
    for copy in copies:
        copy.start()
    for copy in copies:
        copy.wait()
    zero = jnp.zeros((2, LANES), F32)
    for tile in range(tiles):
        for slot, (side, plane, depth) in enumerate(CORNERS):
            up_ref[tile, slot : slot + 1, :] = near[side, plane, tile, depth : depth + 1, :]
            down_ref[tile, slot : slot + 1, :] = near[side, plane, tile, 7 - depth : 8 - depth, :]
        up_ref[tile, 6:8, :] = zero
        down_ref[tile, 6:8, :] = zero


def beside(src, base, z, parity, nexts):
    tiles = src.shape[1]
    lane = lax.broadcasted_iota(jnp.int32, (ROWS, LANES), 1)
    for part in range(2):
        rows = pl.ds(base + 8 * part, 8)
        turned = [pltpu.roll(src[z, tile, rows, :], LANES - 1, 1) for tile in range(tiles)]
        for tile in range(tiles):
            later = turned[tile + 1] if tile + 1 < tiles else 0.0
            nexts[parity, tile, part] = jnp.where(lane == LANES - 1, later, turned[tile])


def width_flux(src, base, z, parity, nexts, nets):
    tiles = src.shape[1]
    lane = lax.broadcasted_iota(jnp.int32, (ROWS, LANES), 1)
    for part in range(2):
        rows = pl.ds(base + 8 * part, 8)
        earlier = None
        for tile in range(tiles):
            u = src[z, tile, rows, :]
            across = flux(nexts[parity, tile, part] - u)
            turned = pltpu.roll(across, 1, 1)
            behind = flux(u) if earlier is None else earlier
            nets[parity, tile, part] = across - jnp.where(lane == 0, behind, turned)
            earlier = turned


def diffuse_plane(src, base, z, parity, nets, held, dst, out, rims):
    tiles = src.shape[1]
    sub = lax.broadcasted_iota(jnp.int32, (ROWS, LANES), 0)
    for tile in range(tiles):
        below = None
        for part in range(2):
            first = base + 8 * part
            u = src[z, tile, pl.ds(first, 8), :]
            if first + 9 <= src.shape[2]:
                above = src[z, tile, pl.ds(first + 1, 8), :]
            else:
                above = pltpu.roll(u, ROWS - 1, 0)
            up = flux(above - u)
            turned = pltpu.roll(up, 1, 0)
            along = up - (turned if part == 0 else jnp.where(sub == 0, below, turned))
            below = turned
            ahead = flux(src[z + 1, tile, pl.ds(first, 8), :] - u)
            total = (nets[parity, tile, part] + along) + (ahead - held[tile, part])
            held[tile, part] = ahead
            dst[out, tile, pl.ds(8 * part, 8), :] = (u + 0.12 * total) * rims[part]


def width_slope(field, z, slope):
    tiles = field.shape[1]
    lane = lax.broadcasted_iota(jnp.int32, (ROWS, LANES), 1)
    rows = pl.ds(OWN, 8)
    now = field[z, 0, rows, :]
    lowered, raised = pltpu.roll(now, LANES - 1, 1), pltpu.roll(now, 1, 1)
    earlier = 0.0
    for tile in range(tiles):
        if tile + 1 < tiles:
            later = field[z, tile + 1, rows, :]
            later_lowered, later_raised = pltpu.roll(later, LANES - 1, 1), pltpu.roll(later, 1, 1)
        else:
            later_lowered, later_raised = 0.0, None
        slope[z, tile] = jnp.where(lane == LANES - 1, later_lowered, lowered) - jnp.where(
            lane == 0, earlier, raised
        )
        earlier, lowered, raised = raised, later_lowered, later_raised


def diffuse(src, base, dst, planes, nexts, nets, held, rims, slope=None):
    for tile in range(src.shape[1]):
        for part in range(2):
            rows = pl.ds(base + 8 * part, 8)
            held[tile, part] = flux(src[1, tile, rows, :] - src[0, tile, rows, :])
    beside(src, base, 1, 1, nexts)
    width_flux(src, base, 1, 1, nexts, nets)
    beside(src, base, 2, 0, nexts)

    def pair(g, carry):
        for k in range(2):
            z = 2 * g + k + 1
            beside(src, base, jnp.minimum(z + 2, planes + 1), 1 - k, nexts)
            width_flux(src, base, z + 1, k, nexts, nets)
            diffuse_plane(src, base, z, 1 - k, nets, held, dst, z - 1, rims)
            if slope is not None:
                width_slope(dst, jnp.maximum(z - 3, 0), slope)
        return carry

    lax.fori_loop(0, planes // 2, pair, 0)
    if slope is not None:
        width_slope(dst, planes - 2, slope)


SHIFTS = (4, 3, 5, 2, 6, 1, 7, 0)
FAR = 3


def render(
    edge_ref,
    tile_ref,
    colour_ref,
    opacity_ref,
    dir_ref,
    light_ref,
    vol_ref,
    low_ref,
    high_ref,
    top_ref,
    bottom_ref,
    top_corner_ref,
    bottom_corner_ref,
    *refs,
    alpha_top,
):
    out_refs, twice_ref, slope_ref = refs[:FAR], refs[FAR], refs[FAR + 1]
    (field, once, twice, slope, nexts, nets, held, rows_in, corners_in, images) = refs[FAR + 2 : -3]
    sem, later_sem, out_sem = refs[-3:]
    cells, tiles = vol_ref.shape[0], vol_ref.shape[1]
    own = pl.ds(BAND, 8)
    copies = [
        pltpu.make_async_copy(low_ref, field.at[pl.ds(0, 3), :, own, :], sem.at[0]),
        pltpu.make_async_copy(high_ref, field.at[pl.ds(cells + 3, 3), :, own, :], sem.at[1]),
        pltpu.make_async_copy(top_corner_ref, corners_in.at[0], sem.at[2]),
        pltpu.make_async_copy(bottom_corner_ref, corners_in.at[1], sem.at[3]),
        pltpu.make_async_copy(top_ref, rows_in.at[0], sem.at[4]),
        pltpu.make_async_copy(bottom_ref, rows_in.at[1], sem.at[5]),
        pltpu.make_async_copy(vol_ref, field.at[pl.ds(3, cells), :, own, :], sem.at[6]),
    ]
    for copy in copies:
        copy.start()

    sub = lax.broadcasted_iota(jnp.int32, (ROWS, LANES), 0)
    keep_low, keep_high = edge_ref[0], edge_ref[1]
    keep_top, keep_bottom = edge_ref[2], edge_ref[3]
    rims = (
        jnp.where(sub < OWN, jnp.full((ROWS, LANES), keep_top), 1.0),
        jnp.where(sub >= OWN, jnp.full((ROWS, LANES), keep_bottom), 1.0),
    )

    zero = jnp.zeros((ROWS, LANES), F32)
    for k in range(3):
        for tile in range(tiles):
            for plane in (k, cells + 3 + k):
                field[plane, tile, 0:8, :] = zero
                field[plane, tile, 16:24, :] = zero
    for copy in copies[:4]:
        copy.wait()
    for k in range(3):
        for tile in range(tiles):
            field[k, tile, own, :] = field[k, tile, own, :] * keep_low
            field[cells + 3 + k, tile, own, :] = field[cells + 3 + k, tile, own, :] * keep_high
    for tile in range(tiles):
        for slot, (side, plane, away) in enumerate(CORNERS):
            at = (cells + 3 if side else 1) + plane
            keep = keep_high if side else keep_low
            field[at, tile, 7 - away : 8 - away, :] = corners_in[0, tile, slot : slot + 1, :] * (
                keep * keep_top
            )
            field[at, tile, 16 + away : 17 + away, :] = corners_in[
                1, tile, slot : slot + 1, :
            ] * (keep * keep_bottom)
    copies[4].wait()
    copies[5].wait()

    def rims_in(g, carry):
        at = pl.multiple_of(24 * g, 24)
        for tile in range(tiles):
            for k in range(8):
                field[8 * g + k + 3, tile, 5:8, :] = (
                    rows_in[0, tile, pl.ds(at + 3 * k, 3), :] * keep_top
                )
                field[8 * g + k + 3, tile, 16:19, :] = (
                    rows_in[1, tile, pl.ds(at + 3 * k, 3), :] * keep_bottom
                )
        return carry

    lax.fori_loop(0, cells // 8, rims_in, 0)
    copies[6].wait()

    diffuse(field, OWN, once, cells + 4, nexts, nets, held, rims)
    for k in range(2):
        for tile in range(tiles):
            for rows in (slice(0, 8), slice(8, 16)):
                once[k, tile, rows, :] = once[k, tile, rows, :] * keep_low
                once[cells + 2 + k, tile, rows, :] = once[cells + 2 + k, tile, rows, :] * keep_high
    diffuse(once, 0, twice, cells + 2, nexts, nets, held, rims, slope)
    own = pl.ds(OWN, 8)
    for tile in range(tiles):
        twice[0, tile, own, :] = twice[0, tile, own, :] * keep_low
        twice[cells + 1, tile, own, :] = twice[cells + 1, tile, own, :] * keep_high

    each = tiles // len(SHIFTS)
    ahead = FAR * each
    later = []
    for k in range(tiles - ahead):
        tile = tile_ref[ahead + k]
        later += [
            pltpu.make_async_copy(twice.at[:, tile], twice_ref.at[k], later_sem.at[0, k]),
            pltpu.make_async_copy(slope.at[:, tile], slope_ref.at[k], later_sem.at[1, k]),
        ]
    for copy in later:
        copy.start()

    def smooth(k, z, row):
        return twice[z, tile_ref[k], pl.ds(row, 8), :]

    def across(k, z):
        return slope[z, tile_ref[k]]

    coefs = (colour_ref, opacity_ref, dir_ref, light_ref)
    shade(coefs, cells, ahead, smooth, across, images, out_refs, out_sem, alpha_top)
    for copy in later:
        copy.wait()


def render_rest(colour_ref, opacity_ref, dir_ref, light_ref, twice_ref, slope_ref, *refs, alpha_top):
    out_refs, (twice, slope, images, sem, out_sem) = refs[:-5], refs[-5:]
    count, cells = slope.shape[0], slope.shape[1] - 1

    def load(k):
        return [
            pltpu.make_async_copy(twice_ref.at[k], twice.at[k], sem.at[0, k]),
            pltpu.make_async_copy(slope_ref.at[k], slope.at[k], sem.at[1, k]),
        ]

    for k in range(count):
        for copy in load(k):
            copy.start()

    def ready(k):
        for copy in load(k):
            copy.wait()

    def smooth(k, z, row):
        return twice[k, z, pl.ds(row, 8), :]

    def across(k, z):
        return slope[k, z]

    coefs = (colour_ref, opacity_ref, dir_ref, light_ref)
    shade(coefs, cells, count, smooth, across, images, out_refs, out_sem, alpha_top, ready)


def shade(
    coefs, cells, count, smooth, across, images, out_refs, out_sem, alpha_top, ready=None
):
    colour_ref, opacity_ref, dir_ref, light_ref = coefs
    each = images.shape[2]
    copies = [
        pltpu.make_async_copy(images.at[i], ref, out_sem.at[i]) for i, ref in enumerate(out_refs)
    ]
    zero = jnp.zeros((ROWS, LANES), F32)
    colour = [[colour_ref[c, j] for j in range(4)] for c in range(3)]
    opac = [opacity_ref[j] for j in range(4)]
    light = [[0.5 * dir_ref[l, d] for d in range(3)] for l in range(4)]

    def poly(c, v):
        return ((c[3] * v + c[2]) * v + c[1]) * v + c[0]

    def column(k, carry):
        if ready is not None:
            ready(k)

        def cell(z, state):
            through, sums, base_sums = state
            v = smooth(k, z + 1, OWN)
            g_z = smooth(k, z + 2, OWN) - smooth(k, z, OWN)
            g_h = smooth(k, z + 1, OWN + 1) - smooth(k, z + 1, OWN - 1)
            g_w = across(k, z + 1)
            inverse = lax.rsqrt(0.25 * (g_z * g_z + g_h * g_h + g_w * g_w) + 1.0)
            p = poly(opac, v)
            s = p * p
            opacity = (alpha_top * s) * inverse_of(1.0 + s)
            weight = through * opacity
            through = through - weight
            half = 0.5 * weight
            shaded = [half + half * jnp.tanh(poly(colour[c], v)) for c in range(3)]
            base_sums = [base_sums[c] + shaded[c] for c in range(3)]
            tilted = [inverse * shaded[c] for c in range(3)]
            new = []
            for l in range(4):
                facing = jnp.abs(g_z * light[l][0] + g_h * light[l][1] + g_w * light[l][2])
                for c in range(3):
                    new.append(sums[3 * l + c] + facing * tilted[c])
            return through, new, base_sums

        state = (jnp.ones((ROWS, LANES), F32), [zero] * 12, [zero] * 3)

        def group(g, state):
            for i in range(8):
                state = cell(g * 8 + i, state)
            return state

        through, sums, base_sums = lax.fori_loop(0, cells // 8, group, state)
        for l in range(4):
            for c in range(3):
                images[k // each, 3 * l + c, k % each] = light_ref[l, c] * (
                    0.2 * base_sums[c] + sums[3 * l + c]
                )
        images[k // each, 12, k % each] = 1.0 - through
        for i, copy in enumerate(copies):
            pl.when(k == (i + 1) * each - 1)(copy.start)
        return carry

    lax.fori_loop(0, count, column, 0)
    for copy in copies:
        copy.wait()


def fold(place_ref, *refs):
    pieces, out_ref = refs[:-1], refs[-1]
    slabs = len(pieces)
    channels, tiles = out_ref.shape[0], out_ref.shape[1]
    owner = [lax.rem(place_ref[0] - by + slabs, slabs) for by in SHIFTS]
    for tile in range(tiles):
        through = [1.0 - ref[12, tile] for ref in pieces]
        weight = []
        for i in range(slabs):
            product = None
            for j in range(slabs):
                if j != i:
                    factor = jnp.where(owner[j] < owner[i], through[j], 1.0)
                    product = factor if product is None else product * factor
            weight.append(product)
        for ch in range(channels):
            out_ref[ch, tile] = sum(weight[i] * pieces[i][ch, tile] for i in range(slabs))


def spread(offsets, place_ref, *refs):
    pieces, out_ref, sem = refs[:-2], refs[-2], refs[-1]
    count = len(pieces)
    tiles = out_ref.shape[1] // count
    copies = []
    for i, ref in enumerate(pieces):
        owner = lax.rem(place_ref[0] - offsets[i] + count, count)
        copies.append(
            pltpu.make_async_copy(ref, out_ref.at[:, pl.ds(owner * tiles, tiles)], sem.at[i])
        )
    for copy in copies:
        copy.start()
    for copy in copies:
        copy.wait()


def in_vmem(count):
    return [pl.BlockSpec(memory_space=VMEM)] * count


def in_smem(count):
    return [pl.BlockSpec(memory_space=pltpu.SMEM)] * count


def anywhere(count):
    return [pl.BlockSpec(memory_space=pl.ANY)] * count


def shape(*dims):
    return jax.ShapeDtypeStruct(dims, F32)


def ring(axis, by):
    count = lax.axis_size(axis)
    return [(i, (i + by) % count) for i in range(count)]


def per_device(volume, colour_coef, opacity_coef, light_dir, light_colour):
    slabs, bands = lax.axis_size("depth"), lax.axis_size("height")
    cells, rows, width = volume.shape
    tiles = width // LANES
    slab, band = lax.axis_index("depth"), lax.axis_index("height")
    limit = pltpu.CompilerParams(vmem_limit_bytes=(64 << 20) - (32 << 10))
    field = volume.reshape(cells, rows, tiles, LANES).transpose(0, 2, 1, 3)

    down, up, first, last = pl.pallas_call(
        pack,
        out_shape=[shape(tiles, 3 * cells, LANES)] * 2 + [shape(3, tiles, rows, LANES)] * 2,
        in_specs=anywhere(1),
        out_specs=anywhere(4),
        scratch_shapes=[
            VMEM((cells, tiles, rows, LANES), F32),
            VMEM((tiles, 3 * cells, LANES), F32),
            VMEM((tiles, 3 * cells, LANES), F32),
            DMA((cells // 8,)),
            DMA((2,)),
            DMA((cells // 4,)),
        ],
        compiler_params=limit,
        name="pack",
    )(field)
    low = lax.ppermute(last, "depth", ring("depth", 1))
    high = lax.ppermute(first, "depth", ring("depth", -1))
    top = lax.ppermute(down, "height", ring("height", 1))
    bottom = lax.ppermute(up, "height", ring("height", -1))
    corner_down, corner_up = pl.pallas_call(
        pack_corners,
        out_shape=[shape(tiles, rows, LANES)] * 2,
        in_specs=anywhere(2),
        out_specs=in_vmem(2),
        scratch_shapes=[VMEM((2, 2, tiles, rows, LANES), F32), DMA((2,))],
        compiler_params=limit,
        cost_estimate=pl.CostEstimate(
            flops=400_000_000, bytes_accessed=80_000_000, transcendentals=0
        ),
        name="pack_corners",
    )(low, high)
    top_corner = lax.ppermute(corner_down, "height", ring("height", 1))
    bottom_corner = lax.ppermute(corner_up, "height", ring("height", -1))

    edges = jnp.stack([slab > 0, slab < slabs - 1, band > 0, band < bands - 1]).astype(F32)
    each = tiles // slabs
    rest = tiles - FAR * each
    alpha_top = 2.0 / (cells * slabs)
    piece = shape(13, each, rows, LANES)
    order = [(slab + by) % slabs * each + k for by in SHIFTS for k in range(each)]
    *pieces, twice, slope = pl.pallas_call(
        functools.partial(render, alpha_top=alpha_top),
        out_shape=[piece] * FAR
        + [shape(rest, cells + 2, 16, LANES), shape(rest, cells + 1, rows, LANES)],
        in_specs=in_smem(6) + anywhere(7),
        out_specs=anywhere(FAR + 2),
        scratch_shapes=[
            VMEM((cells + 6, tiles, 24, LANES), F32),
            VMEM((cells + 4, tiles, 16, LANES), F32),
            VMEM((cells + 2, tiles, 16, LANES), F32),
            VMEM((cells + 1, tiles, rows, LANES), F32),
            VMEM((2, tiles, 2, rows, LANES), F32),
            VMEM((2, tiles, 2, rows, LANES), F32),
            VMEM((tiles, 2, rows, LANES), F32),
            VMEM((2, tiles, 3 * cells, LANES), F32),
            VMEM((2, tiles, rows, LANES), F32),
            VMEM((FAR, 13, each, rows, LANES), F32),
            DMA((7,)),
            DMA((2, rest)),
            DMA((FAR,)),
        ],
        compiler_params=limit,
        name="render",
    )(
        edges,
        jnp.stack(order).astype(jnp.int32),
        colour_coef,
        opacity_coef,
        light_dir,
        light_colour,
        field,
        low,
        high,
        top,
        bottom,
        top_corner,
        bottom_corner,
    )
    pieces += pl.pallas_call(
        functools.partial(render_rest, alpha_top=alpha_top),
        out_shape=[piece] * (slabs - FAR),
        in_specs=in_smem(4) + anywhere(2),
        out_specs=anywhere(slabs - FAR),
        scratch_shapes=[
            VMEM((rest, cells + 2, 16, LANES), F32),
            VMEM((rest, cells + 1, rows, LANES), F32),
            VMEM((slabs - FAR, 13, each, rows, LANES), F32),
            DMA((2, rest)),
            DMA((slabs - FAR,)),
        ],
        compiler_params=limit,
        cost_estimate=pl.CostEstimate(
            flops=50_000_000, bytes_accessed=20_000_000, transcendentals=1_000_000
        ),
        name="render_rest",
    )(colour_coef, opacity_coef, light_dir, light_colour, twice, slope)
    arrived = [
        lax.ppermute(value, "depth", ring("depth", by)) if by else value
        for value, by in zip(pieces, SHIFTS)
    ]
    own = pl.pallas_call(
        fold,
        out_shape=piece,
        in_specs=in_smem(1) + in_vmem(slabs),
        out_specs=pl.BlockSpec(memory_space=VMEM),
        compiler_params=limit,
        name="fold",
    )(slab[None], *arrived)
    known = {0: own}
    for by in (1, -1, 2, -2):
        known[by] = lax.ppermute(own, "depth", ring("depth", by))
    for held, by in ((2, 1), (-2, -1), (2, 2)):
        known[held + by] = lax.ppermute(known[held], "depth", ring("depth", by))
    image = pl.pallas_call(
        functools.partial(spread, list(known)),
        out_shape=shape(13, tiles, rows, LANES),
        in_specs=in_smem(1) + anywhere(slabs),
        out_specs=pl.BlockSpec(memory_space=VMEM),
        scratch_shapes=[DMA((slabs,))],
        compiler_params=limit,
        name="spread",
    )(slab[None], *known.values())
    return image.transpose(0, 2, 1, 3).reshape(13, rows, width)


def solution(mesh):
    placed = (P("depth", "height", None), P(), P(), P(), P())
    return jax.shard_map(
        per_device, mesh=mesh, in_specs=placed, out_specs=P(None, "height", None), check_vma=False
    )
```

```python
import functools

import jax
import jax.numpy as jnp
from jax import lax
from jax.experimental import pallas as pl
from jax.experimental.pallas import tpu as pltpu
from jax.sharding import PartitionSpec as P

VMEM = pltpu.VMEM
DMA = pltpu.SemaphoreType.DMA
F32 = jnp.float32
LANES = 128
ROWS = 8
BAND = 8
OWN = 4


def inverse_of(q):
    return pltpu.reciprocal(q, approx=True)


def flux(d):
    return d * inverse_of(d * d + 1.0)


def pack(vol_ref, down_ref, up_ref, first_ref, last_ref, held, down, up, in_sem, edge_sem, out_sem):
    cells, tiles = vol_ref.shape[0], vol_ref.shape[1]
    groups = cells // 8
    loads = [
        pltpu.make_async_copy(vol_ref.at[pl.ds(8 * g, 8)], held.at[pl.ds(8 * g, 8)], in_sem.at[g])
        for g in range(groups)
    ]
    edges = [
        pltpu.make_async_copy(held.at[pl.ds(0, 3)], first_ref, edge_sem.at[0]),
        pltpu.make_async_copy(held.at[pl.ds(cells - 3, 3)], last_ref, edge_sem.at[1]),
    ]
    for copy in loads:
        copy.start()
    stores = []
    for g in range(groups):
        loads[g].wait()
        if g == 0:
            edges[0].start()
        if g == groups - 1:
            edges[1].start()
        for k in range(8):
            z = 8 * g + k
            for tile in range(tiles):
                up[tile, 3 * z : 3 * z + 3, :] = held[z, tile, 0:3, :]
                down[tile, 3 * z : 3 * z + 3, :] = held[z, tile, 5:8, :]
        part = pl.ds(24 * g, 24)
        for i, (ref, out_ref) in enumerate(((down, down_ref), (up, up_ref))):
            copy = pltpu.make_async_copy(
                ref.at[:, part, :], out_ref.at[:, part, :], out_sem.at[2 * g + i]
            )
            copy.start()
            stores.append(copy)
    for copy in stores + edges:
        copy.wait()


CORNERS = ((0, 1, 0), (0, 0, 0), (0, 1, 1), (1, 0, 0), (1, 1, 0), (1, 0, 1))


def pack_corners(low_ref, high_ref, down_ref, up_ref, near, sem):
    tiles = low_ref.shape[1]
    copies = [
        pltpu.make_async_copy(low_ref.at[pl.ds(1, 2)], near.at[0], sem.at[0]),
        pltpu.make_async_copy(high_ref.at[pl.ds(0, 2)], near.at[1], sem.at[1]),
    ]
    for copy in copies:
        copy.start()
    for copy in copies:
        copy.wait()
    zero = jnp.zeros((2, LANES), F32)
    for tile in range(tiles):
        for slot, (side, plane, depth) in enumerate(CORNERS):
            up_ref[tile, slot : slot + 1, :] = near[side, plane, tile, depth : depth + 1, :]
            down_ref[tile, slot : slot + 1, :] = near[side, plane, tile, 7 - depth : 8 - depth, :]
        up_ref[tile, 6:8, :] = zero
        down_ref[tile, 6:8, :] = zero


def beside(src, base, z, parity, nexts):
    tiles = src.shape[1]
    lane = lax.broadcasted_iota(jnp.int32, (ROWS, LANES), 1)
    for part in range(2):
        rows = pl.ds(base + 8 * part, 8)
        turned = [pltpu.roll(src[z, tile, rows, :], LANES - 1, 1) for tile in range(tiles)]
        for tile in range(tiles):
            later = turned[tile + 1] if tile + 1 < tiles else 0.0
            nexts[parity, tile, part] = jnp.where(lane == LANES - 1, later, turned[tile])


def width_flux(src, base, z, parity, nexts, nets):
    tiles = src.shape[1]
    lane = lax.broadcasted_iota(jnp.int32, (ROWS, LANES), 1)
    for part in range(2):
        rows = pl.ds(base + 8 * part, 8)
        earlier = None
        for tile in range(tiles):
            u = src[z, tile, rows, :]
            across = flux(nexts[parity, tile, part] - u)
            turned = pltpu.roll(across, 1, 1)
            behind = flux(u) if earlier is None else earlier
            nets[parity, tile, part] = across - jnp.where(lane == 0, behind, turned)
            earlier = turned


def diffuse_plane(src, base, z, parity, nets, held, dst, out, rims):
    tiles = src.shape[1]
    sub = lax.broadcasted_iota(jnp.int32, (ROWS, LANES), 0)
    for tile in range(tiles):
        below = None
        for part in range(2):
            first = base + 8 * part
            u = src[z, tile, pl.ds(first, 8), :]
            if first + 9 <= src.shape[2]:
                above = src[z, tile, pl.ds(first + 1, 8), :]
            else:
                above = pltpu.roll(u, ROWS - 1, 0)
            up = flux(above - u)
            turned = pltpu.roll(up, 1, 0)
            along = up - (turned if part == 0 else jnp.where(sub == 0, below, turned))
            below = turned
            ahead = flux(src[z + 1, tile, pl.ds(first, 8), :] - u)
            total = (nets[parity, tile, part] + along) + (ahead - held[tile, part])
            held[tile, part] = ahead
            dst[out, tile, pl.ds(8 * part, 8), :] = (u + 0.12 * total) * rims[part]


def width_slope(field, z, slope):
    tiles = field.shape[1]
    lane = lax.broadcasted_iota(jnp.int32, (ROWS, LANES), 1)
    rows = pl.ds(OWN, 8)
    now = field[z, 0, rows, :]
    lowered, raised = pltpu.roll(now, LANES - 1, 1), pltpu.roll(now, 1, 1)
    earlier = 0.0
    for tile in range(tiles):
        if tile + 1 < tiles:
            later = field[z, tile + 1, rows, :]
            later_lowered, later_raised = pltpu.roll(later, LANES - 1, 1), pltpu.roll(later, 1, 1)
        else:
            later_lowered, later_raised = 0.0, None
        slope[z, tile] = jnp.where(lane == LANES - 1, later_lowered, lowered) - jnp.where(
            lane == 0, earlier, raised
        )
        earlier, lowered, raised = raised, later_lowered, later_raised


def diffuse(src, base, dst, planes, nexts, nets, held, rims, slope=None):
    for tile in range(src.shape[1]):
        for part in range(2):
            rows = pl.ds(base + 8 * part, 8)
            held[tile, part] = flux(src[1, tile, rows, :] - src[0, tile, rows, :])
    beside(src, base, 1, 1, nexts)
    width_flux(src, base, 1, 1, nexts, nets)
    beside(src, base, 2, 0, nexts)

    def pair(g, carry):
        for k in range(2):
            z = 2 * g + k + 1
            beside(src, base, jnp.minimum(z + 2, planes + 1), 1 - k, nexts)
            width_flux(src, base, z + 1, k, nexts, nets)
            diffuse_plane(src, base, z, 1 - k, nets, held, dst, z - 1, rims)
            if slope is not None:
                width_slope(dst, jnp.maximum(z - 3, 0), slope)
        return carry

    lax.fori_loop(0, planes // 2, pair, 0)
    if slope is not None:
        width_slope(dst, planes - 2, slope)


SHIFTS = (3, 5, 4, 2, 6, 1, 7, 0)
FAR = 3


def render(
    edge_ref,
    tile_ref,
    colour_ref,
    opacity_ref,
    dir_ref,
    light_ref,
    vol_ref,
    low_ref,
    high_ref,
    top_ref,
    bottom_ref,
    top_corner_ref,
    bottom_corner_ref,
    *refs,
    alpha_top,
):
    out_refs, twice_ref, slope_ref = refs[:FAR], refs[FAR], refs[FAR + 1]
    (field, once, twice, slope, nexts, nets, held, rows_in, corners_in, images) = refs[FAR + 2 : -3]
    sem, later_sem, out_sem = refs[-3:]
    cells, tiles = vol_ref.shape[0], vol_ref.shape[1]
    own = pl.ds(BAND, 8)
    copies = [
        pltpu.make_async_copy(low_ref, field.at[pl.ds(0, 3), :, own, :], sem.at[0]),
        pltpu.make_async_copy(high_ref, field.at[pl.ds(cells + 3, 3), :, own, :], sem.at[1]),
        pltpu.make_async_copy(top_corner_ref, corners_in.at[0], sem.at[2]),
        pltpu.make_async_copy(bottom_corner_ref, corners_in.at[1], sem.at[3]),
        pltpu.make_async_copy(top_ref, rows_in.at[0], sem.at[4]),
        pltpu.make_async_copy(bottom_ref, rows_in.at[1], sem.at[5]),
        pltpu.make_async_copy(vol_ref, field.at[pl.ds(3, cells), :, own, :], sem.at[6]),
    ]
    for copy in copies:
        copy.start()

    sub = lax.broadcasted_iota(jnp.int32, (ROWS, LANES), 0)
    keep_low, keep_high = edge_ref[0], edge_ref[1]
    keep_top, keep_bottom = edge_ref[2], edge_ref[3]
    rims = (
        jnp.where(sub < OWN, jnp.full((ROWS, LANES), keep_top), 1.0),
        jnp.where(sub >= OWN, jnp.full((ROWS, LANES), keep_bottom), 1.0),
    )

    zero = jnp.zeros((ROWS, LANES), F32)
    for k in range(3):
        for tile in range(tiles):
            for plane in (k, cells + 3 + k):
                field[plane, tile, 0:8, :] = zero
                field[plane, tile, 16:24, :] = zero
    for copy in copies[:4]:
        copy.wait()
    for k in range(3):
        for tile in range(tiles):
            field[k, tile, own, :] = field[k, tile, own, :] * keep_low
            field[cells + 3 + k, tile, own, :] = field[cells + 3 + k, tile, own, :] * keep_high
    for tile in range(tiles):
        for slot, (side, plane, away) in enumerate(CORNERS):
            at = (cells + 3 if side else 1) + plane
            keep = keep_high if side else keep_low
            field[at, tile, 7 - away : 8 - away, :] = corners_in[0, tile, slot : slot + 1, :] * (
                keep * keep_top
            )
            field[at, tile, 16 + away : 17 + away, :] = corners_in[
                1, tile, slot : slot + 1, :
            ] * (keep * keep_bottom)
    copies[4].wait()
    copies[5].wait()

    def rims_in(g, carry):
        at = pl.multiple_of(24 * g, 24)
        for tile in range(tiles):
            for k in range(8):
                field[8 * g + k + 3, tile, 5:8, :] = (
                    rows_in[0, tile, pl.ds(at + 3 * k, 3), :] * keep_top
                )
                field[8 * g + k + 3, tile, 16:19, :] = (
                    rows_in[1, tile, pl.ds(at + 3 * k, 3), :] * keep_bottom
                )
        return carry

    lax.fori_loop(0, cells // 8, rims_in, 0)
    copies[6].wait()

    diffuse(field, OWN, once, cells + 4, nexts, nets, held, rims)
    for k in range(2):
        for tile in range(tiles):
            for rows in (slice(0, 8), slice(8, 16)):
                once[k, tile, rows, :] = once[k, tile, rows, :] * keep_low
                once[cells + 2 + k, tile, rows, :] = once[cells + 2 + k, tile, rows, :] * keep_high
    diffuse(once, 0, twice, cells + 2, nexts, nets, held, rims, slope)
    own = pl.ds(OWN, 8)
    for tile in range(tiles):
        twice[0, tile, own, :] = twice[0, tile, own, :] * keep_low
        twice[cells + 1, tile, own, :] = twice[cells + 1, tile, own, :] * keep_high

    each = tiles // len(SHIFTS)
    ahead = FAR * each
    later = []
    for k in range(tiles - ahead):
        tile = tile_ref[ahead + k]
        later += [
            pltpu.make_async_copy(twice.at[:, tile], twice_ref.at[k], later_sem.at[0, k]),
            pltpu.make_async_copy(slope.at[:, tile], slope_ref.at[k], later_sem.at[1, k]),
        ]
    for copy in later:
        copy.start()

    def smooth(k, z, row):
        return twice[z, tile_ref[k], pl.ds(row, 8), :]

    def across(k, z):
        return slope[z, tile_ref[k]]

    coefs = (colour_ref, opacity_ref, dir_ref, light_ref)
    shade(coefs, cells, ahead, smooth, across, images, out_refs, out_sem, alpha_top)
    for copy in later:
        copy.wait()


def render_rest(colour_ref, opacity_ref, dir_ref, light_ref, twice_ref, slope_ref, *refs, alpha_top):
    out_refs, (twice, slope, images, sem, out_sem) = refs[:-5], refs[-5:]
    count, cells = slope.shape[0], slope.shape[1] - 1

    def load(k):
        return [
            pltpu.make_async_copy(twice_ref.at[k], twice.at[k], sem.at[0, k]),
            pltpu.make_async_copy(slope_ref.at[k], slope.at[k], sem.at[1, k]),
        ]

    for k in range(count):
        for copy in load(k):
            copy.start()

    def ready(k):
        for copy in load(k):
            copy.wait()

    def smooth(k, z, row):
        return twice[k, z, pl.ds(row, 8), :]

    def across(k, z):
        return slope[k, z]

    coefs = (colour_ref, opacity_ref, dir_ref, light_ref)
    shade(coefs, cells, count, smooth, across, images, out_refs, out_sem, alpha_top, ready)


def shade(
    coefs, cells, count, smooth, across, images, out_refs, out_sem, alpha_top, ready=None
):
    colour_ref, opacity_ref, dir_ref, light_ref = coefs
    each = images.shape[2]
    copies = [
        pltpu.make_async_copy(images.at[i], ref, out_sem.at[i]) for i, ref in enumerate(out_refs)
    ]
    zero = jnp.zeros((ROWS, LANES), F32)
    colour = [[colour_ref[c, j] for j in range(4)] for c in range(3)]
    opac = [opacity_ref[j] for j in range(4)]
    light = [[0.5 * dir_ref[l, d] for d in range(3)] for l in range(4)]

    def poly(c, v):
        return ((c[3] * v + c[2]) * v + c[1]) * v + c[0]

    def column(k, carry):
        if ready is not None:
            ready(k)

        def cell(z, state):
            through, sums, base_sums = state
            v = smooth(k, z + 1, OWN)
            g_z = smooth(k, z + 2, OWN) - smooth(k, z, OWN)
            g_h = smooth(k, z + 1, OWN + 1) - smooth(k, z + 1, OWN - 1)
            g_w = across(k, z + 1)
            inverse = lax.rsqrt(0.25 * (g_z * g_z + g_h * g_h + g_w * g_w) + 1.0)
            p = poly(opac, v)
            s = p * p
            opacity = (alpha_top * s) * inverse_of(1.0 + s)
            weight = through * opacity
            through = through - weight
            half = 0.5 * weight
            shaded = [half + half * jnp.tanh(poly(colour[c], v)) for c in range(3)]
            base_sums = [base_sums[c] + shaded[c] for c in range(3)]
            tilted = [inverse * shaded[c] for c in range(3)]
            new = []
            for l in range(4):
                facing = jnp.abs(g_z * light[l][0] + g_h * light[l][1] + g_w * light[l][2])
                for c in range(3):
                    new.append(sums[3 * l + c] + facing * tilted[c])
            return through, new, base_sums

        state = (jnp.ones((ROWS, LANES), F32), [zero] * 12, [zero] * 3)

        def group(g, state):
            for i in range(8):
                state = cell(g * 8 + i, state)
            return state

        through, sums, base_sums = lax.fori_loop(0, cells // 8, group, state)
        for l in range(4):
            for c in range(3):
                images[k // each, 3 * l + c, k % each] = light_ref[l, c] * (
                    0.2 * base_sums[c] + sums[3 * l + c]
                )
        images[k // each, 12, k % each] = 1.0 - through
        for i, copy in enumerate(copies):
            pl.when(k == (i + 1) * each - 1)(copy.start)
        return carry

    lax.fori_loop(0, count, column, 0)
    for copy in copies:
        copy.wait()


def fold(place_ref, *refs):
    pieces, out_ref = refs[:-1], refs[-1]
    slabs = len(pieces)
    channels, tiles = out_ref.shape[0], out_ref.shape[1]
    owner = [lax.rem(place_ref[0] - by + slabs, slabs) for by in SHIFTS]
    for tile in range(tiles):
        through = [1.0 - ref[12, tile] for ref in pieces]
        weight = []
        for i in range(slabs):
            product = None
            for j in range(slabs):
                if j != i:
                    factor = jnp.where(owner[j] < owner[i], through[j], 1.0)
                    product = factor if product is None else product * factor
            weight.append(product)
        for ch in range(channels):
            out_ref[ch, tile] = sum(weight[i] * pieces[i][ch, tile] for i in range(slabs))


def spread(offsets, place_ref, *refs):
    pieces, out_ref, sem = refs[:-2], refs[-2], refs[-1]
    count = len(pieces)
    tiles = out_ref.shape[1] // count
    copies = []
    for i, ref in enumerate(pieces):
        owner = lax.rem(place_ref[0] - offsets[i] + count, count)
        copies.append(
            pltpu.make_async_copy(ref, out_ref.at[:, pl.ds(owner * tiles, tiles)], sem.at[i])
        )
    for copy in copies:
        copy.start()
    for copy in copies:
        copy.wait()


def in_vmem(count):
    return [pl.BlockSpec(memory_space=VMEM)] * count


def in_smem(count):
    return [pl.BlockSpec(memory_space=pltpu.SMEM)] * count


def anywhere(count):
    return [pl.BlockSpec(memory_space=pl.ANY)] * count


def shape(*dims):
    return jax.ShapeDtypeStruct(dims, F32)


def ring(axis, by):
    count = lax.axis_size(axis)
    return [(i, (i + by) % count) for i in range(count)]


def per_device(volume, colour_coef, opacity_coef, light_dir, light_colour):
    slabs, bands = lax.axis_size("depth"), lax.axis_size("height")
    cells, rows, width = volume.shape
    tiles = width // LANES
    slab, band = lax.axis_index("depth"), lax.axis_index("height")
    limit = pltpu.CompilerParams(vmem_limit_bytes=(64 << 20) - (32 << 10))
    field = volume.reshape(cells, rows, tiles, LANES).transpose(0, 2, 1, 3)

    down, up, first, last = pl.pallas_call(
        pack,
        out_shape=[shape(tiles, 3 * cells, LANES)] * 2 + [shape(3, tiles, rows, LANES)] * 2,
        in_specs=anywhere(1),
        out_specs=anywhere(4),
        scratch_shapes=[
            VMEM((cells, tiles, rows, LANES), F32),
            VMEM((tiles, 3 * cells, LANES), F32),
            VMEM((tiles, 3 * cells, LANES), F32),
            DMA((cells // 8,)),
            DMA((2,)),
            DMA((cells // 4,)),
        ],
        compiler_params=limit,
        name="pack",
    )(field)
    low = lax.ppermute(last, "depth", ring("depth", 1))
    high = lax.ppermute(first, "depth", ring("depth", -1))
    top = lax.ppermute(down, "height", ring("height", 1))
    bottom = lax.ppermute(up, "height", ring("height", -1))
    corner_down, corner_up = pl.pallas_call(
        pack_corners,
        out_shape=[shape(tiles, rows, LANES)] * 2,
        in_specs=anywhere(2),
        out_specs=in_vmem(2),
        scratch_shapes=[VMEM((2, 2, tiles, rows, LANES), F32), DMA((2,))],
        compiler_params=limit,
        cost_estimate=pl.CostEstimate(
            flops=400_000_000, bytes_accessed=80_000_000, transcendentals=0
        ),
        name="pack_corners",
    )(low, high)
    top_corner = lax.ppermute(corner_down, "height", ring("height", 1))
    bottom_corner = lax.ppermute(corner_up, "height", ring("height", -1))

    edges = jnp.stack([slab > 0, slab < slabs - 1, band > 0, band < bands - 1]).astype(F32)
    each = tiles // slabs
    rest = tiles - FAR * each
    alpha_top = 2.0 / (cells * slabs)
    piece = shape(13, each, rows, LANES)
    order = [(slab + by) % slabs * each + k for by in SHIFTS for k in range(each)]
    *pieces, twice, slope = pl.pallas_call(
        functools.partial(render, alpha_top=alpha_top),
        out_shape=[piece] * FAR
        + [shape(rest, cells + 2, 16, LANES), shape(rest, cells + 1, rows, LANES)],
        in_specs=in_smem(6) + anywhere(7),
        out_specs=anywhere(FAR + 2),
        scratch_shapes=[
            VMEM((cells + 6, tiles, 24, LANES), F32),
            VMEM((cells + 4, tiles, 16, LANES), F32),
            VMEM((cells + 2, tiles, 16, LANES), F32),
            VMEM((cells + 1, tiles, rows, LANES), F32),
            VMEM((2, tiles, 2, rows, LANES), F32),
            VMEM((2, tiles, 2, rows, LANES), F32),
            VMEM((tiles, 2, rows, LANES), F32),
            VMEM((2, tiles, 3 * cells, LANES), F32),
            VMEM((2, tiles, rows, LANES), F32),
            VMEM((FAR, 13, each, rows, LANES), F32),
            DMA((7,)),
            DMA((2, rest)),
            DMA((FAR,)),
        ],
        compiler_params=limit,
        name="render",
    )(
        edges,
        jnp.stack(order).astype(jnp.int32),
        colour_coef,
        opacity_coef,
        light_dir,
        light_colour,
        field,
        low,
        high,
        top,
        bottom,
        top_corner,
        bottom_corner,
    )
    pieces += pl.pallas_call(
        functools.partial(render_rest, alpha_top=alpha_top),
        out_shape=[piece] * (slabs - FAR),
        in_specs=in_smem(4) + anywhere(2),
        out_specs=anywhere(slabs - FAR),
        scratch_shapes=[
            VMEM((rest, cells + 2, 16, LANES), F32),
            VMEM((rest, cells + 1, rows, LANES), F32),
            VMEM((slabs - FAR, 13, each, rows, LANES), F32),
            DMA((2, rest)),
            DMA((slabs - FAR,)),
        ],
        compiler_params=limit,
        cost_estimate=pl.CostEstimate(
            flops=50_000_000, bytes_accessed=20_000_000, transcendentals=1_000_000
        ),
        name="render_rest",
    )(colour_coef, opacity_coef, light_dir, light_colour, twice, slope)
    arrived = [
        lax.ppermute(value, "depth", ring("depth", by)) if by else value
        for value, by in zip(pieces, SHIFTS)
    ]
    own = pl.pallas_call(
        fold,
        out_shape=piece,
        in_specs=in_smem(1) + in_vmem(slabs),
        out_specs=pl.BlockSpec(memory_space=VMEM),
        compiler_params=limit,
        name="fold",
    )(slab[None], *arrived)
    known = {0: own}
    for by in (1, -1, 2, -2):
        known[by] = lax.ppermute(own, "depth", ring("depth", by))
    for held, by in ((2, 1), (-2, -1), (2, 2)):
        known[held + by] = lax.ppermute(known[held], "depth", ring("depth", by))
    image = pl.pallas_call(
        functools.partial(spread, list(known)),
        out_shape=shape(13, tiles, rows, LANES),
        in_specs=in_smem(1) + anywhere(slabs),
        out_specs=pl.BlockSpec(memory_space=VMEM),
        scratch_shapes=[DMA((slabs,))],
        compiler_params=limit,
        name="spread",
    )(slab[None], *known.values())
    return image.transpose(0, 2, 1, 3).reshape(13, rows, width)


def solution(mesh):
    placed = (P("depth", "height", None), P(), P(), P(), P())
    return jax.shard_map(
        per_device, mesh=mesh, in_specs=placed, out_specs=P(None, "height", None), check_vma=False
    )
```

```python
import functools

import jax
import jax.numpy as jnp
from jax import lax
from jax.experimental import pallas as pl
from jax.experimental.pallas import tpu as pltpu
from jax.sharding import PartitionSpec as P

VMEM = pltpu.VMEM
DMA = pltpu.SemaphoreType.DMA
F32 = jnp.float32
LANES = 128
ROWS = 8
BAND = 8
OWN = 4


def inverse_of(q):
    return pltpu.reciprocal(q, approx=True)


def flux(d):
    return d * inverse_of(d * d + 1.0)


def pack(vol_ref, down_ref, up_ref, first_ref, last_ref, held, down, up, in_sem, edge_sem, out_sem):
    cells, tiles = vol_ref.shape[0], vol_ref.shape[1]
    groups = cells // 8
    loads = [
        pltpu.make_async_copy(vol_ref.at[pl.ds(8 * g, 8)], held.at[pl.ds(8 * g, 8)], in_sem.at[g])
        for g in range(groups)
    ]
    edges = [
        pltpu.make_async_copy(held.at[pl.ds(0, 3)], first_ref, edge_sem.at[0]),
        pltpu.make_async_copy(held.at[pl.ds(cells - 3, 3)], last_ref, edge_sem.at[1]),
    ]
    for copy in loads:
        copy.start()
    stores = []
    for g in range(groups):
        loads[g].wait()
        if g == 0:
            edges[0].start()
        if g == groups - 1:
            edges[1].start()

        def rows_of(tile, carry):
            for z in range(8 * g, 8 * g + 8):
                up[tile, 3 * z : 3 * z + 3, :] = held[z, tile, 0:3, :]
                down[tile, 3 * z : 3 * z + 3, :] = held[z, tile, 5:8, :]
            return carry

        lax.fori_loop(0, tiles, rows_of, 0)
        part = pl.ds(24 * g, 24)
        for i, (ref, out_ref) in enumerate(((down, down_ref), (up, up_ref))):
            copy = pltpu.make_async_copy(
                ref.at[:, part, :], out_ref.at[:, part, :], out_sem.at[2 * g + i]
            )
            copy.start()
            stores.append(copy)
    for copy in stores + edges:
        copy.wait()


CORNERS = ((0, 1, 0), (0, 0, 0), (0, 1, 1), (1, 0, 0), (1, 1, 0), (1, 0, 1))


def pack_corners(low_ref, high_ref, down_ref, up_ref, near, sem):
    tiles = low_ref.shape[1]
    copies = [
        pltpu.make_async_copy(low_ref.at[pl.ds(1, 2)], near.at[0], sem.at[0]),
        pltpu.make_async_copy(high_ref.at[pl.ds(0, 2)], near.at[1], sem.at[1]),
    ]
    for copy in copies:
        copy.start()
    for copy in copies:
        copy.wait()
    zero = jnp.zeros((2, LANES), F32)
    for tile in range(tiles):
        for slot, (side, plane, depth) in enumerate(CORNERS):
            up_ref[tile, slot : slot + 1, :] = near[side, plane, tile, depth : depth + 1, :]
            down_ref[tile, slot : slot + 1, :] = near[side, plane, tile, 7 - depth : 8 - depth, :]
        up_ref[tile, 6:8, :] = zero
        down_ref[tile, 6:8, :] = zero


def beside(src, base, z, parity, nexts):
    tiles = src.shape[1]
    lane = lax.broadcasted_iota(jnp.int32, (ROWS, LANES), 1)
    for part in range(2):
        rows = pl.ds(base + 8 * part, 8)
        turned = [pltpu.roll(src[z, tile, rows, :], LANES - 1, 1) for tile in range(tiles)]
        for tile in range(tiles):
            later = turned[tile + 1] if tile + 1 < tiles else 0.0
            nexts[parity, tile, part] = jnp.where(lane == LANES - 1, later, turned[tile])


def width_flux(src, base, z, parity, nexts, nets):
    tiles = src.shape[1]
    lane = lax.broadcasted_iota(jnp.int32, (ROWS, LANES), 1)
    for part in range(2):
        rows = pl.ds(base + 8 * part, 8)
        earlier = None
        for tile in range(tiles):
            u = src[z, tile, rows, :]
            across = flux(nexts[parity, tile, part] - u)
            turned = pltpu.roll(across, 1, 1)
            behind = flux(u) if earlier is None else earlier
            nets[parity, tile, part] = across - jnp.where(lane == 0, behind, turned)
            earlier = turned


def diffuse_plane(src, base, z, parity, nets, held, dst, out, rims):
    tiles = src.shape[1]
    sub = lax.broadcasted_iota(jnp.int32, (ROWS, LANES), 0)
    for tile in range(tiles):
        below = None
        for part in range(2):
            first = base + 8 * part
            u = src[z, tile, pl.ds(first, 8), :]
            if first + 9 <= src.shape[2]:
                above = src[z, tile, pl.ds(first + 1, 8), :]
            else:
                above = pltpu.roll(u, ROWS - 1, 0)
            up = flux(above - u)
            turned = pltpu.roll(up, 1, 0)
            along = up - (turned if part == 0 else jnp.where(sub == 0, below, turned))
            below = turned
            ahead = flux(src[z + 1, tile, pl.ds(first, 8), :] - u)
            total = (nets[parity, tile, part] + along) + (ahead - held[tile, part])
            held[tile, part] = ahead
            dst[out, tile, pl.ds(8 * part, 8), :] = (u + 0.12 * total) * rims[part]


def width_slope(field, z, slope):
    tiles = field.shape[1]
    lane = lax.broadcasted_iota(jnp.int32, (ROWS, LANES), 1)
    rows = pl.ds(OWN, 8)
    now = field[z, 0, rows, :]
    lowered, raised = pltpu.roll(now, LANES - 1, 1), pltpu.roll(now, 1, 1)
    earlier = 0.0
    for tile in range(tiles):
        if tile + 1 < tiles:
            later = field[z, tile + 1, rows, :]
            later_lowered, later_raised = pltpu.roll(later, LANES - 1, 1), pltpu.roll(later, 1, 1)
        else:
            later_lowered, later_raised = 0.0, None
        slope[z, tile] = jnp.where(lane == LANES - 1, later_lowered, lowered) - jnp.where(
            lane == 0, earlier, raised
        )
        earlier, lowered, raised = raised, later_lowered, later_raised


def diffuse(src, base, dst, planes, nexts, nets, held, rims, slope=None):
    for tile in range(src.shape[1]):
        for part in range(2):
            rows = pl.ds(base + 8 * part, 8)
            held[tile, part] = flux(src[1, tile, rows, :] - src[0, tile, rows, :])
    beside(src, base, 1, 1, nexts)
    width_flux(src, base, 1, 1, nexts, nets)
    beside(src, base, 2, 0, nexts)

    def pair(g, carry):
        for k in range(2):
            z = 2 * g + k + 1
            beside(src, base, jnp.minimum(z + 2, planes + 1), 1 - k, nexts)
            width_flux(src, base, z + 1, k, nexts, nets)
            diffuse_plane(src, base, z, 1 - k, nets, held, dst, z - 1, rims)
            if slope is not None:
                width_slope(dst, jnp.maximum(z - 3, 0), slope)
        return carry

    lax.fori_loop(0, planes // 2, pair, 0)
    if slope is not None:
        width_slope(dst, planes - 2, slope)


SHIFTS = (4, 3, 5, 2, 6, 1, 7, 0)
FAR = 3


def render(
    edge_ref,
    tile_ref,
    colour_ref,
    opacity_ref,
    dir_ref,
    light_ref,
    vol_ref,
    low_ref,
    high_ref,
    top_ref,
    bottom_ref,
    top_corner_ref,
    bottom_corner_ref,
    *refs,
    alpha_top,
):
    out_refs, twice_ref, slope_ref = refs[:FAR], refs[FAR], refs[FAR + 1]
    (field, once, twice, slope, nexts, nets, held, rows_in, corners_in, images) = refs[FAR + 2 : -3]
    sem, later_sem, out_sem = refs[-3:]
    cells, tiles = vol_ref.shape[0], vol_ref.shape[1]
    own = pl.ds(BAND, 8)
    copies = [
        pltpu.make_async_copy(low_ref, field.at[pl.ds(0, 3), :, own, :], sem.at[0]),
        pltpu.make_async_copy(high_ref, field.at[pl.ds(cells + 3, 3), :, own, :], sem.at[1]),
        pltpu.make_async_copy(top_corner_ref, corners_in.at[0], sem.at[2]),
        pltpu.make_async_copy(bottom_corner_ref, corners_in.at[1], sem.at[3]),
        pltpu.make_async_copy(top_ref, rows_in.at[0], sem.at[4]),
        pltpu.make_async_copy(bottom_ref, rows_in.at[1], sem.at[5]),
        pltpu.make_async_copy(vol_ref, field.at[pl.ds(3, cells), :, own, :], sem.at[6]),
    ]
    for copy in copies:
        copy.start()

    sub = lax.broadcasted_iota(jnp.int32, (ROWS, LANES), 0)
    keep_low, keep_high = edge_ref[0], edge_ref[1]
    keep_top, keep_bottom = edge_ref[2], edge_ref[3]
    rims = (
        jnp.where(sub < OWN, jnp.full((ROWS, LANES), keep_top), 1.0),
        jnp.where(sub >= OWN, jnp.full((ROWS, LANES), keep_bottom), 1.0),
    )

    zero = jnp.zeros((ROWS, LANES), F32)
    for k in range(3):
        for tile in range(tiles):
            for plane in (k, cells + 3 + k):
                field[plane, tile, 0:8, :] = zero
                field[plane, tile, 16:24, :] = zero
    for copy in copies[:4]:
        copy.wait()
    for k in range(3):
        for tile in range(tiles):
            field[k, tile, own, :] = field[k, tile, own, :] * keep_low
            field[cells + 3 + k, tile, own, :] = field[cells + 3 + k, tile, own, :] * keep_high
    for tile in range(tiles):
        for slot, (side, plane, away) in enumerate(CORNERS):
            at = (cells + 3 if side else 1) + plane
            keep = keep_high if side else keep_low
            field[at, tile, 7 - away : 8 - away, :] = corners_in[0, tile, slot : slot + 1, :] * (
                keep * keep_top
            )
            field[at, tile, 16 + away : 17 + away, :] = corners_in[
                1, tile, slot : slot + 1, :
            ] * (keep * keep_bottom)
    copies[4].wait()
    copies[5].wait()

    def rims_in(g, carry):
        at = pl.multiple_of(24 * g, 24)
        for tile in range(tiles):
            for k in range(8):
                field[8 * g + k + 3, tile, 5:8, :] = (
                    rows_in[0, tile, pl.ds(at + 3 * k, 3), :] * keep_top
                )
                field[8 * g + k + 3, tile, 16:19, :] = (
                    rows_in[1, tile, pl.ds(at + 3 * k, 3), :] * keep_bottom
                )
        return carry

    lax.fori_loop(0, cells // 8, rims_in, 0)
    copies[6].wait()

    diffuse(field, OWN, once, cells + 4, nexts, nets, held, rims)
    for k in range(2):
        for tile in range(tiles):
            for rows in (slice(0, 8), slice(8, 16)):
                once[k, tile, rows, :] = once[k, tile, rows, :] * keep_low
                once[cells + 2 + k, tile, rows, :] = once[cells + 2 + k, tile, rows, :] * keep_high
    diffuse(once, 0, twice, cells + 2, nexts, nets, held, rims, slope)
    own = pl.ds(OWN, 8)
    for tile in range(tiles):
        twice[0, tile, own, :] = twice[0, tile, own, :] * keep_low
        twice[cells + 1, tile, own, :] = twice[cells + 1, tile, own, :] * keep_high

    each = tiles // len(SHIFTS)
    ahead = FAR * each
    later = []
    for k in range(tiles - ahead):
        tile = tile_ref[ahead + k]
        later += [
            pltpu.make_async_copy(twice.at[:, tile], twice_ref.at[k], later_sem.at[0, k]),
            pltpu.make_async_copy(slope.at[:, tile], slope_ref.at[k], later_sem.at[1, k]),
        ]
    for copy in later:
        copy.start()

    def smooth(k, z, row):
        return twice[z, tile_ref[k], pl.ds(row, 8), :]

    def across(k, z):
        return slope[z, tile_ref[k]]

    coefs = (colour_ref, opacity_ref, dir_ref, light_ref)
    shade(coefs, cells, ahead, smooth, across, images, out_refs, out_sem, alpha_top)
    for copy in later:
        copy.wait()


def render_rest(colour_ref, opacity_ref, dir_ref, light_ref, twice_ref, slope_ref, *refs, alpha_top):
    out_refs, (twice, slope, images, sem, out_sem) = refs[:-5], refs[-5:]
    count, cells = slope.shape[0], slope.shape[1] - 1

    def load(k):
        return [
            pltpu.make_async_copy(twice_ref.at[k], twice.at[k], sem.at[0, k]),
            pltpu.make_async_copy(slope_ref.at[k], slope.at[k], sem.at[1, k]),
        ]

    for k in range(count):
        for copy in load(k):
            copy.start()

    def ready(k):
        for copy in load(k):
            copy.wait()

    def smooth(k, z, row):
        return twice[k, z, pl.ds(row, 8), :]

    def across(k, z):
        return slope[k, z]

    coefs = (colour_ref, opacity_ref, dir_ref, light_ref)
    shade(coefs, cells, count, smooth, across, images, out_refs, out_sem, alpha_top, ready)


def shade(
    coefs, cells, count, smooth, across, images, out_refs, out_sem, alpha_top, ready=None
):
    colour_ref, opacity_ref, dir_ref, light_ref = coefs
    each = images.shape[2]
    copies = [
        pltpu.make_async_copy(images.at[i], ref, out_sem.at[i]) for i, ref in enumerate(out_refs)
    ]
    zero = jnp.zeros((ROWS, LANES), F32)
    colour = [[colour_ref[c, j] for j in range(4)] for c in range(3)]
    opac = [opacity_ref[j] for j in range(4)]
    light = [[0.5 * dir_ref[l, d] for d in range(3)] for l in range(4)]

    def poly(c, v):
        return ((c[3] * v + c[2]) * v + c[1]) * v + c[0]

    def column(k, carry):
        if ready is not None:
            ready(k)

        def cell(z, state):
            through, sums, base_sums = state
            v = smooth(k, z + 1, OWN)
            g_z = smooth(k, z + 2, OWN) - smooth(k, z, OWN)
            g_h = smooth(k, z + 1, OWN + 1) - smooth(k, z + 1, OWN - 1)
            g_w = across(k, z + 1)
            inverse = lax.rsqrt(0.25 * (g_z * g_z + g_h * g_h + g_w * g_w) + 1.0)
            p = poly(opac, v)
            s = p * p
            opacity = (alpha_top * s) * inverse_of(1.0 + s)
            weight = through * opacity
            through = through - weight
            half = 0.5 * weight
            shaded = [half + half * jnp.tanh(poly(colour[c], v)) for c in range(3)]
            base_sums = [base_sums[c] + shaded[c] for c in range(3)]
            tilted = [inverse * shaded[c] for c in range(3)]
            new = []
            for l in range(4):
                facing = jnp.abs(g_z * light[l][0] + g_h * light[l][1] + g_w * light[l][2])
                for c in range(3):
                    new.append(sums[3 * l + c] + facing * tilted[c])
            return through, new, base_sums

        state = (jnp.ones((ROWS, LANES), F32), [zero] * 12, [zero] * 3)

        def group(g, state):
            for i in range(8):
                state = cell(g * 8 + i, state)
            return state

        through, sums, base_sums = lax.fori_loop(0, cells // 8, group, state)
        for l in range(4):
            for c in range(3):
                images[k // each, 3 * l + c, k % each] = light_ref[l, c] * (
                    0.2 * base_sums[c] + sums[3 * l + c]
                )
        images[k // each, 12, k % each] = 1.0 - through
        for i, copy in enumerate(copies):
            pl.when(k == (i + 1) * each - 1)(copy.start)
        return carry

    lax.fori_loop(0, count, column, 0)
    for copy in copies:
        copy.wait()


def fold(place_ref, *refs):
    pieces, out_ref = refs[:-1], refs[-1]
    slabs = len(pieces)
    channels, tiles = out_ref.shape[0], out_ref.shape[1]
    owner = [lax.rem(place_ref[0] - by + slabs, slabs) for by in SHIFTS]
    for tile in range(tiles):
        through = [1.0 - ref[12, tile] for ref in pieces]
        weight = []
        for i in range(slabs):
            product = None
            for j in range(slabs):
                if j != i:
                    factor = jnp.where(owner[j] < owner[i], through[j], 1.0)
                    product = factor if product is None else product * factor
            weight.append(product)
        for ch in range(channels):
            out_ref[ch, tile] = sum(weight[i] * pieces[i][ch, tile] for i in range(slabs))


def spread(offsets, place_ref, *refs):
    pieces, out_ref, sem = refs[:-2], refs[-2], refs[-1]
    count = len(pieces)
    tiles = out_ref.shape[1] // count
    copies = []
    for i, ref in enumerate(pieces):
        owner = lax.rem(place_ref[0] - offsets[i] + count, count)
        copies.append(
            pltpu.make_async_copy(ref, out_ref.at[:, pl.ds(owner * tiles, tiles)], sem.at[i])
        )
    for copy in copies:
        copy.start()
    for copy in copies:
        copy.wait()


def in_vmem(count):
    return [pl.BlockSpec(memory_space=VMEM)] * count


def in_smem(count):
    return [pl.BlockSpec(memory_space=pltpu.SMEM)] * count


def anywhere(count):
    return [pl.BlockSpec(memory_space=pl.ANY)] * count


def shape(*dims):
    return jax.ShapeDtypeStruct(dims, F32)


def ring(axis, by):
    count = lax.axis_size(axis)
    return [(i, (i + by) % count) for i in range(count)]


def per_device(volume, colour_coef, opacity_coef, light_dir, light_colour):
    slabs, bands = lax.axis_size("depth"), lax.axis_size("height")
    cells, rows, width = volume.shape
    tiles = width // LANES
    slab, band = lax.axis_index("depth"), lax.axis_index("height")
    limit = pltpu.CompilerParams(vmem_limit_bytes=(64 << 20) - (32 << 10))
    field = volume.reshape(cells, rows, tiles, LANES).transpose(0, 2, 1, 3)

    down, up, first, last = pl.pallas_call(
        pack,
        out_shape=[shape(tiles, 3 * cells, LANES)] * 2 + [shape(3, tiles, rows, LANES)] * 2,
        in_specs=anywhere(1),
        out_specs=anywhere(4),
        scratch_shapes=[
            VMEM((cells, tiles, rows, LANES), F32),
            VMEM((tiles, 3 * cells, LANES), F32),
            VMEM((tiles, 3 * cells, LANES), F32),
            DMA((cells // 8,)),
            DMA((2,)),
            DMA((cells // 4,)),
        ],
        compiler_params=limit,
        name="pack",
    )(field)
    low = lax.ppermute(last, "depth", ring("depth", 1))
    high = lax.ppermute(first, "depth", ring("depth", -1))
    top = lax.ppermute(down, "height", ring("height", 1))
    bottom = lax.ppermute(up, "height", ring("height", -1))
    corner_down, corner_up = pl.pallas_call(
        pack_corners,
        out_shape=[shape(tiles, rows, LANES)] * 2,
        in_specs=anywhere(2),
        out_specs=in_vmem(2),
        scratch_shapes=[VMEM((2, 2, tiles, rows, LANES), F32), DMA((2,))],
        compiler_params=limit,
        cost_estimate=pl.CostEstimate(
            flops=400_000_000, bytes_accessed=80_000_000, transcendentals=0
        ),
        name="pack_corners",
    )(low, high)
    top_corner = lax.ppermute(corner_down, "height", ring("height", 1))
    bottom_corner = lax.ppermute(corner_up, "height", ring("height", -1))

    edges = jnp.stack([slab > 0, slab < slabs - 1, band > 0, band < bands - 1]).astype(F32)
    each = tiles // slabs
    rest = tiles - FAR * each
    alpha_top = 2.0 / (cells * slabs)
    piece = shape(13, each, rows, LANES)
    order = [(slab + by) % slabs * each + k for by in SHIFTS for k in range(each)]
    *pieces, twice, slope = pl.pallas_call(
        functools.partial(render, alpha_top=alpha_top),
        out_shape=[piece] * FAR
        + [shape(rest, cells + 2, 16, LANES), shape(rest, cells + 1, rows, LANES)],
        in_specs=in_smem(6) + anywhere(7),
        out_specs=anywhere(FAR + 2),
        scratch_shapes=[
            VMEM((cells + 6, tiles, 24, LANES), F32),
            VMEM((cells + 4, tiles, 16, LANES), F32),
            VMEM((cells + 2, tiles, 16, LANES), F32),
            VMEM((cells + 1, tiles, rows, LANES), F32),
            VMEM((2, tiles, 2, rows, LANES), F32),
            VMEM((2, tiles, 2, rows, LANES), F32),
            VMEM((tiles, 2, rows, LANES), F32),
            VMEM((2, tiles, 3 * cells, LANES), F32),
            VMEM((2, tiles, rows, LANES), F32),
            VMEM((FAR, 13, each, rows, LANES), F32),
            DMA((7,)),
            DMA((2, rest)),
            DMA((FAR,)),
        ],
        compiler_params=limit,
        name="render",
    )(
        edges,
        jnp.stack(order).astype(jnp.int32),
        colour_coef,
        opacity_coef,
        light_dir,
        light_colour,
        field,
        low,
        high,
        top,
        bottom,
        top_corner,
        bottom_corner,
    )
    pieces += pl.pallas_call(
        functools.partial(render_rest, alpha_top=alpha_top),
        out_shape=[piece] * (slabs - FAR),
        in_specs=in_smem(4) + anywhere(2),
        out_specs=anywhere(slabs - FAR),
        scratch_shapes=[
            VMEM((rest, cells + 2, 16, LANES), F32),
            VMEM((rest, cells + 1, rows, LANES), F32),
            VMEM((slabs - FAR, 13, each, rows, LANES), F32),
            DMA((2, rest)),
            DMA((slabs - FAR,)),
        ],
        compiler_params=limit,
        cost_estimate=pl.CostEstimate(
            flops=50_000_000, bytes_accessed=20_000_000, transcendentals=1_000_000
        ),
        name="render_rest",
    )(colour_coef, opacity_coef, light_dir, light_colour, twice, slope)
    arrived = [
        lax.ppermute(value, "depth", ring("depth", by)) if by else value
        for value, by in zip(pieces, SHIFTS)
    ]
    own = pl.pallas_call(
        fold,
        out_shape=piece,
        in_specs=in_smem(1) + in_vmem(slabs),
        out_specs=pl.BlockSpec(memory_space=VMEM),
        compiler_params=limit,
        name="fold",
    )(slab[None], *arrived)
    known = {0: own}
    for by in (1, -1, 2, -2):
        known[by] = lax.ppermute(own, "depth", ring("depth", by))
    for held, by in ((2, 1), (-2, -1), (2, 2)):
        known[held + by] = lax.ppermute(known[held], "depth", ring("depth", by))
    image = pl.pallas_call(
        functools.partial(spread, list(known)),
        out_shape=shape(13, tiles, rows, LANES),
        in_specs=in_smem(1) + anywhere(slabs),
        out_specs=pl.BlockSpec(memory_space=VMEM),
        scratch_shapes=[DMA((slabs,))],
        compiler_params=limit,
        name="spread",
    )(slab[None], *known.values())
    return image.transpose(0, 2, 1, 3).reshape(13, rows, width)


def solution(mesh):
    placed = (P("depth", "height", None), P(), P(), P(), P())
    return jax.shard_map(
        per_device, mesh=mesh, in_specs=placed, out_specs=P(None, "height", None), check_vma=False
    )
```

```python
import functools

import jax
import jax.numpy as jnp
from jax import lax
from jax.experimental import pallas as pl
from jax.experimental.pallas import tpu as pltpu
from jax.sharding import PartitionSpec as P

VMEM = pltpu.VMEM
DMA = pltpu.SemaphoreType.DMA
F32 = jnp.float32
LANES = 128
ROWS = 8
BAND = 8
OWN = 4


def inverse_of(q):
    return pltpu.reciprocal(q, approx=True)


def flux(d):
    return d * inverse_of(d * d + 1.0)


def pack(vol_ref, down_ref, up_ref, first_ref, last_ref, held, down, up, in_sem, edge_sem, out_sem):
    cells, tiles = vol_ref.shape[0], vol_ref.shape[1]
    groups = cells // 8
    loads = [
        pltpu.make_async_copy(vol_ref.at[pl.ds(8 * g, 8)], held.at[pl.ds(8 * g, 8)], in_sem.at[g])
        for g in range(groups)
    ]
    edges = [
        pltpu.make_async_copy(held.at[pl.ds(0, 3)], first_ref, edge_sem.at[0]),
        pltpu.make_async_copy(held.at[pl.ds(cells - 3, 3)], last_ref, edge_sem.at[1]),
    ]
    for copy in loads:
        copy.start()
    stores = []
    for g in range(groups):
        loads[g].wait()
        if g == 0:
            edges[0].start()
        if g == groups - 1:
            edges[1].start()
        for k in range(8):
            z = 8 * g + k
            for tile in range(tiles):
                up[tile, 3 * z : 3 * z + 3, :] = held[z, tile, 0:3, :]
                down[tile, 3 * z : 3 * z + 3, :] = held[z, tile, 5:8, :]
        part = pl.ds(24 * g, 24)
        for i, (ref, out_ref) in enumerate(((down, down_ref), (up, up_ref))):
            copy = pltpu.make_async_copy(
                ref.at[:, part, :], out_ref.at[:, part, :], out_sem.at[2 * g + i]
            )
            copy.start()
            stores.append(copy)
    for copy in stores + edges:
        copy.wait()


CORNERS = ((0, 1, 0), (0, 0, 0), (0, 1, 1), (1, 0, 0), (1, 1, 0), (1, 0, 1))


def pack_corners(low_ref, high_ref, down_ref, up_ref, near, sem):
    tiles = low_ref.shape[1]
    copies = [
        pltpu.make_async_copy(low_ref.at[pl.ds(1, 2)], near.at[0], sem.at[0]),
        pltpu.make_async_copy(high_ref.at[pl.ds(0, 2)], near.at[1], sem.at[1]),
    ]
    for copy in copies:
        copy.start()
    for copy in copies:
        copy.wait()
    zero = jnp.zeros((2, LANES), F32)
    for tile in range(tiles):
        for slot, (side, plane, depth) in enumerate(CORNERS):
            up_ref[tile, slot : slot + 1, :] = near[side, plane, tile, depth : depth + 1, :]
            down_ref[tile, slot : slot + 1, :] = near[side, plane, tile, 7 - depth : 8 - depth, :]
        up_ref[tile, 6:8, :] = zero
        down_ref[tile, 6:8, :] = zero


def beside(src, base, z, parity, nexts):
    tiles = src.shape[1]
    lane = lax.broadcasted_iota(jnp.int32, (ROWS, LANES), 1)
    for part in range(2):
        rows = pl.ds(base + 8 * part, 8)
        turned = [pltpu.roll(src[z, tile, rows, :], LANES - 1, 1) for tile in range(tiles)]
        for tile in range(tiles):
            later = turned[tile + 1] if tile + 1 < tiles else 0.0
            nexts[parity, tile, part] = jnp.where(lane == LANES - 1, later, turned[tile])


def width_flux(src, base, z, parity, nexts, nets):
    tiles = src.shape[1]
    lane = lax.broadcasted_iota(jnp.int32, (ROWS, LANES), 1)
    for part in range(2):
        rows = pl.ds(base + 8 * part, 8)
        earlier = None
        for tile in range(tiles):
            u = src[z, tile, rows, :]
            across = flux(nexts[parity, tile, part] - u)
            turned = pltpu.roll(across, 1, 1)
            behind = flux(u) if earlier is None else earlier
            nets[parity, tile, part] = across - jnp.where(lane == 0, behind, turned)
            earlier = turned


def diffuse_plane(src, base, z, parity, nets, held, dst, out, rims):
    tiles = src.shape[1]
    sub = lax.broadcasted_iota(jnp.int32, (ROWS, LANES), 0)
    for tile in range(tiles):
        below = None
        for part in range(2):
            first = base + 8 * part
            u = src[z, tile, pl.ds(first, 8), :]
            if first + 9 <= src.shape[2]:
                above = src[z, tile, pl.ds(first + 1, 8), :]
            else:
                above = pltpu.roll(u, ROWS - 1, 0)
            up = flux(above - u)
            turned = pltpu.roll(up, 1, 0)
            along = up - (turned if part == 0 else jnp.where(sub == 0, below, turned))
            below = turned
            ahead = flux(src[z + 1, tile, pl.ds(first, 8), :] - u)
            total = (nets[parity, tile, part] + along) + (ahead - held[tile, part])
            held[tile, part] = ahead
            dst[out, tile, pl.ds(8 * part, 8), :] = (u + 0.12 * total) * rims[part]


def width_slope(field, z, slope):
    tiles = field.shape[1]
    lane = lax.broadcasted_iota(jnp.int32, (ROWS, LANES), 1)
    rows = pl.ds(OWN, 8)
    now = field[z, 0, rows, :]
    lowered, raised = pltpu.roll(now, LANES - 1, 1), pltpu.roll(now, 1, 1)
    earlier = 0.0
    for tile in range(tiles):
        if tile + 1 < tiles:
            later = field[z, tile + 1, rows, :]
            later_lowered, later_raised = pltpu.roll(later, LANES - 1, 1), pltpu.roll(later, 1, 1)
        else:
            later_lowered, later_raised = 0.0, None
        slope[z, tile] = jnp.where(lane == LANES - 1, later_lowered, lowered) - jnp.where(
            lane == 0, earlier, raised
        )
        earlier, lowered, raised = raised, later_lowered, later_raised


def diffuse(src, base, dst, planes, nexts, nets, held, rims, slope=None):
    for tile in range(src.shape[1]):
        for part in range(2):
            rows = pl.ds(base + 8 * part, 8)
            held[tile, part] = flux(src[1, tile, rows, :] - src[0, tile, rows, :])
    beside(src, base, 1, 1, nexts)
    width_flux(src, base, 1, 1, nexts, nets)
    beside(src, base, 2, 0, nexts)

    def pair(g, carry):
        for k in range(2):
            z = 2 * g + k + 1
            beside(src, base, jnp.minimum(z + 2, planes + 1), 1 - k, nexts)
            width_flux(src, base, z + 1, k, nexts, nets)
            diffuse_plane(src, base, z, 1 - k, nets, held, dst, z - 1, rims)
            if slope is not None:
                width_slope(dst, jnp.maximum(z - 3, 0), slope)
        return carry

    lax.fori_loop(0, planes // 2, pair, 0)
    if slope is not None:
        width_slope(dst, planes - 2, slope)


SHIFTS = (4, 3, 5, 2, 6, 1, 7, 0)
FAR = 4


def render(
    edge_ref,
    tile_ref,
    colour_ref,
    opacity_ref,
    dir_ref,
    light_ref,
    vol_ref,
    low_ref,
    high_ref,
    top_ref,
    bottom_ref,
    top_corner_ref,
    bottom_corner_ref,
    *refs,
    alpha_top,
):
    out_refs, twice_ref, slope_ref = refs[:FAR], refs[FAR], refs[FAR + 1]
    (field, once, twice, slope, nexts, nets, held, rows_in, corners_in, images) = refs[FAR + 2 : -3]
    sem, later_sem, out_sem = refs[-3:]
    cells, tiles = vol_ref.shape[0], vol_ref.shape[1]
    own = pl.ds(BAND, 8)
    copies = [
        pltpu.make_async_copy(low_ref, field.at[pl.ds(0, 3), :, own, :], sem.at[0]),
        pltpu.make_async_copy(high_ref, field.at[pl.ds(cells + 3, 3), :, own, :], sem.at[1]),
        pltpu.make_async_copy(top_corner_ref, corners_in.at[0], sem.at[2]),
        pltpu.make_async_copy(bottom_corner_ref, corners_in.at[1], sem.at[3]),
        pltpu.make_async_copy(top_ref, rows_in.at[0], sem.at[4]),
        pltpu.make_async_copy(bottom_ref, rows_in.at[1], sem.at[5]),
        pltpu.make_async_copy(vol_ref, field.at[pl.ds(3, cells), :, own, :], sem.at[6]),
    ]
    for copy in copies:
        copy.start()

    sub = lax.broadcasted_iota(jnp.int32, (ROWS, LANES), 0)
    keep_low, keep_high = edge_ref[0], edge_ref[1]
    keep_top, keep_bottom = edge_ref[2], edge_ref[3]
    rims = (
        jnp.where(sub < OWN, jnp.full((ROWS, LANES), keep_top), 1.0),
        jnp.where(sub >= OWN, jnp.full((ROWS, LANES), keep_bottom), 1.0),
    )

    zero = jnp.zeros((ROWS, LANES), F32)
    for k in range(3):
        for tile in range(tiles):
            for plane in (k, cells + 3 + k):
                field[plane, tile, 0:8, :] = zero
                field[plane, tile, 16:24, :] = zero
    for copy in copies[:4]:
        copy.wait()
    for k in range(3):
        for tile in range(tiles):
            field[k, tile, own, :] = field[k, tile, own, :] * keep_low
            field[cells + 3 + k, tile, own, :] = field[cells + 3 + k, tile, own, :] * keep_high
    for tile in range(tiles):
        for slot, (side, plane, away) in enumerate(CORNERS):
            at = (cells + 3 if side else 1) + plane
            keep = keep_high if side else keep_low
            field[at, tile, 7 - away : 8 - away, :] = corners_in[0, tile, slot : slot + 1, :] * (
                keep * keep_top
            )
            field[at, tile, 16 + away : 17 + away, :] = corners_in[
                1, tile, slot : slot + 1, :
            ] * (keep * keep_bottom)
    copies[4].wait()
    copies[5].wait()

    def rims_in(g, carry):
        at = pl.multiple_of(24 * g, 24)
        for tile in range(tiles):
            for k in range(8):
                field[8 * g + k + 3, tile, 5:8, :] = (
                    rows_in[0, tile, pl.ds(at + 3 * k, 3), :] * keep_top
                )
                field[8 * g + k + 3, tile, 16:19, :] = (
                    rows_in[1, tile, pl.ds(at + 3 * k, 3), :] * keep_bottom
                )
        return carry

    lax.fori_loop(0, cells // 8, rims_in, 0)
    copies[6].wait()

    diffuse(field, OWN, once, cells + 4, nexts, nets, held, rims)
    for k in range(2):
        for tile in range(tiles):
            for rows in (slice(0, 8), slice(8, 16)):
                once[k, tile, rows, :] = once[k, tile, rows, :] * keep_low
                once[cells + 2 + k, tile, rows, :] = once[cells + 2 + k, tile, rows, :] * keep_high
    diffuse(once, 0, twice, cells + 2, nexts, nets, held, rims, slope)
    own = pl.ds(OWN, 8)
    for tile in range(tiles):
        twice[0, tile, own, :] = twice[0, tile, own, :] * keep_low
        twice[cells + 1, tile, own, :] = twice[cells + 1, tile, own, :] * keep_high

    each = tiles // len(SHIFTS)
    ahead = FAR * each
    later = []
    for k in range(tiles - ahead):
        tile = tile_ref[ahead + k]
        later += [
            pltpu.make_async_copy(twice.at[:, tile], twice_ref.at[k], later_sem.at[0, k]),
            pltpu.make_async_copy(slope.at[:, tile], slope_ref.at[k], later_sem.at[1, k]),
        ]
    for copy in later:
        copy.start()

    def smooth(k, z, row):
        return twice[z, tile_ref[k], pl.ds(row, 8), :]

    def across(k, z):
        return slope[z, tile_ref[k]]

    coefs = (colour_ref, opacity_ref, dir_ref, light_ref)
    shade(coefs, cells, ahead, smooth, across, images, out_refs, out_sem, alpha_top)
    for copy in later:
        copy.wait()


def render_rest(colour_ref, opacity_ref, dir_ref, light_ref, twice_ref, slope_ref, *refs, alpha_top):
    out_refs, (twice, slope, images, sem, out_sem) = refs[:-5], refs[-5:]
    count, cells = slope.shape[0], slope.shape[1] - 1

    def load(k):
        return [
            pltpu.make_async_copy(twice_ref.at[k], twice.at[k], sem.at[0, k]),
            pltpu.make_async_copy(slope_ref.at[k], slope.at[k], sem.at[1, k]),
        ]

    for k in range(count):
        for copy in load(k):
            copy.start()

    def ready(k):
        for copy in load(k):
            copy.wait()

    def smooth(k, z, row):
        return twice[k, z, pl.ds(row, 8), :]

    def across(k, z):
        return slope[k, z]

    coefs = (colour_ref, opacity_ref, dir_ref, light_ref)
    shade(coefs, cells, count, smooth, across, images, out_refs, out_sem, alpha_top, ready)


def shade(
    coefs, cells, count, smooth, across, images, out_refs, out_sem, alpha_top, ready=None
):
    colour_ref, opacity_ref, dir_ref, light_ref = coefs
    each = images.shape[2]
    copies = [
        pltpu.make_async_copy(images.at[i], ref, out_sem.at[i]) for i, ref in enumerate(out_refs)
    ]
    zero = jnp.zeros((ROWS, LANES), F32)
    colour = [[colour_ref[c, j] for j in range(4)] for c in range(3)]
    opac = [opacity_ref[j] for j in range(4)]
    light = [[0.5 * dir_ref[l, d] for d in range(3)] for l in range(4)]

    def poly(c, v):
        return ((c[3] * v + c[2]) * v + c[1]) * v + c[0]

    def column(k, carry):
        if ready is not None:
            ready(k)

        def cell(z, state):
            through, sums, base_sums = state
            v = smooth(k, z + 1, OWN)
            g_z = smooth(k, z + 2, OWN) - smooth(k, z, OWN)
            g_h = smooth(k, z + 1, OWN + 1) - smooth(k, z + 1, OWN - 1)
            g_w = across(k, z + 1)
            inverse = lax.rsqrt(0.25 * (g_z * g_z + g_h * g_h + g_w * g_w) + 1.0)
            p = poly(opac, v)
            s = p * p
            opacity = (alpha_top * s) * inverse_of(1.0 + s)
            weight = through * opacity
            through = through - weight
            half = 0.5 * weight
            shaded = [half + half * jnp.tanh(poly(colour[c], v)) for c in range(3)]
            base_sums = [base_sums[c] + shaded[c] for c in range(3)]
            tilted = [inverse * shaded[c] for c in range(3)]
            new = []
            for l in range(4):
                facing = jnp.abs(g_z * light[l][0] + g_h * light[l][1] + g_w * light[l][2])
                for c in range(3):
                    new.append(sums[3 * l + c] + facing * tilted[c])
            return through, new, base_sums

        state = (jnp.ones((ROWS, LANES), F32), [zero] * 12, [zero] * 3)

        def group(g, state):
            for i in range(8):
                state = cell(g * 8 + i, state)
            return state

        through, sums, base_sums = lax.fori_loop(0, cells // 8, group, state)
        for l in range(4):
            for c in range(3):
                images[k // each, 3 * l + c, k % each] = light_ref[l, c] * (
                    0.2 * base_sums[c] + sums[3 * l + c]
                )
        images[k // each, 12, k % each] = 1.0 - through
        for i, copy in enumerate(copies):
            pl.when(k == (i + 1) * each - 1)(copy.start)
        return carry

    lax.fori_loop(0, count, column, 0)
    for copy in copies:
        copy.wait()


def fold(place_ref, *refs):
    pieces, out_ref = refs[:-1], refs[-1]
    slabs = len(pieces)
    channels, tiles = out_ref.shape[0], out_ref.shape[1]
    owner = [lax.rem(place_ref[0] - by + slabs, slabs) for by in SHIFTS]
    for tile in range(tiles):
        through = [1.0 - ref[12, tile] for ref in pieces]
        weight = []
        for i in range(slabs):
            product = None
            for j in range(slabs):
                if j != i:
                    factor = jnp.where(owner[j] < owner[i], through[j], 1.0)
                    product = factor if product is None else product * factor
            weight.append(product)
        for ch in range(channels):
            out_ref[ch, tile] = sum(weight[i] * pieces[i][ch, tile] for i in range(slabs))


def spread(offsets, place_ref, *refs):
    pieces, out_ref, sem = refs[:-2], refs[-2], refs[-1]
    count = len(pieces)
    tiles = out_ref.shape[1] // count
    copies = []
    for i, ref in enumerate(pieces):
        owner = lax.rem(place_ref[0] - offsets[i] + count, count)
        copies.append(
            pltpu.make_async_copy(ref, out_ref.at[:, pl.ds(owner * tiles, tiles)], sem.at[i])
        )
    for copy in copies:
        copy.start()
    for copy in copies:
        copy.wait()


def in_vmem(count):
    return [pl.BlockSpec(memory_space=VMEM)] * count


def in_smem(count):
    return [pl.BlockSpec(memory_space=pltpu.SMEM)] * count


def anywhere(count):
    return [pl.BlockSpec(memory_space=pl.ANY)] * count


def shape(*dims):
    return jax.ShapeDtypeStruct(dims, F32)


def ring(axis, by):
    count = lax.axis_size(axis)
    return [(i, (i + by) % count) for i in range(count)]


def per_device(volume, colour_coef, opacity_coef, light_dir, light_colour):
    slabs, bands = lax.axis_size("depth"), lax.axis_size("height")
    cells, rows, width = volume.shape
    tiles = width // LANES
    slab, band = lax.axis_index("depth"), lax.axis_index("height")
    limit = pltpu.CompilerParams(vmem_limit_bytes=(64 << 20) - (32 << 10))
    field = volume.reshape(cells, rows, tiles, LANES).transpose(0, 2, 1, 3)

    down, up, first, last = pl.pallas_call(
        pack,
        out_shape=[shape(tiles, 3 * cells, LANES)] * 2 + [shape(3, tiles, rows, LANES)] * 2,
        in_specs=anywhere(1),
        out_specs=anywhere(4),
        scratch_shapes=[
            VMEM((cells, tiles, rows, LANES), F32),
            VMEM((tiles, 3 * cells, LANES), F32),
            VMEM((tiles, 3 * cells, LANES), F32),
            DMA((cells // 8,)),
            DMA((2,)),
            DMA((cells // 4,)),
        ],
        compiler_params=limit,
        name="pack",
    )(field)
    low = lax.ppermute(last, "depth", ring("depth", 1))
    high = lax.ppermute(first, "depth", ring("depth", -1))
    top = lax.ppermute(down, "height", ring("height", 1))
    bottom = lax.ppermute(up, "height", ring("height", -1))
    corner_down, corner_up = pl.pallas_call(
        pack_corners,
        out_shape=[shape(tiles, rows, LANES)] * 2,
        in_specs=anywhere(2),
        out_specs=in_vmem(2),
        scratch_shapes=[VMEM((2, 2, tiles, rows, LANES), F32), DMA((2,))],
        compiler_params=limit,
        cost_estimate=pl.CostEstimate(
            flops=400_000_000, bytes_accessed=80_000_000, transcendentals=0
        ),
        name="pack_corners",
    )(low, high)
    top_corner = lax.ppermute(corner_down, "height", ring("height", 1))
    bottom_corner = lax.ppermute(corner_up, "height", ring("height", -1))

    edges = jnp.stack([slab > 0, slab < slabs - 1, band > 0, band < bands - 1]).astype(F32)
    each = tiles // slabs
    rest = tiles - FAR * each
    alpha_top = 2.0 / (cells * slabs)
    piece = shape(13, each, rows, LANES)
    order = [(slab + by) % slabs * each + k for by in SHIFTS for k in range(each)]
    *pieces, twice, slope = pl.pallas_call(
        functools.partial(render, alpha_top=alpha_top),
        out_shape=[piece] * FAR
        + [shape(rest, cells + 2, 16, LANES), shape(rest, cells + 1, rows, LANES)],
        in_specs=in_smem(6) + anywhere(7),
        out_specs=anywhere(FAR + 2),
        scratch_shapes=[
            VMEM((cells + 6, tiles, 24, LANES), F32),
            VMEM((cells + 4, tiles, 16, LANES), F32),
            VMEM((cells + 2, tiles, 16, LANES), F32),
            VMEM((cells + 1, tiles, rows, LANES), F32),
            VMEM((2, tiles, 2, rows, LANES), F32),
            VMEM((2, tiles, 2, rows, LANES), F32),
            VMEM((tiles, 2, rows, LANES), F32),
            VMEM((2, tiles, 3 * cells, LANES), F32),
            VMEM((2, tiles, rows, LANES), F32),
            VMEM((FAR, 13, each, rows, LANES), F32),
            DMA((7,)),
            DMA((2, rest)),
            DMA((FAR,)),
        ],
        compiler_params=limit,
        name="render",
    )(
        edges,
        jnp.stack(order).astype(jnp.int32),
        colour_coef,
        opacity_coef,
        light_dir,
        light_colour,
        field,
        low,
        high,
        top,
        bottom,
        top_corner,
        bottom_corner,
    )
    pieces += pl.pallas_call(
        functools.partial(render_rest, alpha_top=alpha_top),
        out_shape=[piece] * (slabs - FAR),
        in_specs=in_smem(4) + anywhere(2),
        out_specs=anywhere(slabs - FAR),
        scratch_shapes=[
            VMEM((rest, cells + 2, 16, LANES), F32),
            VMEM((rest, cells + 1, rows, LANES), F32),
            VMEM((slabs - FAR, 13, each, rows, LANES), F32),
            DMA((2, rest)),
            DMA((slabs - FAR,)),
        ],
        compiler_params=limit,
        cost_estimate=pl.CostEstimate(
            flops=50_000_000, bytes_accessed=20_000_000, transcendentals=1_000_000
        ),
        name="render_rest",
    )(colour_coef, opacity_coef, light_dir, light_colour, twice, slope)
    arrived = [
        lax.ppermute(value, "depth", ring("depth", by)) if by else value
        for value, by in zip(pieces, SHIFTS)
    ]
    own = pl.pallas_call(
        fold,
        out_shape=piece,
        in_specs=in_smem(1) + in_vmem(slabs),
        out_specs=pl.BlockSpec(memory_space=VMEM),
        compiler_params=limit,
        name="fold",
    )(slab[None], *arrived)
    known = {0: own}
    for by in (1, -1, 2, -2):
        known[by] = lax.ppermute(own, "depth", ring("depth", by))
    for held, by in ((2, 1), (-2, -1), (2, 2)):
        known[held + by] = lax.ppermute(known[held], "depth", ring("depth", by))
    image = pl.pallas_call(
        functools.partial(spread, list(known)),
        out_shape=shape(13, tiles, rows, LANES),
        in_specs=in_smem(1) + anywhere(slabs),
        out_specs=pl.BlockSpec(memory_space=VMEM),
        scratch_shapes=[DMA((slabs,))],
        compiler_params=limit,
        name="spread",
    )(slab[None], *known.values())
    return image.transpose(0, 2, 1, 3).reshape(13, rows, width)


def solution(mesh):
    placed = (P("depth", "height", None), P(), P(), P(), P())
    return jax.shard_map(
        per_device, mesh=mesh, in_specs=placed, out_specs=P(None, "height", None), check_vma=False
    )
```

```python
import functools

import jax
import jax.numpy as jnp
from jax import lax
from jax.experimental import pallas as pl
from jax.experimental.pallas import tpu as pltpu
from jax.sharding import PartitionSpec as P

VMEM = pltpu.VMEM
DMA = pltpu.SemaphoreType.DMA
F32 = jnp.float32
LANES = 128
ROWS = 8
BAND = 8
OWN = 4


def inverse_of(q):
    return pltpu.reciprocal(q, approx=True)


def flux(d):
    return d * inverse_of(d * d + 1.0)


def pack(vol_ref, down_ref, up_ref, first_ref, last_ref, held, down, up, in_sem, edge_sem, out_sem):
    cells, tiles = vol_ref.shape[0], vol_ref.shape[1]
    groups = cells // 8
    loads = [
        pltpu.make_async_copy(vol_ref.at[pl.ds(8 * g, 8)], held.at[pl.ds(8 * g, 8)], in_sem.at[g])
        for g in range(groups)
    ]
    edges = [
        pltpu.make_async_copy(held.at[pl.ds(0, 3)], first_ref, edge_sem.at[0]),
        pltpu.make_async_copy(held.at[pl.ds(cells - 3, 3)], last_ref, edge_sem.at[1]),
    ]
    for copy in loads:
        copy.start()
    stores = []
    for g in range(groups):
        loads[g].wait()
        if g == 0:
            edges[0].start()
        if g == groups - 1:
            edges[1].start()
        for k in range(8):
            z = 8 * g + k
            for tile in range(tiles):
                up[tile, 3 * z : 3 * z + 3, :] = held[z, tile, 0:3, :]
                down[tile, 3 * z : 3 * z + 3, :] = held[z, tile, 5:8, :]
        part = pl.ds(24 * g, 24)
        for i, (ref, out_ref) in enumerate(((down, down_ref), (up, up_ref))):
            copy = pltpu.make_async_copy(
                ref.at[:, part, :], out_ref.at[:, part, :], out_sem.at[2 * g + i]
            )
            copy.start()
            stores.append(copy)
    for copy in stores + edges:
        copy.wait()


CORNERS = ((0, 1, 0), (0, 0, 0), (0, 1, 1), (1, 0, 0), (1, 1, 0), (1, 0, 1))


def pack_corners(low_ref, high_ref, down_ref, up_ref, near, sem):
    tiles = low_ref.shape[1]
    copies = [
        pltpu.make_async_copy(low_ref.at[pl.ds(1, 2)], near.at[0], sem.at[0]),
        pltpu.make_async_copy(high_ref.at[pl.ds(0, 2)], near.at[1], sem.at[1]),
    ]
    for copy in copies:
        copy.start()
    for copy in copies:
        copy.wait()
    zero = jnp.zeros((2, LANES), F32)
    for tile in range(tiles):
        for slot, (side, plane, depth) in enumerate(CORNERS):
            up_ref[tile, slot : slot + 1, :] = near[side, plane, tile, depth : depth + 1, :]
            down_ref[tile, slot : slot + 1, :] = near[side, plane, tile, 7 - depth : 8 - depth, :]
        up_ref[tile, 6:8, :] = zero
        down_ref[tile, 6:8, :] = zero


def beside(src, base, z, parity, nexts):
    tiles = src.shape[1]
    lane = lax.broadcasted_iota(jnp.int32, (ROWS, LANES), 1)
    for part in range(2):
        rows = pl.ds(base + 8 * part, 8)
        turned = [pltpu.roll(src[z, tile, rows, :], LANES - 1, 1) for tile in range(tiles)]
        for tile in range(tiles):
            later = turned[tile + 1] if tile + 1 < tiles else 0.0
            nexts[parity, tile, part] = jnp.where(lane == LANES - 1, later, turned[tile])


def width_flux(src, base, z, parity, nexts, nets):
    tiles = src.shape[1]
    lane = lax.broadcasted_iota(jnp.int32, (ROWS, LANES), 1)
    for part in range(2):
        rows = pl.ds(base + 8 * part, 8)
        earlier = None
        for tile in range(tiles):
            u = src[z, tile, rows, :]
            across = flux(nexts[parity, tile, part] - u)
            turned = pltpu.roll(across, 1, 1)
            behind = flux(u) if earlier is None else earlier
            nets[parity, tile, part] = across - jnp.where(lane == 0, behind, turned)
            earlier = turned


def diffuse_plane(src, base, z, parity, nets, held, dst, out, rims):
    tiles = src.shape[1]
    sub = lax.broadcasted_iota(jnp.int32, (ROWS, LANES), 0)
    for tile in range(tiles):
        below = None
        for part in range(2):
            first = base + 8 * part
            u = src[z, tile, pl.ds(first, 8), :]
            if first + 9 <= src.shape[2]:
                above = src[z, tile, pl.ds(first + 1, 8), :]
            else:
                above = pltpu.roll(u, ROWS - 1, 0)
            up = flux(above - u)
            turned = pltpu.roll(up, 1, 0)
            along = up - (turned if part == 0 else jnp.where(sub == 0, below, turned))
            below = turned
            ahead = flux(src[z + 1, tile, pl.ds(first, 8), :] - u)
            total = (nets[parity, tile, part] + along) + (ahead - held[tile, part])
            held[tile, part] = ahead
            dst[out, tile, pl.ds(8 * part, 8), :] = (u + 0.12 * total) * rims[part]


def width_slope(field, z, slope):
    tiles = field.shape[1]
    lane = lax.broadcasted_iota(jnp.int32, (ROWS, LANES), 1)
    rows = pl.ds(OWN, 8)
    now = field[z, 0, rows, :]
    lowered, raised = pltpu.roll(now, LANES - 1, 1), pltpu.roll(now, 1, 1)
    earlier = 0.0
    for tile in range(tiles):
        if tile + 1 < tiles:
            later = field[z, tile + 1, rows, :]
            later_lowered, later_raised = pltpu.roll(later, LANES - 1, 1), pltpu.roll(later, 1, 1)
        else:
            later_lowered, later_raised = 0.0, None
        slope[z, tile] = jnp.where(lane == LANES - 1, later_lowered, lowered) - jnp.where(
            lane == 0, earlier, raised
        )
        earlier, lowered, raised = raised, later_lowered, later_raised


def diffuse(src, base, dst, planes, nexts, nets, held, rims, slope=None):
    for tile in range(src.shape[1]):
        for part in range(2):
            rows = pl.ds(base + 8 * part, 8)
            held[tile, part] = flux(src[1, tile, rows, :] - src[0, tile, rows, :])
    beside(src, base, 1, 1, nexts)
    width_flux(src, base, 1, 1, nexts, nets)
    beside(src, base, 2, 0, nexts)

    def pair(g, carry):
        for k in range(2):
            z = 2 * g + k + 1
            beside(src, base, jnp.minimum(z + 2, planes + 1), 1 - k, nexts)
            width_flux(src, base, z + 1, k, nexts, nets)
            diffuse_plane(src, base, z, 1 - k, nets, held, dst, z - 1, rims)
            if slope is not None:
                width_slope(dst, jnp.maximum(z - 3, 0), slope)
        return carry

    lax.fori_loop(0, planes // 2, pair, 0)
    if slope is not None:
        width_slope(dst, planes - 2, slope)


SHIFTS = (4, 3, 5, 2, 6, 1, 7, 0)
FAR = 5


def render(
    edge_ref,
    tile_ref,
    colour_ref,
    opacity_ref,
    dir_ref,
    light_ref,
    vol_ref,
    low_ref,
    high_ref,
    top_ref,
    bottom_ref,
    top_corner_ref,
    bottom_corner_ref,
    *refs,
    alpha_top,
):
    out_refs, twice_ref, slope_ref = refs[:FAR], refs[FAR], refs[FAR + 1]
    (field, once, twice, slope, nexts, nets, held, rows_in, corners_in, images) = refs[FAR + 2 : -3]
    sem, later_sem, out_sem = refs[-3:]
    cells, tiles = vol_ref.shape[0], vol_ref.shape[1]
    own = pl.ds(BAND, 8)
    copies = [
        pltpu.make_async_copy(low_ref, field.at[pl.ds(0, 3), :, own, :], sem.at[0]),
        pltpu.make_async_copy(high_ref, field.at[pl.ds(cells + 3, 3), :, own, :], sem.at[1]),
        pltpu.make_async_copy(top_corner_ref, corners_in.at[0], sem.at[2]),
        pltpu.make_async_copy(bottom_corner_ref, corners_in.at[1], sem.at[3]),
        pltpu.make_async_copy(top_ref, rows_in.at[0], sem.at[4]),
        pltpu.make_async_copy(bottom_ref, rows_in.at[1], sem.at[5]),
        pltpu.make_async_copy(vol_ref, field.at[pl.ds(3, cells), :, own, :], sem.at[6]),
    ]
    for copy in copies:
        copy.start()

    sub = lax.broadcasted_iota(jnp.int32, (ROWS, LANES), 0)
    keep_low, keep_high = edge_ref[0], edge_ref[1]
    keep_top, keep_bottom = edge_ref[2], edge_ref[3]
    rims = (
        jnp.where(sub < OWN, jnp.full((ROWS, LANES), keep_top), 1.0),
        jnp.where(sub >= OWN, jnp.full((ROWS, LANES), keep_bottom), 1.0),
    )

    zero = jnp.zeros((ROWS, LANES), F32)
    for k in range(3):
        for tile in range(tiles):
            for plane in (k, cells + 3 + k):
                field[plane, tile, 0:8, :] = zero
                field[plane, tile, 16:24, :] = zero
    for copy in copies[:4]:
        copy.wait()
    for k in range(3):
        for tile in range(tiles):
            field[k, tile, own, :] = field[k, tile, own, :] * keep_low
            field[cells + 3 + k, tile, own, :] = field[cells + 3 + k, tile, own, :] * keep_high
    for tile in range(tiles):
        for slot, (side, plane, away) in enumerate(CORNERS):
            at = (cells + 3 if side else 1) + plane
            keep = keep_high if side else keep_low
            field[at, tile, 7 - away : 8 - away, :] = corners_in[0, tile, slot : slot + 1, :] * (
                keep * keep_top
            )
            field[at, tile, 16 + away : 17 + away, :] = corners_in[
                1, tile, slot : slot + 1, :
            ] * (keep * keep_bottom)
    copies[4].wait()
    copies[5].wait()

    def rims_in(g, carry):
        at = pl.multiple_of(24 * g, 24)
        for tile in range(tiles):
            for k in range(8):
                field[8 * g + k + 3, tile, 5:8, :] = (
                    rows_in[0, tile, pl.ds(at + 3 * k, 3), :] * keep_top
                )
                field[8 * g + k + 3, tile, 16:19, :] = (
                    rows_in[1, tile, pl.ds(at + 3 * k, 3), :] * keep_bottom
                )
        return carry

    lax.fori_loop(0, cells // 8, rims_in, 0)
    copies[6].wait()

    diffuse(field, OWN, once, cells + 4, nexts, nets, held, rims)
    for k in range(2):
        for tile in range(tiles):
            for rows in (slice(0, 8), slice(8, 16)):
                once[k, tile, rows, :] = once[k, tile, rows, :] * keep_low
                once[cells + 2 + k, tile, rows, :] = once[cells + 2 + k, tile, rows, :] * keep_high
    diffuse(once, 0, twice, cells + 2, nexts, nets, held, rims, slope)
    own = pl.ds(OWN, 8)
    for tile in range(tiles):
        twice[0, tile, own, :] = twice[0, tile, own, :] * keep_low
        twice[cells + 1, tile, own, :] = twice[cells + 1, tile, own, :] * keep_high

    each = tiles // len(SHIFTS)
    ahead = FAR * each
    later = []
    for k in range(tiles - ahead):
        tile = tile_ref[ahead + k]
        later += [
            pltpu.make_async_copy(twice.at[:, tile], twice_ref.at[k], later_sem.at[0, k]),
            pltpu.make_async_copy(slope.at[:, tile], slope_ref.at[k], later_sem.at[1, k]),
        ]
    for copy in later:
        copy.start()

    def smooth(k, z, row):
        return twice[z, tile_ref[k], pl.ds(row, 8), :]

    def across(k, z):
        return slope[z, tile_ref[k]]

    coefs = (colour_ref, opacity_ref, dir_ref, light_ref)
    shade(coefs, cells, ahead, smooth, across, images, out_refs, out_sem, alpha_top)
    for copy in later:
        copy.wait()


def render_rest(colour_ref, opacity_ref, dir_ref, light_ref, twice_ref, slope_ref, *refs, alpha_top):
    out_refs, (twice, slope, images, sem, out_sem) = refs[:-5], refs[-5:]
    count, cells = slope.shape[0], slope.shape[1] - 1

    def load(k):
        return [
            pltpu.make_async_copy(twice_ref.at[k], twice.at[k], sem.at[0, k]),
            pltpu.make_async_copy(slope_ref.at[k], slope.at[k], sem.at[1, k]),
        ]

    for k in range(count):
        for copy in load(k):
            copy.start()

    def ready(k):
        for copy in load(k):
            copy.wait()

    def smooth(k, z, row):
        return twice[k, z, pl.ds(row, 8), :]

    def across(k, z):
        return slope[k, z]

    coefs = (colour_ref, opacity_ref, dir_ref, light_ref)
    shade(coefs, cells, count, smooth, across, images, out_refs, out_sem, alpha_top, ready)


def shade(
    coefs, cells, count, smooth, across, images, out_refs, out_sem, alpha_top, ready=None
):
    colour_ref, opacity_ref, dir_ref, light_ref = coefs
    each = images.shape[2]
    copies = [
        pltpu.make_async_copy(images.at[i], ref, out_sem.at[i]) for i, ref in enumerate(out_refs)
    ]
    zero = jnp.zeros((ROWS, LANES), F32)
    colour = [[colour_ref[c, j] for j in range(4)] for c in range(3)]
    opac = [opacity_ref[j] for j in range(4)]
    light = [[0.5 * dir_ref[l, d] for d in range(3)] for l in range(4)]

    def poly(c, v):
        return ((c[3] * v + c[2]) * v + c[1]) * v + c[0]

    def column(k, carry):
        if ready is not None:
            ready(k)

        def cell(z, state):
            through, sums, base_sums = state
            v = smooth(k, z + 1, OWN)
            g_z = smooth(k, z + 2, OWN) - smooth(k, z, OWN)
            g_h = smooth(k, z + 1, OWN + 1) - smooth(k, z + 1, OWN - 1)
            g_w = across(k, z + 1)
            inverse = lax.rsqrt(0.25 * (g_z * g_z + g_h * g_h + g_w * g_w) + 1.0)
            p = poly(opac, v)
            s = p * p
            opacity = (alpha_top * s) * inverse_of(1.0 + s)
            weight = through * opacity
            through = through - weight
            half = 0.5 * weight
            shaded = [half + half * jnp.tanh(poly(colour[c], v)) for c in range(3)]
            base_sums = [base_sums[c] + shaded[c] for c in range(3)]
            tilted = [inverse * shaded[c] for c in range(3)]
            new = []
            for l in range(4):
                facing = jnp.abs(g_z * light[l][0] + g_h * light[l][1] + g_w * light[l][2])
                for c in range(3):
                    new.append(sums[3 * l + c] + facing * tilted[c])
            return through, new, base_sums

        state = (jnp.ones((ROWS, LANES), F32), [zero] * 12, [zero] * 3)

        def group(g, state):
            for i in range(8):
                state = cell(g * 8 + i, state)
            return state

        through, sums, base_sums = lax.fori_loop(0, cells // 8, group, state)
        for l in range(4):
            for c in range(3):
                images[k // each, 3 * l + c, k % each] = light_ref[l, c] * (
                    0.2 * base_sums[c] + sums[3 * l + c]
                )
        images[k // each, 12, k % each] = 1.0 - through
        for i, copy in enumerate(copies):
            pl.when(k == (i + 1) * each - 1)(copy.start)
        return carry

    lax.fori_loop(0, count, column, 0)
    for copy in copies:
        copy.wait()


def fold(place_ref, *refs):
    pieces, out_ref = refs[:-1], refs[-1]
    slabs = len(pieces)
    channels, tiles = out_ref.shape[0], out_ref.shape[1]
    owner = [lax.rem(place_ref[0] - by + slabs, slabs) for by in SHIFTS]
    for tile in range(tiles):
        through = [1.0 - ref[12, tile] for ref in pieces]
        weight = []
        for i in range(slabs):
            product = None
            for j in range(slabs):
                if j != i:
                    factor = jnp.where(owner[j] < owner[i], through[j], 1.0)
                    product = factor if product is None else product * factor
            weight.append(product)
        for ch in range(channels):
            out_ref[ch, tile] = sum(weight[i] * pieces[i][ch, tile] for i in range(slabs))


def spread(offsets, place_ref, *refs):
    pieces, out_ref, sem = refs[:-2], refs[-2], refs[-1]
    count = len(pieces)
    tiles = out_ref.shape[1] // count
    copies = []
    for i, ref in enumerate(pieces):
        owner = lax.rem(place_ref[0] - offsets[i] + count, count)
        copies.append(
            pltpu.make_async_copy(ref, out_ref.at[:, pl.ds(owner * tiles, tiles)], sem.at[i])
        )
    for copy in copies:
        copy.start()
    for copy in copies:
        copy.wait()


def in_vmem(count):
    return [pl.BlockSpec(memory_space=VMEM)] * count


def in_smem(count):
    return [pl.BlockSpec(memory_space=pltpu.SMEM)] * count


def anywhere(count):
    return [pl.BlockSpec(memory_space=pl.ANY)] * count


def shape(*dims):
    return jax.ShapeDtypeStruct(dims, F32)


def ring(axis, by):
    count = lax.axis_size(axis)
    return [(i, (i + by) % count) for i in range(count)]


def per_device(volume, colour_coef, opacity_coef, light_dir, light_colour):
    slabs, bands = lax.axis_size("depth"), lax.axis_size("height")
    cells, rows, width = volume.shape
    tiles = width // LANES
    slab, band = lax.axis_index("depth"), lax.axis_index("height")
    limit = pltpu.CompilerParams(vmem_limit_bytes=(64 << 20) - (32 << 10))
    field = volume.reshape(cells, rows, tiles, LANES).transpose(0, 2, 1, 3)

    down, up, first, last = pl.pallas_call(
        pack,
        out_shape=[shape(tiles, 3 * cells, LANES)] * 2 + [shape(3, tiles, rows, LANES)] * 2,
        in_specs=anywhere(1),
        out_specs=anywhere(4),
        scratch_shapes=[
            VMEM((cells, tiles, rows, LANES), F32),
            VMEM((tiles, 3 * cells, LANES), F32),
            VMEM((tiles, 3 * cells, LANES), F32),
            DMA((cells // 8,)),
            DMA((2,)),
            DMA((cells // 4,)),
        ],
        compiler_params=limit,
        name="pack",
    )(field)
    low = lax.ppermute(last, "depth", ring("depth", 1))
    high = lax.ppermute(first, "depth", ring("depth", -1))
    top = lax.ppermute(down, "height", ring("height", 1))
    bottom = lax.ppermute(up, "height", ring("height", -1))
    corner_down, corner_up = pl.pallas_call(
        pack_corners,
        out_shape=[shape(tiles, rows, LANES)] * 2,
        in_specs=anywhere(2),
        out_specs=in_vmem(2),
        scratch_shapes=[VMEM((2, 2, tiles, rows, LANES), F32), DMA((2,))],
        compiler_params=limit,
        cost_estimate=pl.CostEstimate(
            flops=400_000_000, bytes_accessed=80_000_000, transcendentals=0
        ),
        name="pack_corners",
    )(low, high)
    top_corner = lax.ppermute(corner_down, "height", ring("height", 1))
    bottom_corner = lax.ppermute(corner_up, "height", ring("height", -1))

    edges = jnp.stack([slab > 0, slab < slabs - 1, band > 0, band < bands - 1]).astype(F32)
    each = tiles // slabs
    rest = tiles - FAR * each
    alpha_top = 2.0 / (cells * slabs)
    piece = shape(13, each, rows, LANES)
    order = [(slab + by) % slabs * each + k for by in SHIFTS for k in range(each)]
    *pieces, twice, slope = pl.pallas_call(
        functools.partial(render, alpha_top=alpha_top),
        out_shape=[piece] * FAR
        + [shape(rest, cells + 2, 16, LANES), shape(rest, cells + 1, rows, LANES)],
        in_specs=in_smem(6) + anywhere(7),
        out_specs=anywhere(FAR + 2),
        scratch_shapes=[
            VMEM((cells + 6, tiles, 24, LANES), F32),
            VMEM((cells + 4, tiles, 16, LANES), F32),
            VMEM((cells + 2, tiles, 16, LANES), F32),
            VMEM((cells + 1, tiles, rows, LANES), F32),
            VMEM((2, tiles, 2, rows, LANES), F32),
            VMEM((2, tiles, 2, rows, LANES), F32),
            VMEM((tiles, 2, rows, LANES), F32),
            VMEM((2, tiles, 3 * cells, LANES), F32),
            VMEM((2, tiles, rows, LANES), F32),
            VMEM((FAR, 13, each, rows, LANES), F32),
            DMA((7,)),
            DMA((2, rest)),
            DMA((FAR,)),
        ],
        compiler_params=limit,
        name="render",
    )(
        edges,
        jnp.stack(order).astype(jnp.int32),
        colour_coef,
        opacity_coef,
        light_dir,
        light_colour,
        field,
        low,
        high,
        top,
        bottom,
        top_corner,
        bottom_corner,
    )
    pieces += pl.pallas_call(
        functools.partial(render_rest, alpha_top=alpha_top),
        out_shape=[piece] * (slabs - FAR),
        in_specs=in_smem(4) + anywhere(2),
        out_specs=anywhere(slabs - FAR),
        scratch_shapes=[
            VMEM((rest, cells + 2, 16, LANES), F32),
            VMEM((rest, cells + 1, rows, LANES), F32),
            VMEM((slabs - FAR, 13, each, rows, LANES), F32),
            DMA((2, rest)),
            DMA((slabs - FAR,)),
        ],
        compiler_params=limit,
        cost_estimate=pl.CostEstimate(
            flops=50_000_000, bytes_accessed=20_000_000, transcendentals=1_000_000
        ),
        name="render_rest",
    )(colour_coef, opacity_coef, light_dir, light_colour, twice, slope)
    arrived = [
        lax.ppermute(value, "depth", ring("depth", by)) if by else value
        for value, by in zip(pieces, SHIFTS)
    ]
    own = pl.pallas_call(
        fold,
        out_shape=piece,
        in_specs=in_smem(1) + in_vmem(slabs),
        out_specs=pl.BlockSpec(memory_space=VMEM),
        compiler_params=limit,
        name="fold",
    )(slab[None], *arrived)
    known = {0: own}
    for by in (1, -1, 2, -2):
        known[by] = lax.ppermute(own, "depth", ring("depth", by))
    for held, by in ((2, 1), (-2, -1), (2, 2)):
        known[held + by] = lax.ppermute(known[held], "depth", ring("depth", by))
    image = pl.pallas_call(
        functools.partial(spread, list(known)),
        out_shape=shape(13, tiles, rows, LANES),
        in_specs=in_smem(1) + anywhere(slabs),
        out_specs=pl.BlockSpec(memory_space=VMEM),
        scratch_shapes=[DMA((slabs,))],
        compiler_params=limit,
        name="spread",
    )(slab[None], *known.values())
    return image.transpose(0, 2, 1, 3).reshape(13, rows, width)


def solution(mesh):
    placed = (P("depth", "height", None), P(), P(), P(), P())
    return jax.shard_map(
        per_device, mesh=mesh, in_specs=placed, out_specs=P(None, "height", None), check_vma=False
    )
```
